128 devices in a mesh: lat: 8 (over x, y_lo), lon: 16 (over y_hi, z, core).
Axes of the slice: x: 4, y: 4 (y_hi: 2, y_lo: 2; y = y_hi * 2 + y_lo), z: 4, core: 2. Of those that a mesh axis runs over, the one named last changes fastest.
Arguments:
- tokens: bfloat16 [192, 384, 512], P('lat', 'lon'), may hold values from -6 to 6
- qkv_fine: bfloat16 [512, 1536], replicated, may hold values from -2 to 2, as said below
- out_fine: bfloat16 [512, 512], replicated, may hold values from -0.25 to 0.25
- merge_fine: bfloat16 [2048, 1024], replicated, may hold values from -0.125 to 0.125
- qkv_mid: bfloat16 [1024, 3072], replicated, may hold values from -2 to 2, as said below
- out_mid: bfloat16 [1024, 1024], replicated, may hold values from -0.1875 to 0.1875
- merge_mid: bfloat16 [4096, 2048], P('lon'), may hold values from -0.09375 to 0.09375
- qkv_coarse: bfloat16 [2048, 6144], P(None, 'lon'), may hold values from -2 to 2, as said below
- out_coarse: bfloat16 [2048, 2048], P('lon'), may hold values from -0.125 to 0.125
- grad_fine: bfloat16 [192, 384, 512], P('lat', 'lon'), may hold values from -6 to 6
- grad_mid: bfloat16 [96, 192, 1024], P('lat', 'lon'), may hold values from -6 to 6
- grad_coarse: bfloat16 [48, 96, 2048], P('lat', 'lon'), may hold values from -6 to 6
Outputs:
- grad_input: bfloat16 [192, 384, 512], P('lat', 'lon')
- coarse: bfloat16 [48, 96, 2048], P('lat', 'lon')
The draws below stay inside these ranges and needn't reach their ends.
Inputs may be any that keep to these rules, and one draw needn't show every extreme that they name: `qkv_fine`: head-major columns: each head's query, key and value blocks of 64 columns lie side by side. `qkv_mid`: head-major columns as for qkv_fine. `qkv_coarse`: head-major columns as for qkv_fine.
All inputs are finite; a program needn't handle non-finite values.
Results may differ from the reference program's by a relative error of at most 0.029.
Values may be sent and summed in bfloat16 or wider, within the bound.
A program may use at most 128 MiB of HBM per device.

```python
import jax
import jax.numpy as jnp
from jax import lax

C1 = 512
C2 = 1024
C3 = 2048
HD = 64
WH = 6
WW = 12
NLAT = 192
NLON = 384


def attention_weights(key, features, boost, share):
    head_count = features // HD
    entries = jax.random.normal(jax.random.fold_in(key, 11), (features, head_count, 3, HD), jnp.float32)
    chosen = jax.random.uniform(jax.random.fold_in(key, 12), (1, head_count, 1, 1)) < share
    keyed = jnp.where(chosen, entries[:, :, 0:1], entries[:, :, 1:2])
    value_part = entries[:, :, 2:3] * jnp.where(chosen, 1.0, 1.0)
    stacked = jnp.concatenate([entries[:, :, 0:1] * jnp.where(chosen, boost, 1.0), keyed * jnp.where(chosen, boost, 1.0), value_part], 2)
    scaled = jnp.clip(stacked * features ** (-0.5), -2.0, 2.0)
    return scaled.reshape(features, head_count * 3 * HD).astype(jnp.bfloat16)


def draw_qkv_fine(key, part):
    key = jax.random.fold_in(key, 1)
    return attention_weights(key, C1, 1.0, 0.0)


def draw_qkv_mid(key, part):
    key = jax.random.fold_in(key, 2)
    return attention_weights(key, C2, 1.0, 0.0)


def draw_qkv_coarse(key, part):
    key = jax.random.fold_in(key, 3)
    return attention_weights(key, C3, 1.0, 0.0)


def level_of(own_key, dims, cuts, low, high):
    def one(position, shards_of):
        draws = jax.random.uniform(jax.random.fold_in(jax.random.fold_in(own_key, 6), position), (shards_of,), jnp.float32, low / len(cuts), high / len(cuts))
        return jnp.repeat(jnp.exp(draws), dims[position] // shards_of).reshape((-1,) + (1,) * (len(dims) - position - 1))

    gain = one(*cuts[0])
    for cut in cuts[1:]:
        gain = gain * one(*cut)
    return gain


def noise(stream_key, dims, scale, limit, cuts=(), dtype=jnp.bfloat16):
    drawn = scale * jax.random.normal(stream_key, dims, jnp.float32)
    if cuts:
        drawn = drawn * level_of(stream_key, dims, cuts, -0.22, 0.18)
    return jnp.clip(drawn, -limit, limit).astype(dtype)


def setup_inputs(seed: int = 0) -> dict:
    streams_of = jax.random.split(jax.random.key(seed), 13)
    return {
        "tokens": noise(streams_of[0], (NLAT, NLON, C1), 1.0, 6.0, ((0, 8), (1, 16))),
        "qkv_fine": draw_qkv_fine(jax.random.fold_in(streams_of[12], 71), 0),
        "out_fine": noise(streams_of[2], (C1, C1), C1 ** -0.5, 0.25),
        "merge_fine": noise(streams_of[3], (4 * C1, C2), (4 * C1) ** -0.5, 0.125),
        "qkv_mid": draw_qkv_mid(jax.random.fold_in(streams_of[12], 71), 0),
        "out_mid": noise(streams_of[5], (C2, C2), C2 ** -0.5, 0.1875),
        "merge_mid": noise(streams_of[6], (4 * C2, C3), (4 * C2) ** -0.5, 0.09375, ((0, 16),)),
        "qkv_coarse": draw_qkv_coarse(jax.random.fold_in(streams_of[12], 71), 0),
        "out_coarse": noise(streams_of[8], (C3, C3), C3 ** -0.5, 0.125, ((0, 16),)),
        "grad_fine": noise(streams_of[9], (NLAT, NLON, C1), 1.0, 6.0, ((0, 8), (1, 16))),
        "grad_mid": noise(streams_of[10], (NLAT // 2, NLON // 2, C2), 1.0, 6.0, ((0, 8), (1, 16))),
        "grad_coarse": noise(streams_of[11], (NLAT // 4, NLON // 4, C3), 1.0, 6.0, ((0, 8), (1, 16))),
    }


epsilon = 1e-05

def normed(values):
    wide = values.astype(jnp.float32)
    average = lax.optimization_barrier(jnp.mean(wide, axis=-1, keepdims=True))
    centred = wide - average
    spread = lax.optimization_barrier(jnp.mean(centred * centred, axis=-1, keepdims=True))
    return (centred * lax.rsqrt(spread + epsilon)).astype(jnp.bfloat16)

def window_mix(triples, wrapped):
    row_count, col_count, features = triples.shape
    head_count = features // (3 * HD)
    tiles = triples.reshape(row_count // WH, WH, col_count // WW, WW, head_count, 3, HD)
    tiles = tiles.transpose(0, 2, 4, 5, 1, 3, 6).reshape(row_count // WH, col_count // WW, head_count, 3, WH * WW, HD)
    queries = tiles[:, :, :, 0].astype(jnp.float32)
    keyed = tiles[:, :, :, 1].astype(jnp.float32)
    values = tiles[:, :, :, 2].astype(jnp.float32)
    scores = jnp.einsum('abhqd,abhkd->abhqk', queries, keyed) * HD ** (-0.5)
    groups = jnp.broadcast_to(wrapped.reshape(row_count // WH, WH, 1), (row_count // WH, WH, WW))
    groups = groups.reshape(row_count // WH, 1, 1, WH * WW)
    allowed = groups[..., :, None] == groups[..., None, :]
    scores = jnp.where(allowed, scores, -1e+30)
    highest = lax.optimization_barrier(jnp.max(scores, axis=-1, keepdims=True))
    weights = jnp.exp(scores - highest)
    weights = (weights / lax.optimization_barrier(jnp.sum(weights, axis=-1, keepdims=True))).astype(jnp.bfloat16)
    result = jnp.einsum('abhqk,abhkd->abhqd', weights.astype(jnp.float32), values).astype(jnp.bfloat16)
    result = result.reshape(row_count // WH, col_count // WW, head_count, WH, WW, HD)
    return result.transpose(0, 3, 1, 4, 2, 5).reshape(row_count, col_count, head_count * HD)

def attend(moved, w_qkv, w_out, wrapped):
    triples = jnp.dot(normed(moved), w_qkv, preferred_element_type=jnp.float32).astype(jnp.bfloat16)
    mixed = window_mix(triples, wrapped)
    projected = jnp.dot(mixed, w_out, preferred_element_type=jnp.float32)
    return (moved.astype(jnp.float32) + projected).astype(jnp.bfloat16)

def shifted_block(lattice, w_qkv, w_out):
    moved = jnp.roll(lattice, (WH // 2, WW // 2), axis=(0, 1))
    wrapped = (jnp.arange(lattice.shape[0]) < WH // 2).astype(jnp.float32)
    return jnp.roll(attend(moved, w_qkv, w_out, wrapped), (-(WH // 2), -(WW // 2)), axis=(0, 1))

def fold_quad(lattice):
    row_count, col_count, features = lattice.shape
    tiles = lattice.reshape(row_count // 2, 2, col_count // 2, 2, features).transpose(0, 2, 3, 1, 4)
    return tiles.reshape(row_count // 2, col_count // 2, 4 * features)

def merged(lattice, w_merge):
    return jnp.dot(normed(fold_quad(lattice)), w_merge, preferred_element_type=jnp.float32).astype(jnp.bfloat16)

def forward(tokens, qkv_fine, out_fine, merge_fine, qkv_mid, out_mid, merge_mid, qkv_coarse, out_coarse):
    fine = shifted_block(tokens, qkv_fine, out_fine)
    middle = shifted_block(merged(fine, merge_fine), qkv_mid, out_mid)
    coarse = shifted_block(merged(middle, merge_mid), qkv_coarse, out_coarse)
    return (fine, middle, coarse)

def reference(tokens, qkv_fine, out_fine, merge_fine, qkv_mid, out_mid, merge_mid, qkv_coarse, out_coarse, grad_fine, grad_mid, grad_coarse):

    def sections(moving):
        return forward(moving, qkv_fine, out_fine, merge_fine, qkv_mid, out_mid, merge_mid, qkv_coarse, out_coarse)
    outputs, pullback = jax.vjp(sections, tokens)
    gradient = pullback((grad_fine, grad_mid, grad_coarse))[0]
    return (gradient, outputs[2])
```

```python
from types import SimpleNamespace

import jax
import jax.numpy as jnp
import numpy as np
from jax import lax
from jax.experimental import pallas as pl
from jax.experimental.pallas import tpu as pltpu
from jax.sharding import PartitionSpec as P

HD = 64
WH = 6
WW = 12
WP = 80
KP = 48
EPS = 1e-05
LAT = 8
LON = 16
bf16 = jnp.bfloat16
f32 = jnp.float32
MESH = pl.DeviceIdType.MESH


def window_order(cols):
    across = cols // WW

    def index(r, c):
        return ((r // WH) * across + c // WW) * WP + (r % WH) * WW + c % WW

    return index


def raster(stride):
    return lambda r, c: r * stride + c


def fold_order(inner, stride):
    def index(r, c):
        return ((c % 2) * 2 + r % 2) * stride + inner(r // 2, c // 2)

    return index


def shift_maps(size, src, n_src, dst, n_dst):
    dr, dc = WH // 2, WW // 2
    up = -(-(size - dr) * dc // 32) * 32
    down = -(-max(dr * (size - dc), 0) // 32) * 32
    corner = 32
    parts = [(0, up, 0, 1), (up, down, 1, 0), (up + down, corner, 1, 1)]
    total = up + down + corner
    own = np.zeros((n_dst, n_src), np.float32)
    halo = np.zeros((n_dst, total), np.float32)
    pack = np.zeros((total, n_src), np.float32)
    for r in range(size):
        for c in range(size):
            to = dst(r, c)
            if r >= dr and c >= dc:
                own[to, src(r - dr, c - dc)] = 1
                continue
            if r >= dr:
                slot = (r - dr) * dc + c
            elif c >= dc:
                slot = up + r * (size - dc) + c - dc
            else:
                slot = up + down + r * dc + c
            halo[to, slot] = 1
            pack[slot, src((r - dr) % size, (c - dc) % size)] = 1
    return own, halo, pack, [part for part in parts if part[1]]


def window_bias(stride, rows, groups):
    token = np.arange(rows)
    real = token % stride < groups * 2
    upper = token % stride < groups
    allowed = np.broadcast_to(real[None, :], (rows, rows))
    split = allowed & (upper[:, None] == upper[None, :])
    both = np.stack([allowed, split])
    both = np.concatenate([both, both], 1)
    return np.where(both, 0.0, -1e30).astype(np.float32)


FINE = shift_maps(24, raster(24), 576, window_order(24), 640)
FOLD = shift_maps(24, window_order(24), 640, fold_order(window_order(12), 160), 640)
MID = shift_maps(12, raster(16), 192, window_order(12), 160)
FOLDC = shift_maps(12, window_order(12), 160, fold_order(raster(6), KP), 4 * KP)
COARSE = shift_maps(6, raster(16), 96, raster(6), KP)
BIAS = window_bias(WP, WP, 36)
BIASC = window_bias(KP, 2 * KP, 18)

SQUEEZE = np.zeros((144, 4 * KP), np.float32)
for k in range(4):
    SQUEEZE[k * 36 : (k + 1) * 36, k * KP : k * KP + 36] = np.eye(36)
TOP = 80
FINE_BAND = np.ascontiguousarray(FINE[0][160:320, 144 - TOP : 304 - TOP])
FINE_BAND_BACK = np.ascontiguousarray(FINE[0][160:480, 144:288].T)
CONSTANTS = dict(
    fine_own=FINE_BAND, fine_halo=FINE[1], fine_pack=FINE[2],
    fine_own_t=FINE_BAND_BACK, fine_halo_t=FINE[1].T, fine_pack_t=FINE[2].T,
    fold_own=FOLD[0], fold_halo=FOLD[1], fold_pack=FOLD[2], fold_halo_t=FOLD[1].T, fold_pack_t=FOLD[2].T,
    mid_own=MID[0], mid_halo=MID[1], mid_pack=MID[2],
    foldc_own=FOLDC[0], foldc_halo=FOLDC[1], foldc_pack=FOLDC[2],
    foldc_own_t=FOLDC[0].T, foldc_halo_t=FOLDC[1].T, foldc_pack_t=FOLDC[2].T,
    squeeze=SQUEEZE, squeeze_t=SQUEEZE.T,
    coarse_halo=COARSE[1], coarse_pack=COARSE[2], coarse_halo_t=COARSE[1].T, coarse_pack_t=COARSE[2].T,
)

LOADED = (
    tuple(dict(tokens=1, fine_pack=1, fine_own=1, fine_halo=1)),
    tuple(dict(
        qkv_f=1, g_coarse=1, coarse_pack=1, g_mid=1, mid_pack=1, g_fine=1, bias=1, out_f=1, fold_pack=1, fold_own=1, fold_halo=1,
    )),
    tuple(dict(
        mrg_f=1, coarse_halo=1, squeeze=1, squeeze_t=1, qkv_m=1, out_m=1, foldc_pack=1, foldc_own=1, foldc_halo=1, biasc=1,
        mid_own=1, mid_halo=1, foldc_halo_t=1, foldc_own_t=1, foldc_pack_t=1, fold_halo_t=1, fold_pack_t=1,
        fine_halo_t=1, fine_own_t=1, fine_pack_t=1, coarse_halo_t=1, coarse_pack_t=1,
    )),
)
ALL_LOADED = [name for group in LOADED for name in group]


def nn(a, b):
    return jnp.dot(a, b, preferred_element_type=f32)


def nt(a, b):
    return lax.dot_general(a, b, (((1,), (1,)), ((), ())), preferred_element_type=f32)


def tn(a, b):
    return lax.dot_general(a, b, (((0,), (0,)), ((), ())), preferred_element_type=f32)


def norm_rows(x):
    centred = x - jnp.mean(x, axis=-1, keepdims=True)
    scale = lax.rsqrt(jnp.mean(centred * centred, axis=-1, keepdims=True) + EPS)
    return centred * scale, scale


def norm_back(d, h, scale):
    d = d.astype(bf16).astype(f32)
    h = h.astype(f32)
    return scale * (d - jnp.mean(d, axis=-1, keepdims=True) - h * jnp.mean(d * h, axis=-1, keepdims=True))


def norm_split(parts):
    size = sum(p.shape[-1] for p in parts)
    average = sum(jnp.sum(p, axis=-1, keepdims=True) for p in parts) / size
    parts = [p - average for p in parts]
    scale = lax.rsqrt(sum(jnp.sum(p * p, axis=-1, keepdims=True) for p in parts) / size + EPS)
    return [p * scale for p in parts], scale


def norm_back_split(ds, hs, scale):
    size = sum(d.shape[-1] for d in ds)
    ds = [d.astype(bf16).astype(f32) for d in ds]
    hs = [h.astype(f32) for h in hs]
    mean_d = sum(jnp.sum(d, axis=-1, keepdims=True) for d in ds) / size
    mean_dh = sum(jnp.sum(d * h, axis=-1, keepdims=True) for d, h in zip(ds, hs)) / size
    return [scale * (d - mean_d - h * mean_dh) for d, h in zip(ds, hs)]


def aligned(start, size, multiple):
    return pl.ds(pl.multiple_of(start, multiple), size)


def project_qkv(h, weight, tr, trr, rows, pairs, step):
    @pl.loop(0, rows // step)
    def _(i):
        part = aligned(i * step, step, 16)

        @pl.loop(0, pairs)
        def _(p):
            wide = nn(h[part, :], weight(p))
            tr[part, aligned(p * 384, 384, 128)] = wide.astype(bf16)
            ra, rb, rc = (pltpu.roll(wide[:, k * 128 : (k + 1) * 128], 64, 1) for k in range(3))
            low = lax.broadcasted_iota(jnp.int32, (1, 128), 1) < 64
            trr[part, aligned(p * 256, 128, 128)] = jnp.where(low, ra, rc).astype(bf16)
            trr[part, aligned(p * 256 + 128, 128, 128)] = jnp.where(low, rb, ra).astype(bf16)


def halves():
    lane = lax.broadcasted_iota(jnp.int32, (1, 128), 1)
    low = lane < 64
    one = jnp.where(low, 1.0, 0.0)
    return low, one.astype(bf16), (1.0 - one).astype(bf16)


def attend(tr, trr, ps, mix, bias, pairs, windows, wp, split, unroll, part=0, parts=1):
    steps = pairs * windows // unroll // parts

    @pl.loop(part * steps, (part + 1) * steps)
    def _(step):
        low, mlo, mhi = halves()
        for u in range(unroll):
            item = step * unroll + u
            w, p = lax.div(item, pairs), lax.rem(item, pairs)
            part = aligned(w * wp, wp, 16)
            a, b, c = (tr[part, aligned(p * 384 + k * 128, 128, 128)] for k in range(3))
            k2 = trr[part, aligned(p * 256, 128, 128)]
            eighth = jnp.asarray(HD**-0.5, bf16)
            q2 = jnp.concatenate([a * (mlo * eighth), b * (mhi * eighth)], 0)
            scores = nt(q2, k2) + bias[split(w)]
            e = jnp.exp(scores - jnp.max(scores, axis=-1, keepdims=True))
            weights = (e / jnp.sum(e, axis=-1, keepdims=True)).astype(bf16)
            ps[item] = weights
            mixed = jnp.where(low, nn(weights[:wp], b), nn(weights[wp:], c))
            mix[part, aligned(p * 128, 128, 128)] = mixed.astype(bf16)


def attend_back(tr, trr, ps, dmix, pairs, windows, wp, unroll):
    @pl.loop(0, pairs * windows // unroll)
    def _(step):
        low, mlo, mhi = halves()
        for u in range(unroll):
            item = step * unroll + u
            w, p = lax.div(item, pairs), lax.rem(item, pairs)
            part = aligned(w * wp, wp, 16)
            places = [(part, aligned(p * 384 + k * 128, 128, 128)) for k in range(3)]
            b, c = tr[places[1]], tr[places[2]]
            k2, q2 = (trr[part, aligned(p * 256 + k * 128, 128, 128)] for k in range(2))
            do = dmix[part, aligned(p * 128, 128, 128)]
            weights = ps[item]
            outs = []
            for half, mask, values in ((0, mlo, b), (1, mhi, c)):
                wt = weights[half * wp : (half + 1) * wp]
                wide = wt.astype(f32)
                dw = nt(do * mask, values)
                ds = wide * (dw - jnp.sum(wide * dw, axis=-1, keepdims=True)) * HD**-0.5
                outs.append((wt, ds.astype(bf16)))
            (w0, ds0), (w1, ds1) = outs
            tr[places[0]] = jnp.where(low, nn(ds0, k2), tn(ds0, q2)).astype(bf16)
            tr[places[1]] = jnp.where(low, tn(w0, do), nn(ds1, k2)).astype(bf16)
            tr[places[2]] = jnp.where(low, tn(ds1, q2), tn(w1, do)).astype(bf16)


def tiles(rows, step, cols, width, body):
    @pl.loop(0, rows // step)
    def _(i):
        part = aligned(i * step, step, 16)

        @pl.loop(0, cols // width)
        def _(j):
            body(part, aligned(j * width, width, 128))


VMEM_SCRATCH = dict(
    xf=((640, 512), bf16), hf=((640, 512), bf16), sf=((640, 1), f32), trf=((640, 1536), bf16),
    trrf=((640, 1024), bf16), psf=((32, 2 * WP, WP), bf16), mixf=((640, 512), bf16), yf=((640, 512), bf16),
    wide=((640, 512), f32),
    ff=((160, 2048), bf16), sff=((160, 1), f32),
    xm=((160, 1024), bf16), hm=((160, 1024), bf16), sm=((160, 1), f32), trm=((160, 3072), bf16),
    trrm=((160, 2048), bf16), psm=((16, 2 * WP, WP), bf16), mixm=((160, 1024), bf16), ym=((160, 1024), bf16),
    fc=((KP, 4096), bf16), sfc=((KP, 1), f32), fcs=((4, KP, 1024), bf16), fcr=((4, KP, 1024), bf16),
    pms=((4, 144, 512), bf16), pmr=((4, 144, 512), bf16), dmo=((144, 512), bf16), dms=((4, 144, 512), bf16), stage=((4, KP, 2048), bf16),
    dsr=((4, KP, 1024), bf16), dfc=((4 * KP, 1024), bf16),
    gm=((192, 1024), bf16), gc=((96, 2048), bf16),
    xc=((KP, 2048), bf16), hc=((KP, 2048), bf16), sc=((KP, 1), f32), hcs=((144, 512), bf16), hcr=((4, 144, 512), bf16),
    ac=((KP, 2048), bf16), acs=((144, 512), bf16), acr=((4, 144, 512), bf16),
    trc=((4 * KP, 1536), bf16), trrc=((4 * KP, 1024), bf16), psc=((8, 4 * KP, 2 * KP), bf16),
    mixc=((4 * KP, 512), bf16), dmixc=((4 * KP, 512), bf16),
    dhs=((4, 144, 512), bf16), dhr=((4, 144, 512), bf16), pos=((4, 144, 512), bf16), por=((4, 144, 512), bf16),
    yc=((KP, 2048), bf16),
    wm=((4, 256, 2048), bf16), wq=((4, 2048, 384), bf16), wo=((4, 128, 2048), bf16),
)
EXCHANGES = dict(
    tok=(FINE, 512, 1), gf=(FINE, 512, 1), gm=(MID, 1024, 1), gc=(COARSE, 2048, 1), fold=(FOLD, 512, 1), foldc=(FOLDC, 1024, 1),
    foldc_b=(FOLDC, 1024, -1), fold_b=(FOLD, 512, -1), fine_b=(FINE, 512, -1), coarse_b=(COARSE, 2048, -1),
)
SENT_FROM = dict(fold="tok", fold_b="tok", fine_b="tok", foldc_b="foldc", coarse_b="gc")
N_LOCAL = len(ALL_LOADED) + 7
N_REMOTE = 96


class Lazy:
    def __init__(self, make):
        self.make = make

    def __getattr__(self, name):
        value = self.make(name)
        setattr(self, name, value)
        return value


def build(shapes):
    scratch = dict(VMEM_SCRATCH)
    loaded = {name: shapes[name] for name in ALL_LOADED}
    for name in ("tokens", "g_fine"):
        loaded[name] = ((TOP + 576, 512), bf16)
    sends, receives = {}, {}
    for name, (maps, width, _) in EXCHANGES.items():
        receives[name] = ((maps[1].shape[1], width), bf16)
        if name not in SENT_FROM:
            sends[name] = receives[name]

    def kernel(*refs):
        refs = list(refs)

        def take(names):
            return {name: refs.pop(0) for name in names}

        hbm = take(shapes)
        grad_ref, coarse_ref = refs.pop(0), refs.pop(0)
        v = SimpleNamespace(**take(scratch))
        vm, send_buf, recv_buf = take(loaded), take(sends), take(receives)
        local_sem, send_sem, recv_sem = refs

        lat, lon = lax.axis_index("lat"), lax.axis_index("lon")
        y, z, core = lax.div(lon, 8), lax.rem(lax.div(lon, 2), 4), lax.rem(lon, 2)

        def near(dlat, dlon):
            return (lax.rem(lat + dlat + LAT, LAT), lax.rem(lon + dlon + LON, LON))

        def at(yy, zz, cc):
            return (lat, yy * 8 + zz * 2 + cc)

        def turn(k):
            return lax.rem(z + k, 4)

        loads = {}
        for i, name in enumerate(ALL_LOADED):
            dest = vm[name].at[pl.ds(TOP, 576)] if name in ("tokens", "g_fine") else vm[name]
            loads[name] = pltpu.make_async_copy(hbm[name], dest, local_sem.at[i])

        def start_loads(group):
            for name in group:
                loads[name].start()

        start_loads(LOADED[0])

        def wait_load(name):
            loads[name].wait()
            return vm[name]

        got = Lazy(wait_load)

        own_slot = y * 2 + core
        own_loads = []
        for i, name in enumerate(("wm", "wq", "wo")):
            copy = pltpu.make_async_copy(hbm[name], getattr(v, name).at[own_slot], local_sem.at[len(ALL_LOADED) + i])
            own_loads.append(copy)

        barrier = pltpu.get_barrier_semaphore()
        others = [near(1, 0), near(-1, 0), near(1, 1), near(-1, -1)]
        others += [(lat + 1 - 2 * lax.rem(lat, 2), lax.rem(lon + 8, LON))]
        others += [(lat, y * 8 + lax.rem(lax.rem(lon, 8) + k, 8)) for k in range(1, 8)]
        for device in others:
            pl.semaphore_signal(barrier, inc=1, device_id=device, device_id_type=MESH)
        place = lax.rem(lon, 8)

        @pl.when(place == 7)
        def _():
            pl.semaphore_signal(barrier, inc=1, device_id=near(0, 1), device_id_type=MESH)

        @pl.when(place == 0)
        def _():
            pl.semaphore_signal(barrier, inc=1, device_id=near(0, -1), device_id_type=MESH)

        edge = jnp.where((place == 7) | (place == 0), 1, 0)
        pl.semaphore_wait(barrier, len(others) + edge)

        counter = [0]

        def sems(n):
            counter[0] += n
            assert counter[0] <= N_REMOTE
            return counter[0] - n

        def remote(src, dst, send, recv, device):
            return pltpu.make_async_remote_copy(
                src_ref=src, dst_ref=dst, send_sem=send_sem.at[send], recv_sem=recv_sem.at[recv],
                device_id=device, device_id_type=MESH,
            )

        pending = []

        def sender(name):
            return send_buf[SENT_FROM.get(name, name)]

        def finish(copies):
            for copy in copies:
                copy.wait()

        def sent(copies):
            for copy in copies:
                copy.wait_send()

        def shift(name):
            maps, _, sign = EXCHANGES[name]
            base = sems(3)
            copies = []
            for k, (start, size, dlat, dlon) in enumerate(maps[3]):
                part = pl.ds(start, size)
                copies.append(
                    remote(sender(name).at[part], recv_buf[name].at[part], base + k, base + k, near(sign * dlat, sign * dlon))
                )
            for copy in copies:
                copy.start()
            return copies

        def received(copies):
            for copy in copies:
                copy.wait_recv()

        sibling = at(y, z, 1 - core)
        partner_slot = (1 - y) * 2 + core
        y_low = lax.rem(lat, 2)
        beside = lat + 1 - 2 * y_low

        def weight_piece(name, start, size):
            base = sems(2)
            dest = getattr(v, name)
            half = hbm[name].shape[0] // 2
            mine = aligned(y_low * half + start, size, 16)
            other = aligned((1 - y_low) * half + start, size, 16)
            there = dest.at[partner_slot, other]
            return (
                remote(hbm[name].at[mine], dest.at[own_slot, mine], base, base, (beside, lax.rem(lon + 8, LON))),
                remote(there, there, base + 1, base + 1, (beside, lon)),
            )

        def core_copies(name):
            base = sems(2)
            dest = getattr(v, name)
            there = dest.at[partner_slot]
            return (
                remote(hbm[name], dest.at[own_slot], base, base, sibling),
                remote(there, there, base + 1, base + 1, sibling),
            )

        pieces = dict(
            wm=[weight_piece("wm", 0, 128)],
            wq=[weight_piece("wq", 0, 640), weight_piece("wq", 640, 384)],
            wo=[weight_piece("wo", 0, 64)],
        )
        between_cores = {name: core_copies(name) for name in pieces}

        def cross_weights(name, i):
            pieces[name][i][0].start()

        def relay_weights(name, i):
            pieces[name][i][0].wait_recv()
            pieces[name][i][1].start()

        def pass_weights(name):
            for piece in pieces[name]:
                piece[1].wait_recv()
            between_cores[name][1].start()

        def weights_ready(name):
            for copy in between_cores[name]:
                copy.wait_recv()
                pending.append(copy)
            for piece in pieces[name]:
                pending.extend(piece)

        def pack(name, source, matrix):
            sender(name)[...] = nn(matrix[...], source).astype(bf16)

        tokens = got.tokens
        pack("tok", tokens[TOP:, :], got.fine_pack)
        shift_tok = shift("tok")
        start_loads(LOADED[1])
        tokens[0:TOP, :] = jnp.zeros((TOP, 512), bf16)
        vm["g_fine"][0:TOP, :] = jnp.zeros((TOP, 512), bf16)
        v.gm[...] = jnp.zeros_like(v.gm)
        v.gc[...] = jnp.zeros_like(v.gc)
        fine_own, fine_halo, qkv_f = got.fine_own, got.fine_halo, got.qkv_f

        def placed(part, source, name, own, halo):
            return nn(own[part, :], source[...]) + nn(halo[part, :], recv_buf[name][...])

        def placed_fine(i, source, name):
            return nn(fine_own[...], source[aligned(i * 144, 160, 16), :]) + nn(
                fine_halo[aligned(i * 160, 160, 16), :], recv_buf[name][...]
            )

        received(shift_tok)
        cross_weights("wm", 0)

        @pl.loop(0, 4)
        def _(i):
            part = aligned(i * 160, 160, 16)
            x = placed_fine(i, tokens, "tok")
            v.xf[part, :] = x.astype(bf16)
            h, scale = norm_rows(x)
            v.hf[part, :] = h.astype(bf16)
            v.sf[part, :] = scale

        start_loads(LOADED[2])
        for copy in own_loads:
            copy.start()
        for name in pieces:
            between_cores[name][0].start()
        project_qkv(v.hf, lambda p: qkv_f[:, aligned(p * 384, 384, 128)], v.trf, v.trrf, 640, 4, 320)
        first = lat == 0
        bias, out_f = got.bias, got.out_f
        for part in range(2):
            if part == 1:
                relay_weights("wm", 0)
                for r in range(6):
                    v.gc[16 * r : 16 * r + 6, :] = got.g_coarse[r]
                for r in range(12):
                    v.gm[16 * r : 16 * r + 12, :] = got.g_mid[r]
                pack("gc", v.gc[...], got.coarse_pack)
                shift_gc = shift("gc")
                pack("gf", got.g_fine[TOP:, :], got.fine_pack)
                shift_gf = shift("gf")
                pack("gm", v.gm[...], got.mid_pack)
                shift_gm = shift("gm")
                cross_weights("wq", 0)
            attend(v.trf, v.trrf, v.psf, v.mixf, bias, 4, 8, WP, lambda w: jnp.where(first & (w < 2), 1, 0), 4, part, 2)

        def out_fine(part, cols):
            v.yf[part, cols] = (nn(v.mixf[part, :], out_f[:, cols]) + v.xf[part, cols].astype(f32)).astype(bf16)

        tiles(640, 320, 512, 256, out_fine)

        sent(shift_tok)
        pack("fold", v.yf[...], got.fold_pack)
        shift_fold = shift("fold")
        fold_own, fold_halo, mrg_f = got.fold_own, got.fold_halo, got.mrg_f
        slot = lax.rem(z, 2) * 2 + core
        wide_group = lax.div(z, 2)

        def squeeze(x, dest):
            stacked = jnp.concatenate([x[:, k * 512 : (k + 1) * 512] for k in range(4)], 0)
            dest[...] = nn(got.squeeze[...], stacked).astype(bf16)

        def spread(packed):
            stacked = nn(got.squeeze_t[...], packed.astype(bf16))
            return [stacked[k * KP : (k + 1) * KP] for k in range(4)]

        def spread_all(packed):
            for s in range(4):
                for k, part in enumerate(spread(packed[s])):
                    v.stage[s, :, k * 512 : (k + 1) * 512] = part.astype(bf16)

        def total_of(packed):
            return jnp.concatenate(spread(sum(packed[k].astype(f32) for k in range(4))), 1)

        def to_group(source, dest):
            send, recv = sems(4), sems(4)
            for k in range(1, 4):
                copy = remote(source, dest.at[slot], send + k, recv + slot, at(y, turn(k), wide_group))
                copy.start()
                pending.append(copy)
            across = remote(source, dest.at[slot], send, recv + slot, sibling)

            @pl.when(core == wide_group)
            def _():
                dest[slot] = source[...]

            @pl.when(core != wide_group)
            def _():
                across.start()
                across.wait_send()

            return source, dest, send, recv

        def is_own(s):
            return (z == core * 2 + s // 2) & (core == s % 2)

        def from_group(handle):
            source, dest, send, recv = handle
            for s in range(4):

                @pl.when(jnp.logical_not(is_own(s)))
                def _(s=s):
                    remote(source, dest.at[s], send, recv + s, sibling).wait_recv()

        def to_owners(source, dest):
            send, recv = sems(4), sems(4)
            for s in range(4):
                copy = remote(source.at[s], dest.at[z], send + s, recv + z, at(y, core * 2 + s // 2, s % 2))

                @pl.when(is_own(s))
                def _(s=s):
                    dest[z] = source[s]

                @pl.when(jnp.logical_not(is_own(s)))
                def _(copy=copy):
                    copy.start()

            return source, dest, send, recv

        def from_members(handle):
            source, dest, send, recv = handle
            for k in range(4):

                @pl.when(jnp.logical_not((z == k) & (core == wide_group)))
                def _(k=k):
                    remote(source.at[0], dest.at[k], send, recv + k, sibling).wait_recv()

            for s in range(4):

                @pl.when(jnp.logical_not(is_own(s)))
                def _(s=s):
                    remote(source.at[s], dest.at[0], send + s, recv, sibling).wait_send()

        def around(pick, dest, own):
            base = sems(4)
            copies = []
            for k in range(1, 4):
                copy = remote(pick(k), dest.at[z], base + k, base + k, at(y, turn(k), core))
                copy.start()
                copies.append(copy)
            dest[z] = own
            return copies

        received(shift_fold)

        quads = [placed(slice(k * 160, (k + 1) * 160), v.yf, "fold", fold_own, fold_halo) for k in range(4)]
        normed, scale = norm_split(quads)
        for k in range(4):
            v.ff[:, k * 512 : (k + 1) * 512] = normed[k].astype(bf16)
        v.sff[...] = scale
        relay_weights("wq", 0)
        cross_weights("wq", 1)
        finish(shift_gf)
        finish(shift_gc)
        v.ac[...] = nn(got.coarse_halo[...], recv_buf["gc"][...]).astype(bf16)
        squeeze(v.ac[...], v.acs)
        adjoint = to_group(v.acs, v.acr)

        @pl.loop(0, 4)
        def _(i):
            part = aligned(i * 160, 160, 16)
            v.yf[part, :] = placed_fine(i, got.g_fine, "gf").astype(bf16)

        def merge_fine(part, cols):
            v.xm[part, cols] = nn(v.ff[part, :], mrg_f[:, cols]).astype(bf16)

        tiles(160, 160, 1024, 256, merge_fine)

        qkv_m, out_m = got.qkv_m, got.out_m
        h, scale = norm_rows(v.xm[...].astype(f32))
        v.hm[...] = h.astype(bf16)
        v.sm[...] = scale
        project_qkv(v.hm, lambda p: qkv_m[:, aligned(p * 384, 384, 128)], v.trm, v.trrm, 160, 8, 160)
        attend(v.trm, v.trrm, v.psm, v.mixm, bias, 8, 2, WP, lambda w: jnp.where(first & (w < 1), 1, 0), 4)

        pass_weights("wm")

        def out_mid(part, cols):
            v.ym[part, cols] = (nn(v.mixm[part, :], out_m[:, cols]) + v.xm[part, cols].astype(f32)).astype(bf16)

        tiles(160, 160, 1024, 256, out_mid)

        pack("foldc", v.ym[...], got.foldc_pack)
        shift_foldc = shift("foldc")
        for copy in own_loads:
            copy.wait()
        weights_ready("wm")
        foldc_own, foldc_halo = got.foldc_own, got.foldc_halo
        received(shift_foldc)
        relay_weights("wq", 1)
        cross_weights("wo", 0)
        folded = placed(slice(None), v.ym, "foldc", foldc_own, foldc_halo)
        quads = [folded[k * KP : (k + 1) * KP] for k in range(4)]
        normed, scale = norm_split(quads)
        v.sfc[...] = scale
        for k in range(4):
            h = normed[k].astype(bf16)
            v.fc[:, k * 1024 : (k + 1) * 1024] = h
            for j in range(2):
                block = 2 * k + j
                v.fcs[block % 4, :, (block // 4) * 512 : (block // 4 + 1) * 512] = h[:, j * 512 : (j + 1) * 512]
        copies = around(lambda k: v.fcs.at[turn(k)], v.fcr, v.fcs[z])
        finish(copies)
        gathered = v.fcr[...].reshape(4 * KP, 1024)

        @pl.loop(0, 8)
        def _(j):
            cols = aligned(j * 256, 256, 128)
            total = nn(gathered[:, 0:256], v.wm[0, :, cols])
            for s in range(1, 4):
                total += nn(gathered[:, s * 256 : (s + 1) * 256], v.wm[s, :, cols])
            v.stage[:, :, cols] = total.astype(bf16).reshape(4, KP, 256)

        for k in range(4):
            squeeze(v.stage[k], v.pms.at[k])
        copies = around(lambda k: v.pms.at[turn(k)], v.pmr, v.pms[z])
        relay_weights("wo", 0)
        pass_weights("wq")
        finish(copies)
        x = total_of(v.pmr).astype(bf16)
        v.xc[...] = x
        h, scale = norm_rows(x.astype(f32))
        v.hc[...] = h.astype(bf16)
        v.sc[...] = scale

        squeeze(v.hc[...], v.hcs)
        forward = to_group(v.hcs, v.hcr)
        biasc = got.biasc
        weights_ready("wq")
        from_group(forward)
        spread_all(v.hcr)
        pass_weights("wo")
        project_qkv(v.stage.reshape(4 * KP, 2048), lambda p: v.wq[p], v.trc, v.trrc, 4 * KP, 4, 4 * KP)
        attend(v.trc, v.trrc, v.psc, v.mixc, biasc, 4, 2, 2 * KP, lambda w: jnp.where(first, 1, 0), 4)
        from_group(adjoint)
        weights_ready("wo")
        spread_all(v.acr)
        for p in range(4):
            v.dmixc[:, p * 128 : (p + 1) * 128] = nt(v.stage[...].reshape(4 * KP, 2048), v.wo[p]).astype(bf16)
        attend_back(v.trc, v.trrc, v.psc, v.dmixc, 4, 2, 2 * KP, 4)

        @pl.loop(0, 8)
        def _(j):
            rows = aligned(j * 256, 256, 128)
            total = nt(v.trc[:, 0:384], v.wq[0, rows, :])
            for s in range(1, 4):
                total += nt(v.trc[:, s * 384 : (s + 1) * 384], v.wq[s, rows, :])
            v.stage[:, :, rows] = total.astype(bf16).reshape(4, KP, 256)

        for k in range(4):
            squeeze(v.stage[k], v.dhs.at[k])
        backward = to_owners(v.dhs, v.dhr)

        @pl.loop(0, 8)
        def _(j):
            cols = aligned(j * 256, 256, 128)
            total = nn(v.mixc[:, 0:128], v.wo[0, :, cols])
            for s in range(1, 4):
                total += nn(v.mixc[:, s * 128 : (s + 1) * 128], v.wo[s, :, cols])
            v.stage[:, :, cols] = total.astype(bf16).reshape(4, KP, 256)

        for k in range(4):
            squeeze(v.stage[k], v.pos.at[k])
        from_members(backward)
        d = total_of(v.dhr)
        d = norm_back(d, v.hc[...], v.sc[...])
        d = (d.astype(bf16).astype(f32) + v.ac[...].astype(f32)).astype(bf16)
        squeeze(d, v.dmo)

        copies = around(lambda k: v.dmo, v.dms, v.dmo[...])
        finish(copies)
        spread_all(v.dms)
        gathered_d = v.stage[...].reshape(4 * KP, 2048)
        for s in range(4):
            block = nt(gathered_d, v.wm[s]).astype(bf16)
            v.fcs[:, :, s * 256 : (s + 1) * 256] = block.reshape(4, KP, 256)
        copies = around(lambda k: v.fcs.at[turn(k)], v.dsr, v.fcs[z])
        outward = to_owners(v.pos, v.por)
        finish(copies)

        ds = []
        hs = []
        for b in range(8):
            ds.append(v.dsr[b % 4, :, (b // 4) * 512 : (b // 4 + 1) * 512])
            hs.append(v.fc[:, b * 512 : (b + 1) * 512])
        for b, d in enumerate(norm_back_split(ds, hs, v.sfc[...])):
            k = b // 2
            v.dfc[k * KP : (k + 1) * KP, (b % 2) * 512 : (b % 2 + 1) * 512] = d.astype(bf16)
        sent(shift_foldc)
        pack("foldc_b", v.dfc[...], got.foldc_halo_t)
        copies = shift("foldc_b")
        foldc_own_t, foldc_pack_t = got.foldc_own_t, got.foldc_pack_t
        finish(shift_gm)
        adjoint_mid = placed(slice(None), v.gm, "gm", got.mid_own, got.mid_halo).astype(bf16).astype(f32)
        finish(copies)
        d = placed(slice(None), v.dfc, "foldc_b", foldc_own_t, foldc_pack_t)
        v.ym[...] = (adjoint_mid + d.astype(bf16).astype(f32)).astype(bf16)

        def dmix_mid(part, cols):
            v.mixm[part, cols] = nt(v.ym[part, :], out_m[cols, :]).astype(bf16)

        tiles(160, 160, 1024, 256, dmix_mid)
        attend_back(v.trm, v.trrm, v.psm, v.mixm, 8, 2, WP, 4)

        from_members(outward)
        total = total_of(v.por)
        v.yc[...] = (v.xc[...].astype(f32) + total).astype(bf16)
        pack("coarse_b", v.yc[...], got.coarse_halo_t)
        shift_out = shift("coarse_b")

        def to_wide(left, weight, blocks):
            @pl.loop(0, 2 * blocks)
            def _(j):
                v.wide[aligned(lax.div(j, 2) * 160, 160, 16), aligned(lax.rem(j, 2) * 256, 256, 128)] = nt(
                    left[...], weight[aligned(j * 256, 256, 128), :]
                )

        def wide_back(blocks, h, scale):
            ds = [v.wide[k * 160 : (k + 1) * 160, :] for k in range(blocks)]
            hs = [h[:, k * 512 : (k + 1) * 512] for k in range(blocks)]
            return [d.astype(bf16) for d in norm_back_split(ds, hs, scale[...])]

        to_wide(v.trm, qkv_m, 2)
        for k, d in enumerate(wide_back(2, v.hm, v.sm)):
            cols = slice(k * 512, (k + 1) * 512)
            v.xm[:, cols] = (d.astype(f32) + v.ym[:, cols].astype(f32)).astype(bf16)

        to_wide(v.xm, mrg_f, 4)
        for k, d in enumerate(wide_back(4, v.ff, v.sff)):
            v.mixf[k * 160 : (k + 1) * 160, :] = d
        sent(shift_fold)
        pack("fold_b", v.mixf[...], got.fold_halo_t)
        copies = shift("fold_b")
        fold_pack_t = got.fold_pack_t
        finish(copies)

        @pl.loop(0, 5)
        def _(i):
            part = aligned(i * 128, 128, 128)
            d = tn(fold_own[:, part], v.mixf[...]) + nn(fold_pack_t[part, :], recv_buf["fold_b"][...])
            v.yf[part, :] = (v.yf[part, :].astype(f32) + d.astype(bf16).astype(f32)).astype(bf16)

        def dmix_fine(part, cols):
            v.mixf[part, cols] = nt(v.yf[part, :], out_f[cols, :]).astype(bf16)

        tiles(640, 320, 512, 256, dmix_fine)
        attend_back(v.trf, v.trrf, v.psf, v.mixf, 4, 8, WP, 4)

        def dh_fine(part, cols):
            v.wide[part, cols] = nt(v.trf[part, :], qkv_f[cols, :])

        tiles(640, 320, 512, 256, dh_fine)

        @pl.loop(0, 4)
        def _(i):
            part = aligned(i * 160, 160, 16)
            d = norm_back(v.wide[part, :], v.hf[part, :], v.sf[part, :])
            v.xf[part, :] = (d.astype(bf16).astype(f32) + v.yf[part, :].astype(f32)).astype(bf16)

        pack("fine_b", v.xf[...], got.fine_halo_t)
        copies = shift("fine_b")
        fine_pack_t = got.fine_pack_t
        finish(shift_out)
        out = nn(got.coarse_pack_t[...], recv_buf["coarse_b"][...]).astype(bf16)
        for r in range(6):
            coarse_ref[r] = out[16 * r : 16 * r + 6]
        finish(copies)
        writes = []
        fine_own_t = got.fine_own_t
        for j in range(4):
            part = pl.ds(j * 144, 144)
            here = (j * 160, min(j * 160 + 320, 640))
            d = nn(fine_own_t[:, : here[1] - here[0]], v.xf[here[0] : here[1], :])
            d += nn(fine_pack_t[part, :], recv_buf["fine_b"][...])
            tokens[part, :] = d.astype(bf16)
            writes.append(pltpu.make_async_copy(tokens.at[part], grad_ref.at[part], local_sem.at[len(ALL_LOADED) + 3 + j]))
            writes[-1].start()
        for write in writes:
            write.wait()
        for copy in pending:
            copy.wait_send()
        for name in ALL_LOADED:
            getattr(got, name)

    any_space = pl.BlockSpec(memory_space=pl.ANY)
    whole = pl.BlockSpec(memory_space=pltpu.VMEM)
    return pl.pallas_call(
        kernel,
        out_shape=(jax.ShapeDtypeStruct((576, 512), bf16), jax.ShapeDtypeStruct((6, 6, 2048), bf16)),
        in_specs=[any_space] * len(shapes),
        out_specs=(any_space, whole),
        scratch_shapes=[pltpu.VMEM(*shape) for group in (scratch, loaded, sends, receives) for shape in group.values()]
        + [pltpu.SemaphoreType.DMA((N_LOCAL,)), pltpu.SemaphoreType.DMA((N_REMOTE,)), pltpu.SemaphoreType.DMA((N_REMOTE,))],
        compiler_params=pltpu.CompilerParams(
            collective_id=0, has_side_effects=True, vmem_limit_bytes=66_584_576
        ),
    )


def shards(
    tokens, qkv_fine, out_fine, merge_fine, qkv_mid, out_mid, merge_mid, qkv_coarse, out_coarse, grad_fine, grad_mid, grad_coarse
):
    values = dict(
        tokens=tokens.reshape(576, 512),
        qkv_f=qkv_fine,
        out_f=out_fine,
        mrg_f=merge_fine,
        qkv_m=qkv_mid,
        out_m=out_mid,
        wm=merge_mid,
        wq=qkv_coarse,
        wo=out_coarse,
        g_fine=grad_fine.reshape(576, 512),
        g_mid=grad_mid,
        g_coarse=grad_coarse,
        bias=jnp.asarray(BIAS),
        biasc=jnp.asarray(BIASC),
    )
    for name, matrix in CONSTANTS.items():
        values[name] = jnp.asarray(matrix, bf16)
    shapes = {name: (value.shape, value.dtype) for name, value in values.items()}
    gradient, coarse = build(shapes)(*values.values())
    return gradient.reshape(24, 24, 512), coarse


def solution(mesh):
    placed = (
        P("lat", "lon", None),
        P(),
        P(),
        P(),
        P(),
        P(),
        P("lon", None),
        P(None, "lon"),
        P("lon", None),
        P("lat", "lon", None),
        P("lat", "lon", None),
        P("lat", "lon", None),
    )
    return jax.shard_map(
        shards,
        mesh=mesh,
        in_specs=placed,
        out_specs=(P("lat", "lon", None), P("lat", "lon", None)),
        check_vma=False,
    )
```

```python
from types import SimpleNamespace

import jax
import jax.numpy as jnp
import numpy as np
from jax import lax
from jax.experimental import pallas as pl
from jax.experimental.pallas import tpu as pltpu
from jax.sharding import PartitionSpec as P

HD = 64
WH = 6
WW = 12
WP = 80
KP = 48
EPS = 1e-05
LAT = 8
LON = 16
bf16 = jnp.bfloat16
f32 = jnp.float32
MESH = pl.DeviceIdType.MESH


def window_order(cols):
    across = cols // WW

    def index(r, c):
        return ((r // WH) * across + c // WW) * WP + (r % WH) * WW + c % WW

    return index


def raster(stride):
    return lambda r, c: r * stride + c


def fold_order(inner, stride):
    def index(r, c):
        return ((c % 2) * 2 + r % 2) * stride + inner(r // 2, c // 2)

    return index


def shift_maps(size, src, n_src, dst, n_dst):
    dr, dc = WH // 2, WW // 2
    up = -(-(size - dr) * dc // 32) * 32
    down = -(-max(dr * (size - dc), 0) // 32) * 32
    corner = 32
    parts = [(0, up, 0, 1), (up, down, 1, 0), (up + down, corner, 1, 1)]
    total = up + down + corner
    own = np.zeros((n_dst, n_src), np.float32)
    halo = np.zeros((n_dst, total), np.float32)
    pack = np.zeros((total, n_src), np.float32)
    for r in range(size):
        for c in range(size):
            to = dst(r, c)
            if r >= dr and c >= dc:
                own[to, src(r - dr, c - dc)] = 1
                continue
            if r >= dr:
                slot = (r - dr) * dc + c
            elif c >= dc:
                slot = up + r * (size - dc) + c - dc
            else:
                slot = up + down + r * dc + c
            halo[to, slot] = 1
            pack[slot, src((r - dr) % size, (c - dc) % size)] = 1
    return own, halo, pack, [part for part in parts if part[1]]


def window_bias(stride, rows, groups):
    token = np.arange(rows)
    real = token % stride < groups * 2
    upper = token % stride < groups
    allowed = np.broadcast_to(real[None, :], (rows, rows))
    split = allowed & (upper[:, None] == upper[None, :])
    both = np.stack([allowed, split])
    both = np.concatenate([both, both], 1)
    return np.where(both, 0.0, -1e30).astype(np.float32)


FINE = shift_maps(24, raster(24), 576, window_order(24), 640)
FOLD = shift_maps(24, window_order(24), 640, fold_order(window_order(12), 160), 640)
MID = shift_maps(12, raster(16), 192, window_order(12), 160)
FOLDC = shift_maps(12, window_order(12), 160, fold_order(raster(6), KP), 4 * KP)
COARSE = shift_maps(6, raster(16), 96, raster(6), KP)
BIAS = window_bias(WP, WP, 36)
BIASC = window_bias(KP, 2 * KP, 18)

SQUEEZE = np.zeros((144, 4 * KP), np.float32)
for k in range(4):
    SQUEEZE[k * 36 : (k + 1) * 36, k * KP : k * KP + 36] = np.eye(36)
TOP = 80
FINE_BAND = np.ascontiguousarray(FINE[0][160:320, 144 - TOP : 304 - TOP])
FINE_BAND_BACK = np.ascontiguousarray(FINE[0][160:480, 144:288].T)
CONSTANTS = dict(
    fine_own=FINE_BAND, fine_halo=FINE[1], fine_pack=FINE[2],
    fine_own_t=FINE_BAND_BACK, fine_halo_t=FINE[1].T, fine_pack_t=FINE[2].T,
    fold_own=FOLD[0], fold_halo=FOLD[1], fold_pack=FOLD[2], fold_halo_t=FOLD[1].T, fold_pack_t=FOLD[2].T,
    mid_own=MID[0], mid_halo=MID[1], mid_pack=MID[2],
    foldc_own=FOLDC[0], foldc_halo=FOLDC[1], foldc_pack=FOLDC[2],
    foldc_own_t=FOLDC[0].T, foldc_halo_t=FOLDC[1].T, foldc_pack_t=FOLDC[2].T,
    squeeze=SQUEEZE, squeeze_t=SQUEEZE.T,
    coarse_halo=COARSE[1], coarse_pack=COARSE[2], coarse_halo_t=COARSE[1].T, coarse_pack_t=COARSE[2].T,
)

LOADED = (
    tuple(dict(tokens=1, fine_pack=1, fine_own=1, fine_halo=1)),
    tuple(dict(
        qkv_f=1, g_coarse=1, coarse_pack=1, g_mid=1, mid_pack=1, g_fine=1, bias=1, out_f=1, fold_pack=1, fold_own=1, fold_halo=1,
    )),
    tuple(dict(
        mrg_f=1, coarse_halo=1, squeeze=1, squeeze_t=1, qkv_m=1, out_m=1, foldc_pack=1, foldc_own=1, foldc_halo=1, biasc=1,
        mid_own=1, mid_halo=1, foldc_halo_t=1, foldc_own_t=1, foldc_pack_t=1, fold_halo_t=1, fold_pack_t=1,
        fine_halo_t=1, fine_own_t=1, fine_pack_t=1, coarse_halo_t=1, coarse_pack_t=1,
    )),
)
ALL_LOADED = [name for group in LOADED for name in group]


def nn(a, b):
    return jnp.dot(a, b, preferred_element_type=f32)


def nt(a, b):
    return lax.dot_general(a, b, (((1,), (1,)), ((), ())), preferred_element_type=f32)


def tn(a, b):
    return lax.dot_general(a, b, (((0,), (0,)), ((), ())), preferred_element_type=f32)


def norm_rows(x):
    centred = x - jnp.mean(x, axis=-1, keepdims=True)
    scale = lax.rsqrt(jnp.mean(centred * centred, axis=-1, keepdims=True) + EPS)
    return centred * scale, scale


def norm_back(d, h, scale):
    d = d.astype(bf16).astype(f32)
    h = h.astype(f32)
    return scale * (d - jnp.mean(d, axis=-1, keepdims=True) - h * jnp.mean(d * h, axis=-1, keepdims=True))


def norm_split(parts):
    size = sum(p.shape[-1] for p in parts)
    average = sum(jnp.sum(p, axis=-1, keepdims=True) for p in parts) / size
    parts = [p - average for p in parts]
    scale = lax.rsqrt(sum(jnp.sum(p * p, axis=-1, keepdims=True) for p in parts) / size + EPS)
    return [p * scale for p in parts], scale


def norm_back_split(ds, hs, scale):
    size = sum(d.shape[-1] for d in ds)
    ds = [d.astype(bf16).astype(f32) for d in ds]
    hs = [h.astype(f32) for h in hs]
    mean_d = sum(jnp.sum(d, axis=-1, keepdims=True) for d in ds) / size
    mean_dh = sum(jnp.sum(d * h, axis=-1, keepdims=True) for d, h in zip(ds, hs)) / size
    return [scale * (d - mean_d - h * mean_dh) for d, h in zip(ds, hs)]


def aligned(start, size, multiple):
    return pl.ds(pl.multiple_of(start, multiple), size)


def project_qkv(h, weight, tr, trr, rows, pairs, step):
    @pl.loop(0, rows // step)
    def _(i):
        part = aligned(i * step, step, 16)

        @pl.loop(0, pairs)
        def _(p):
            wide = nn(h[part, :], weight(p))
            tr[part, aligned(p * 384, 384, 128)] = wide.astype(bf16)
            ra, rb, rc = (pltpu.roll(wide[:, k * 128 : (k + 1) * 128], 64, 1) for k in range(3))
            low = lax.broadcasted_iota(jnp.int32, (1, 128), 1) < 64
            trr[part, aligned(p * 256, 128, 128)] = jnp.where(low, ra, rc).astype(bf16)
            trr[part, aligned(p * 256 + 128, 128, 128)] = jnp.where(low, rb, ra).astype(bf16)


def halves():
    lane = lax.broadcasted_iota(jnp.int32, (1, 128), 1)
    low = lane < 64
    one = jnp.where(low, 1.0, 0.0)
    return low, one.astype(bf16), (1.0 - one).astype(bf16)


def attend(tr, trr, ps, mix, bias, pairs, windows, wp, split, unroll, part=0, parts=1):
    steps = pairs * windows // unroll // parts

    @pl.loop(part * steps, (part + 1) * steps)
    def _(step):
        low, mlo, mhi = halves()
        for u in range(unroll):
            item = step * unroll + u
            w, p = lax.div(item, pairs), lax.rem(item, pairs)
            part = aligned(w * wp, wp, 16)
            a, b, c = (tr[part, aligned(p * 384 + k * 128, 128, 128)] for k in range(3))
            k2 = trr[part, aligned(p * 256, 128, 128)]
            eighth = jnp.asarray(HD**-0.5, bf16)
            q2 = jnp.concatenate([a * (mlo * eighth), b * (mhi * eighth)], 0)
            scores = nt(q2, k2) + bias[split(w)]
            e = jnp.exp(scores - jnp.max(scores, axis=-1, keepdims=True))
            weights = (e / jnp.sum(e, axis=-1, keepdims=True)).astype(bf16)
            ps[item] = weights
            mixed = jnp.where(low, nn(weights[:wp], b), nn(weights[wp:], c))
            mix[part, aligned(p * 128, 128, 128)] = mixed.astype(bf16)


def attend_back(tr, trr, ps, dmix, pairs, windows, wp, unroll):
    @pl.loop(0, pairs * windows // unroll)
    def _(step):
        low, mlo, mhi = halves()
        stores = []
        for u in range(unroll):
            item = step * unroll + u
            w, p = lax.div(item, pairs), lax.rem(item, pairs)
            part = aligned(w * wp, wp, 16)
            places = [(part, aligned(p * 384 + k * 128, 128, 128)) for k in range(3)]
            b, c = tr[places[1]], tr[places[2]]
            k2, q2 = (trr[part, aligned(p * 256 + k * 128, 128, 128)] for k in range(2))
            do = dmix[part, aligned(p * 128, 128, 128)]
            weights = ps[item]
            outs = []
            for half, mask, values in ((0, mlo, b), (1, mhi, c)):
                wt = weights[half * wp : (half + 1) * wp]
                wide = wt.astype(f32)
                dw = nt(do * mask, values)
                ds = wide * (dw - jnp.sum(wide * dw, axis=-1, keepdims=True)) * HD**-0.5
                outs.append((wt, ds.astype(bf16)))
            (w0, ds0), (w1, ds1) = outs
            stores.append((places[0], jnp.where(low, nn(ds0, k2), tn(ds0, q2)).astype(bf16)))
            stores.append((places[1], jnp.where(low, tn(w0, do), nn(ds1, k2)).astype(bf16)))
            stores.append((places[2], jnp.where(low, tn(ds1, q2), tn(w1, do)).astype(bf16)))
        for place, value in stores:
            tr[place] = value


def tiles(rows, step, cols, width, body):
    @pl.loop(0, rows // step)
    def _(i):
        part = aligned(i * step, step, 16)

        @pl.loop(0, cols // width)
        def _(j):
            body(part, aligned(j * width, width, 128))


VMEM_SCRATCH = dict(
    xf=((640, 512), bf16), hf=((640, 512), bf16), sf=((640, 1), f32), trf=((640, 1536), bf16),
    trrf=((640, 1024), bf16), psf=((32, 2 * WP, WP), bf16), mixf=((640, 512), bf16), yf=((640, 512), bf16),
    wide=((640, 512), f32),
    ff=((160, 2048), bf16), sff=((160, 1), f32),
    xm=((160, 1024), bf16), hm=((160, 1024), bf16), sm=((160, 1), f32), trm=((160, 3072), bf16),
    trrm=((160, 2048), bf16), psm=((16, 2 * WP, WP), bf16), mixm=((160, 1024), bf16), ym=((160, 1024), bf16),
    fc=((KP, 4096), bf16), sfc=((KP, 1), f32), fcs=((4, KP, 1024), bf16), fcr=((4, KP, 1024), bf16),
    pms=((4, 144, 512), bf16), pmr=((4, 144, 512), bf16), dmo=((144, 512), bf16), dms=((4, 144, 512), bf16), stage=((4, KP, 2048), bf16),
    dsr=((4, KP, 1024), bf16), dfc=((4 * KP, 1024), bf16),
    gm=((192, 1024), bf16), gc=((96, 2048), bf16),
    xc=((KP, 2048), bf16), hc=((KP, 2048), bf16), sc=((KP, 1), f32), hcs=((144, 512), bf16), hcr=((4, 144, 512), bf16),
    ac=((KP, 2048), bf16), acs=((144, 512), bf16), acr=((4, 144, 512), bf16),
    trc=((4 * KP, 1536), bf16), trrc=((4 * KP, 1024), bf16), psc=((8, 4 * KP, 2 * KP), bf16),
    mixc=((4 * KP, 512), bf16), dmixc=((4 * KP, 512), bf16),
    dhs=((4, 144, 512), bf16), dhr=((4, 144, 512), bf16), pos=((4, 144, 512), bf16), por=((4, 144, 512), bf16),
    yc=((KP, 2048), bf16),
    wm=((4, 256, 2048), bf16), wq=((4, 2048, 384), bf16), wo=((4, 128, 2048), bf16),
)
EXCHANGES = dict(
    tok=(FINE, 512, 1), gf=(FINE, 512, 1), gm=(MID, 1024, 1), gc=(COARSE, 2048, 1), fold=(FOLD, 512, 1), foldc=(FOLDC, 1024, 1),
    foldc_b=(FOLDC, 1024, -1), fold_b=(FOLD, 512, -1), fine_b=(FINE, 512, -1), coarse_b=(COARSE, 2048, -1),
)
SENT_FROM = dict(fold="tok", fold_b="tok", fine_b="tok", foldc_b="foldc", coarse_b="gc")
N_LOCAL = len(ALL_LOADED) + 7
N_REMOTE = 96


class Lazy:
    def __init__(self, make):
        self.make = make

    def __getattr__(self, name):
        value = self.make(name)
        setattr(self, name, value)
        return value


def build(shapes):
    scratch = dict(VMEM_SCRATCH)
    loaded = {name: shapes[name] for name in ALL_LOADED}
    for name in ("tokens", "g_fine"):
        loaded[name] = ((TOP + 576, 512), bf16)
    sends, receives = {}, {}
    for name, (maps, width, _) in EXCHANGES.items():
        receives[name] = ((maps[1].shape[1], width), bf16)
        if name not in SENT_FROM:
            sends[name] = receives[name]

    def kernel(*refs):
        refs = list(refs)

        def take(names):
            return {name: refs.pop(0) for name in names}

        hbm = take(shapes)
        grad_ref, coarse_ref = refs.pop(0), refs.pop(0)
        v = SimpleNamespace(**take(scratch))
        vm, send_buf, recv_buf = take(loaded), take(sends), take(receives)
        local_sem, send_sem, recv_sem = refs

        lat, lon = lax.axis_index("lat"), lax.axis_index("lon")
        y, z, core = lax.div(lon, 8), lax.rem(lax.div(lon, 2), 4), lax.rem(lon, 2)

        def near(dlat, dlon):
            return (lax.rem(lat + dlat + LAT, LAT), lax.rem(lon + dlon + LON, LON))

        def at(yy, zz, cc):
            return (lat, yy * 8 + zz * 2 + cc)

        def turn(k):
            return lax.rem(z + k, 4)

        loads = {}
        for i, name in enumerate(ALL_LOADED):
            dest = vm[name].at[pl.ds(TOP, 576)] if name in ("tokens", "g_fine") else vm[name]
            loads[name] = pltpu.make_async_copy(hbm[name], dest, local_sem.at[i])

        def start_loads(group):
            for name in group:
                loads[name].start()

        start_loads(LOADED[0])

        def wait_load(name):
            loads[name].wait()
            return vm[name]

        got = Lazy(wait_load)

        own_slot = y * 2 + core
        own_loads = []
        for i, name in enumerate(("wm", "wq", "wo")):
            copy = pltpu.make_async_copy(hbm[name], getattr(v, name).at[own_slot], local_sem.at[len(ALL_LOADED) + i])
            own_loads.append(copy)

        barrier = pltpu.get_barrier_semaphore()
        others = [near(1, 0), near(-1, 0), near(1, 1), near(-1, -1)]
        others += [(lat + 1 - 2 * lax.rem(lat, 2), lax.rem(lon + 8, LON))]
        others += [(lat, y * 8 + lax.rem(lax.rem(lon, 8) + k, 8)) for k in range(1, 8)]
        for device in others:
            pl.semaphore_signal(barrier, inc=1, device_id=device, device_id_type=MESH)
        place = lax.rem(lon, 8)

        @pl.when(place == 7)
        def _():
            pl.semaphore_signal(barrier, inc=1, device_id=near(0, 1), device_id_type=MESH)

        @pl.when(place == 0)
        def _():
            pl.semaphore_signal(barrier, inc=1, device_id=near(0, -1), device_id_type=MESH)

        edge = jnp.where((place == 7) | (place == 0), 1, 0)
        pl.semaphore_wait(barrier, len(others) + edge)

        counter = [0]

        def sems(n):
            counter[0] += n
            assert counter[0] <= N_REMOTE
            return counter[0] - n

        def remote(src, dst, send, recv, device):
            return pltpu.make_async_remote_copy(
                src_ref=src, dst_ref=dst, send_sem=send_sem.at[send], recv_sem=recv_sem.at[recv],
                device_id=device, device_id_type=MESH,
            )

        pending = []

        def sender(name):
            return send_buf[SENT_FROM.get(name, name)]

        def finish(copies):
            for copy in copies:
                copy.wait()

        def sent(copies):
            for copy in copies:
                copy.wait_send()

        def shift(name):
            maps, _, sign = EXCHANGES[name]
            base = sems(3)
            copies = []
            for k, (start, size, dlat, dlon) in enumerate(maps[3]):
                part = pl.ds(start, size)
                copies.append(
                    remote(sender(name).at[part], recv_buf[name].at[part], base + k, base + k, near(sign * dlat, sign * dlon))
                )
            for copy in copies:
                copy.start()
            return copies

        def received(copies):
            for copy in copies:
                copy.wait_recv()

        sibling = at(y, z, 1 - core)
        partner_slot = (1 - y) * 2 + core
        y_low = lax.rem(lat, 2)
        beside = lat + 1 - 2 * y_low

        def weight_piece(name, start, size):
            base = sems(2)
            dest = getattr(v, name)
            half = hbm[name].shape[0] // 2
            mine = aligned(y_low * half + start, size, 16)
            other = aligned((1 - y_low) * half + start, size, 16)
            there = dest.at[partner_slot, other]
            return (
                remote(hbm[name].at[mine], dest.at[own_slot, mine], base, base, (beside, lax.rem(lon + 8, LON))),
                remote(there, there, base + 1, base + 1, (beside, lon)),
            )

        def core_copies(name):
            base = sems(2)
            dest = getattr(v, name)
            there = dest.at[partner_slot]
            return (
                remote(hbm[name], dest.at[own_slot], base, base, sibling),
                remote(there, there, base + 1, base + 1, sibling),
            )

        pieces = dict(
            wm=[weight_piece("wm", 0, 128)],
            wq=[weight_piece("wq", 0, 640), weight_piece("wq", 640, 384)],
            wo=[weight_piece("wo", 0, 64)],
        )
        between_cores = {name: core_copies(name) for name in pieces}

        def cross_weights(name, i):
            pieces[name][i][0].start()

        def relay_weights(name, i):
            pieces[name][i][0].wait_recv()
            pieces[name][i][1].start()

        def pass_weights(name):
            for piece in pieces[name]:
                piece[1].wait_recv()
            between_cores[name][1].start()

        def weights_ready(name):
            for copy in between_cores[name]:
                copy.wait_recv()
                pending.append(copy)
            for piece in pieces[name]:
                pending.extend(piece)

        def pack(name, source, matrix):
            sender(name)[...] = nn(matrix[...], source).astype(bf16)

        tokens = got.tokens
        pack("tok", tokens[TOP:, :], got.fine_pack)
        shift_tok = shift("tok")
        start_loads(LOADED[1])
        tokens[0:TOP, :] = jnp.zeros((TOP, 512), bf16)
        vm["g_fine"][0:TOP, :] = jnp.zeros((TOP, 512), bf16)
        v.gm[...] = jnp.zeros_like(v.gm)
        v.gc[...] = jnp.zeros_like(v.gc)
        fine_own, fine_halo, qkv_f = got.fine_own, got.fine_halo, got.qkv_f

        def placed(part, source, name, own, halo):
            return nn(own[part, :], source[...]) + nn(halo[part, :], recv_buf[name][...])

        def placed_fine(i, source, name):
            return nn(fine_own[...], source[aligned(i * 144, 160, 16), :]) + nn(
                fine_halo[aligned(i * 160, 160, 16), :], recv_buf[name][...]
            )

        received(shift_tok)
        cross_weights("wm", 0)

        @pl.loop(0, 4)
        def _(i):
            part = aligned(i * 160, 160, 16)
            x = placed_fine(i, tokens, "tok")
            v.xf[part, :] = x.astype(bf16)
            h, scale = norm_rows(x)
            v.hf[part, :] = h.astype(bf16)
            v.sf[part, :] = scale

        for r in range(6):
            v.gc[16 * r : 16 * r + 6, :] = got.g_coarse[r]
        pack("gc", v.gc[...], got.coarse_pack)
        shift_gc = shift("gc")
        start_loads(LOADED[2])
        for copy in own_loads:
            copy.start()
        for name in pieces:
            between_cores[name][0].start()
        project_qkv(v.hf, lambda p: qkv_f[:, aligned(p * 384, 384, 128)], v.trf, v.trrf, 640, 4, 320)
        first = lat == 0
        bias, out_f = got.bias, got.out_f
        attend(v.trf, v.trrf, v.psf, v.mixf, bias, 4, 8, WP, lambda w: jnp.where(first & (w < 2), 1, 0), 4)

        def out_fine(part, cols):
            v.yf[part, cols] = (nn(v.mixf[part, :], out_f[:, cols]) + v.xf[part, cols].astype(f32)).astype(bf16)

        tiles(640, 320, 512, 256, out_fine)

        sent(shift_tok)
        pack("fold", v.yf[...], got.fold_pack)
        shift_fold = shift("fold")
        fold_own, fold_halo, mrg_f = got.fold_own, got.fold_halo, got.mrg_f
        slot = lax.rem(z, 2) * 2 + core
        wide_group = lax.div(z, 2)

        def squeeze(x, dest):
            stacked = jnp.concatenate([x[:, k * 512 : (k + 1) * 512] for k in range(4)], 0)
            dest[...] = nn(got.squeeze[...], stacked).astype(bf16)

        def spread(packed):
            stacked = nn(got.squeeze_t[...], packed.astype(bf16))
            return [stacked[k * KP : (k + 1) * KP] for k in range(4)]

        def spread_all(packed):
            for s in range(4):
                for k, part in enumerate(spread(packed[s])):
                    v.stage[s, :, k * 512 : (k + 1) * 512] = part.astype(bf16)

        def total_of(packed):
            return jnp.concatenate(spread(sum(packed[k].astype(f32) for k in range(4))), 1)

        def to_group(source, dest):
            send, recv = sems(4), sems(4)
            for k in range(1, 4):
                copy = remote(source, dest.at[slot], send + k, recv + slot, at(y, turn(k), wide_group))
                copy.start()
                pending.append(copy)
            across = remote(source, dest.at[slot], send, recv + slot, sibling)

            @pl.when(core == wide_group)
            def _():
                dest[slot] = source[...]

            @pl.when(core != wide_group)
            def _():
                across.start()

            return source, dest, send, recv, across

        def is_own(s):
            return (z == core * 2 + s // 2) & (core == s % 2)

        def from_group(handle):
            source, dest, send, recv, across = handle

            @pl.when(core != wide_group)
            def _():
                across.wait_send()

            for s in range(4):

                @pl.when(jnp.logical_not(is_own(s)))
                def _(s=s):
                    remote(source, dest.at[s], send, recv + s, sibling).wait_recv()

        def to_owners(source, dest):
            send, recv = sems(4), sems(4)
            for s in range(4):
                copy = remote(source.at[s], dest.at[z], send + s, recv + z, at(y, core * 2 + s // 2, s % 2))

                @pl.when(is_own(s))
                def _(s=s):
                    dest[z] = source[s]

                @pl.when(jnp.logical_not(is_own(s)))
                def _(copy=copy):
                    copy.start()

            return source, dest, send, recv

        def from_members(handle):
            source, dest, send, recv = handle
            for k in range(4):

                @pl.when(jnp.logical_not((z == k) & (core == wide_group)))
                def _(k=k):
                    remote(source.at[0], dest.at[k], send, recv + k, sibling).wait_recv()

            for s in range(4):

                @pl.when(jnp.logical_not(is_own(s)))
                def _(s=s):
                    remote(source.at[s], dest.at[0], send + s, recv, sibling).wait_send()

        def around(pick, dest, own):
            base = sems(4)
            copies = []
            for k in range(1, 4):
                copy = remote(pick(k), dest.at[z], base + k, base + k, at(y, turn(k), core))
                copy.start()
                copies.append(copy)
            dest[z] = own
            return copies

        finish(shift_gc)
        v.ac[...] = nn(got.coarse_halo[...], recv_buf["gc"][...]).astype(bf16)
        squeeze(v.ac[...], v.acs)
        received(shift_fold)
        adjoint = to_group(v.acs, v.acr)
        relay_weights("wm", 0)
        cross_weights("wq", 0)

        quads = [placed(slice(k * 160, (k + 1) * 160), v.yf, "fold", fold_own, fold_halo) for k in range(4)]
        normed, scale = norm_split(quads)
        for k in range(4):
            v.ff[:, k * 512 : (k + 1) * 512] = normed[k].astype(bf16)
        v.sff[...] = scale
        def merge_fine(part, cols):
            v.xm[part, cols] = nn(v.ff[part, :], mrg_f[:, cols]).astype(bf16)

        tiles(160, 160, 1024, 256, merge_fine)

        for r in range(12):
            v.gm[16 * r : 16 * r + 12, :] = got.g_mid[r]
        pack("gm", v.gm[...], got.mid_pack)
        shift_gm = shift("gm")
        pack("gf", got.g_fine[TOP:, :], got.fine_pack)
        shift_gf = shift("gf")

        qkv_m, out_m = got.qkv_m, got.out_m
        h, scale = norm_rows(v.xm[...].astype(f32))
        v.hm[...] = h.astype(bf16)
        v.sm[...] = scale
        project_qkv(v.hm, lambda p: qkv_m[:, aligned(p * 384, 384, 128)], v.trm, v.trrm, 160, 8, 160)
        attend(v.trm, v.trrm, v.psm, v.mixm, bias, 8, 2, WP, lambda w: jnp.where(first & (w < 1), 1, 0), 4)

        def out_mid(part, cols):
            v.ym[part, cols] = (nn(v.mixm[part, :], out_m[:, cols]) + v.xm[part, cols].astype(f32)).astype(bf16)

        tiles(160, 160, 1024, 256, out_mid)

        pack("foldc", v.ym[...], got.foldc_pack)
        shift_foldc = shift("foldc")
        foldc_own, foldc_halo = got.foldc_own, got.foldc_halo
        received(shift_foldc)
        relay_weights("wq", 0)
        cross_weights("wq", 1)
        cross_weights("wo", 0)
        pass_weights("wm")
        folded = placed(slice(None), v.ym, "foldc", foldc_own, foldc_halo)
        quads = [folded[k * KP : (k + 1) * KP] for k in range(4)]
        normed, scale = norm_split(quads)
        v.sfc[...] = scale
        for k in range(4):
            h = normed[k].astype(bf16)
            v.fc[:, k * 1024 : (k + 1) * 1024] = h
            for j in range(2):
                block = 2 * k + j
                v.fcs[block % 4, :, (block // 4) * 512 : (block // 4 + 1) * 512] = h[:, j * 512 : (j + 1) * 512]
        copies = around(lambda k: v.fcs.at[turn(k)], v.fcr, v.fcs[z])
        finish(copies)
        for copy in own_loads:
            copy.wait()
        weights_ready("wm")
        gathered = v.fcr[...].reshape(4 * KP, 1024)

        @pl.loop(0, 8)
        def _(j):
            cols = aligned(j * 256, 256, 128)
            total = nn(gathered[:, 0:256], v.wm[0, :, cols])
            for s in range(1, 4):
                total += nn(gathered[:, s * 256 : (s + 1) * 256], v.wm[s, :, cols])
            v.stage[:, :, cols] = total.astype(bf16).reshape(4, KP, 256)

        for k in range(4):
            squeeze(v.stage[k], v.pms.at[k])
        copies = around(lambda k: v.pms.at[turn(k)], v.pmr, v.pms[z])
        relay_weights("wq", 1)
        relay_weights("wo", 0)
        finish(shift_gf)

        @pl.loop(0, 4)
        def _(i):
            part = aligned(i * 160, 160, 16)
            v.yf[part, :] = placed_fine(i, got.g_fine, "gf").astype(bf16)

        finish(copies)
        x = total_of(v.pmr).astype(bf16)
        v.xc[...] = x
        h, scale = norm_rows(x.astype(f32))
        v.hc[...] = h.astype(bf16)
        v.sc[...] = scale

        squeeze(v.hc[...], v.hcs)
        forward = to_group(v.hcs, v.hcr)
        pass_weights("wq")
        pass_weights("wo")
        biasc = got.biasc
        from_group(adjoint)
        spread_all(v.acr)
        weights_ready("wo")
        for p in range(4):
            v.dmixc[:, p * 128 : (p + 1) * 128] = nt(v.stage[...].reshape(4 * KP, 2048), v.wo[p]).astype(bf16)
        weights_ready("wq")
        from_group(forward)
        spread_all(v.hcr)
        project_qkv(v.stage.reshape(4 * KP, 2048), lambda p: v.wq[p], v.trc, v.trrc, 4 * KP, 4, 4 * KP)
        attend(v.trc, v.trrc, v.psc, v.mixc, biasc, 4, 2, 2 * KP, lambda w: jnp.where(first, 1, 0), 4)
        attend_back(v.trc, v.trrc, v.psc, v.dmixc, 4, 2, 2 * KP, 4)

        @pl.loop(0, 8)
        def _(j):
            rows = aligned(j * 256, 256, 128)
            total = nt(v.trc[:, 0:384], v.wq[0, rows, :])
            for s in range(1, 4):
                total += nt(v.trc[:, s * 384 : (s + 1) * 384], v.wq[s, rows, :])
            v.stage[:, :, rows] = total.astype(bf16).reshape(4, KP, 256)

        for k in range(4):
            squeeze(v.stage[k], v.dhs.at[k])
        backward = to_owners(v.dhs, v.dhr)

        @pl.loop(0, 8)
        def _(j):
            cols = aligned(j * 256, 256, 128)
            total = nn(v.mixc[:, 0:128], v.wo[0, :, cols])
            for s in range(1, 4):
                total += nn(v.mixc[:, s * 128 : (s + 1) * 128], v.wo[s, :, cols])
            v.stage[:, :, cols] = total.astype(bf16).reshape(4, KP, 256)

        for k in range(4):
            squeeze(v.stage[k], v.pos.at[k])
        from_members(backward)
        d = total_of(v.dhr)
        d = norm_back(d, v.hc[...], v.sc[...])
        d = (d.astype(bf16).astype(f32) + v.ac[...].astype(f32)).astype(bf16)
        squeeze(d, v.dmo)

        copies = around(lambda k: v.dmo, v.dms, v.dmo[...])
        finish(copies)
        spread_all(v.dms)
        gathered_d = v.stage[...].reshape(4 * KP, 2048)
        for s in range(4):
            block = nt(gathered_d, v.wm[s]).astype(bf16)
            v.fcs[:, :, s * 256 : (s + 1) * 256] = block.reshape(4, KP, 256)
        copies = around(lambda k: v.fcs.at[turn(k)], v.dsr, v.fcs[z])
        outward = to_owners(v.pos, v.por)
        finish(copies)

        ds = []
        hs = []
        for b in range(8):
            ds.append(v.dsr[b % 4, :, (b // 4) * 512 : (b // 4 + 1) * 512])
            hs.append(v.fc[:, b * 512 : (b + 1) * 512])
        for b, d in enumerate(norm_back_split(ds, hs, v.sfc[...])):
            k = b // 2
            v.dfc[k * KP : (k + 1) * KP, (b % 2) * 512 : (b % 2 + 1) * 512] = d.astype(bf16)
        sent(shift_foldc)
        pack("foldc_b", v.dfc[...], got.foldc_halo_t)
        copies = shift("foldc_b")
        foldc_own_t, foldc_pack_t = got.foldc_own_t, got.foldc_pack_t
        finish(shift_gm)
        adjoint_mid = placed(slice(None), v.gm, "gm", got.mid_own, got.mid_halo).astype(bf16).astype(f32)
        finish(copies)
        d = placed(slice(None), v.dfc, "foldc_b", foldc_own_t, foldc_pack_t)
        v.ym[...] = (adjoint_mid + d.astype(bf16).astype(f32)).astype(bf16)

        def dmix_mid(part, cols):
            v.mixm[part, cols] = nt(v.ym[part, :], out_m[cols, :]).astype(bf16)

        tiles(160, 160, 1024, 256, dmix_mid)
        attend_back(v.trm, v.trrm, v.psm, v.mixm, 8, 2, WP, 4)

        from_members(outward)
        total = total_of(v.por)
        v.yc[...] = (v.xc[...].astype(f32) + total).astype(bf16)
        pack("coarse_b", v.yc[...], got.coarse_halo_t)
        shift_out = shift("coarse_b")

        def to_wide(left, weight, blocks):
            @pl.loop(0, 2 * blocks)
            def _(j):
                v.wide[aligned(lax.div(j, 2) * 160, 160, 16), aligned(lax.rem(j, 2) * 256, 256, 128)] = nt(
                    left[...], weight[aligned(j * 256, 256, 128), :]
                )

        def wide_back(blocks, h, scale):
            ds = [v.wide[k * 160 : (k + 1) * 160, :] for k in range(blocks)]
            hs = [h[:, k * 512 : (k + 1) * 512] for k in range(blocks)]
            return [d.astype(bf16) for d in norm_back_split(ds, hs, scale[...])]

        to_wide(v.trm, qkv_m, 2)
        for k, d in enumerate(wide_back(2, v.hm, v.sm)):
            cols = slice(k * 512, (k + 1) * 512)
            v.xm[:, cols] = (d.astype(f32) + v.ym[:, cols].astype(f32)).astype(bf16)

        to_wide(v.xm, mrg_f, 4)
        for k, d in enumerate(wide_back(4, v.ff, v.sff)):
            v.mixf[k * 160 : (k + 1) * 160, :] = d
        sent(shift_fold)
        pack("fold_b", v.mixf[...], got.fold_halo_t)
        copies = shift("fold_b")
        fold_pack_t = got.fold_pack_t
        finish(copies)

        @pl.loop(0, 5)
        def _(i):
            part = aligned(i * 128, 128, 128)
            d = tn(fold_own[:, part], v.mixf[...]) + nn(fold_pack_t[part, :], recv_buf["fold_b"][...])
            v.yf[part, :] = (v.yf[part, :].astype(f32) + d.astype(bf16).astype(f32)).astype(bf16)

        def dmix_fine(part, cols):
            v.mixf[part, cols] = nt(v.yf[part, :], out_f[cols, :]).astype(bf16)

        tiles(640, 320, 512, 256, dmix_fine)
        attend_back(v.trf, v.trrf, v.psf, v.mixf, 4, 8, WP, 4)

        def dh_fine(part, cols):
            v.wide[part, cols] = nt(v.trf[part, :], qkv_f[cols, :])

        tiles(640, 320, 512, 256, dh_fine)

        @pl.loop(0, 4)
        def _(i):
            part = aligned(i * 160, 160, 16)
            d = norm_back(v.wide[part, :], v.hf[part, :], v.sf[part, :])
            v.xf[part, :] = (d.astype(bf16).astype(f32) + v.yf[part, :].astype(f32)).astype(bf16)

        pack("fine_b", v.xf[...], got.fine_halo_t)
        copies = shift("fine_b")
        fine_pack_t = got.fine_pack_t
        finish(shift_out)
        out = nn(got.coarse_pack_t[...], recv_buf["coarse_b"][...]).astype(bf16)
        for r in range(6):
            coarse_ref[r] = out[16 * r : 16 * r + 6]
        writes = []
        fine_own_t = got.fine_own_t
        for j in range(4):
            here = (j * 160, min(j * 160 + 320, 640))
            v.wide[pl.ds(j * 144, 144), :] = nn(fine_own_t[:, : here[1] - here[0]], v.xf[here[0] : here[1], :])
        finish(copies)
        for j in range(4):
            part = pl.ds(j * 144, 144)
            d = v.wide[part, :] + nn(fine_pack_t[part, :], recv_buf["fine_b"][...])
            tokens[part, :] = d.astype(bf16)
            writes.append(pltpu.make_async_copy(tokens.at[part], grad_ref.at[part], local_sem.at[len(ALL_LOADED) + 3 + j]))
            writes[-1].start()
        for write in writes:
            write.wait()
        for copy in pending:
            copy.wait_send()
        for name in ALL_LOADED:
            getattr(got, name)

    any_space = pl.BlockSpec(memory_space=pl.ANY)
    whole = pl.BlockSpec(memory_space=pltpu.VMEM)
    return pl.pallas_call(
        kernel,
        out_shape=(jax.ShapeDtypeStruct((576, 512), bf16), jax.ShapeDtypeStruct((6, 6, 2048), bf16)),
        in_specs=[any_space] * len(shapes),
        out_specs=(any_space, whole),
        scratch_shapes=[pltpu.VMEM(*shape) for group in (scratch, loaded, sends, receives) for shape in group.values()]
        + [pltpu.SemaphoreType.DMA((N_LOCAL,)), pltpu.SemaphoreType.DMA((N_REMOTE,)), pltpu.SemaphoreType.DMA((N_REMOTE,))],
        compiler_params=pltpu.CompilerParams(
            collective_id=0, has_side_effects=True, vmem_limit_bytes=66_584_576
        ),
    )


def shards(
    tokens, qkv_fine, out_fine, merge_fine, qkv_mid, out_mid, merge_mid, qkv_coarse, out_coarse, grad_fine, grad_mid, grad_coarse
):
    values = dict(
        tokens=tokens.reshape(576, 512),
        qkv_f=qkv_fine,
        out_f=out_fine,
        mrg_f=merge_fine,
        qkv_m=qkv_mid,
        out_m=out_mid,
        wm=merge_mid,
        wq=qkv_coarse,
        wo=out_coarse,
        g_fine=grad_fine.reshape(576, 512),
        g_mid=grad_mid,
        g_coarse=grad_coarse,
        bias=jnp.asarray(BIAS),
        biasc=jnp.asarray(BIASC),
    )
    for name, matrix in CONSTANTS.items():
        values[name] = jnp.asarray(matrix, bf16)
    shapes = {name: (value.shape, value.dtype) for name, value in values.items()}
    gradient, coarse = build(shapes)(*values.values())
    return gradient.reshape(24, 24, 512), coarse


def solution(mesh):
    placed = (
        P("lat", "lon", None),
        P(),
        P(),
        P(),
        P(),
        P(),
        P("lon", None),
        P(None, "lon"),
        P("lon", None),
        P("lat", "lon", None),
        P("lat", "lon", None),
        P("lat", "lon", None),
    )
    return jax.shard_map(
        shards,
        mesh=mesh,
        in_specs=placed,
        out_specs=(P("lat", "lon", None), P("lat", "lon", None)),
        check_vma=False,
    )
```

```python
from types import SimpleNamespace

import jax
import jax.numpy as jnp
import numpy as np
from jax import lax
from jax.experimental import pallas as pl
from jax.experimental.pallas import tpu as pltpu
from jax.sharding import PartitionSpec as P

HD = 64
WH = 6
WW = 12
WP = 80
KP = 48
EPS = 1e-05
LAT = 8
LON = 16
bf16 = jnp.bfloat16
f32 = jnp.float32
MESH = pl.DeviceIdType.MESH


def window_order(cols):
    across = cols // WW

    def index(r, c):
        return ((r // WH) * across + c // WW) * WP + (r % WH) * WW + c % WW

    return index


def raster(stride):
    return lambda r, c: r * stride + c


def fold_order(inner, stride):
    def index(r, c):
        return ((c % 2) * 2 + r % 2) * stride + inner(r // 2, c // 2)

    return index


def shift_maps(size, src, n_src, dst, n_dst):
    dr, dc = WH // 2, WW // 2
    up = -(-(size - dr) * dc // 32) * 32
    down = -(-max(dr * (size - dc), 0) // 32) * 32
    corner = 32
    parts = [(0, up, 0, 1), (up, down, 1, 0), (up + down, corner, 1, 1)]
    total = up + down + corner
    own = np.zeros((n_dst, n_src), np.float32)
    halo = np.zeros((n_dst, total), np.float32)
    pack = np.zeros((total, n_src), np.float32)
    for r in range(size):
        for c in range(size):
            to = dst(r, c)
            if r >= dr and c >= dc:
                own[to, src(r - dr, c - dc)] = 1
                continue
            if r >= dr:
                slot = (r - dr) * dc + c
            elif c >= dc:
                slot = up + r * (size - dc) + c - dc
            else:
                slot = up + down + r * dc + c
            halo[to, slot] = 1
            pack[slot, src((r - dr) % size, (c - dc) % size)] = 1
    return own, halo, pack, [part for part in parts if part[1]]


def window_bias(stride, rows, groups):
    token = np.arange(rows)
    real = token % stride < groups * 2
    upper = token % stride < groups
    allowed = np.broadcast_to(real[None, :], (rows, rows))
    split = allowed & (upper[:, None] == upper[None, :])
    both = np.stack([allowed, split])
    both = np.concatenate([both, both], 1)
    return np.where(both, 0.0, -1e30).astype(np.float32)


FINE = shift_maps(24, raster(24), 576, window_order(24), 640)
FOLD = shift_maps(24, window_order(24), 640, fold_order(window_order(12), 160), 640)
MID = shift_maps(12, raster(16), 192, window_order(12), 160)
FOLDC = shift_maps(12, window_order(12), 160, fold_order(raster(6), KP), 4 * KP)
COARSE = shift_maps(6, raster(16), 96, raster(6), KP)
BIAS = window_bias(WP, WP, 36)
BIASC = window_bias(KP, 2 * KP, 18)

SQUEEZE = np.zeros((144, 4 * KP), np.float32)
for k in range(4):
    SQUEEZE[k * 36 : (k + 1) * 36, k * KP : k * KP + 36] = np.eye(36)
TOP = 80
FINE_BAND = np.ascontiguousarray(FINE[0][160:320, 144 - TOP : 304 - TOP])
FINE_BAND_BACK = np.ascontiguousarray(FINE[0][160:480, 144:288].T)
CONSTANTS = dict(
    fine_own=FINE_BAND, fine_halo=FINE[1], fine_pack=FINE[2],
    fine_own_t=FINE_BAND_BACK, fine_halo_t=FINE[1].T, fine_pack_t=FINE[2].T,
    fold_own=FOLD[0], fold_halo=FOLD[1], fold_pack=FOLD[2], fold_halo_t=FOLD[1].T, fold_pack_t=FOLD[2].T,
    mid_own=MID[0], mid_halo=MID[1], mid_pack=MID[2],
    foldc_own=FOLDC[0], foldc_halo=FOLDC[1], foldc_pack=FOLDC[2],
    foldc_own_t=FOLDC[0].T, foldc_halo_t=FOLDC[1].T, foldc_pack_t=FOLDC[2].T,
    squeeze=SQUEEZE, squeeze_t=SQUEEZE.T,
    coarse_halo=COARSE[1], coarse_pack=COARSE[2], coarse_halo_t=COARSE[1].T, coarse_pack_t=COARSE[2].T,
)

LOADED = (
    tuple(dict(tokens=1, fine_pack=1, fine_own=1, fine_halo=1)),
    tuple(dict(
        qkv_f=1, g_coarse=1, coarse_pack=1, g_mid=1, mid_pack=1, g_fine=1, bias=1, out_f=1, fold_pack=1, fold_own=1, fold_halo=1,
    )),
    tuple(dict(
        mrg_f=1, coarse_halo=1, squeeze=1, squeeze_t=1, qkv_m=1, out_m=1, foldc_pack=1, foldc_own=1, foldc_halo=1, biasc=1,
        mid_own=1, mid_halo=1, foldc_halo_t=1, foldc_own_t=1, foldc_pack_t=1, fold_halo_t=1, fold_pack_t=1,
        fine_halo_t=1, fine_own_t=1, fine_pack_t=1, coarse_halo_t=1, coarse_pack_t=1,
    )),
)
ALL_LOADED = [name for group in LOADED for name in group]


def nn(a, b):
    return jnp.dot(a, b, preferred_element_type=f32)


def nt(a, b):
    return lax.dot_general(a, b, (((1,), (1,)), ((), ())), preferred_element_type=f32)


def tn(a, b):
    return lax.dot_general(a, b, (((0,), (0,)), ((), ())), preferred_element_type=f32)


def norm_rows(x):
    centred = x - jnp.mean(x, axis=-1, keepdims=True)
    scale = lax.rsqrt(jnp.mean(centred * centred, axis=-1, keepdims=True) + EPS)
    return centred * scale, scale


def norm_back(d, h, scale):
    d = d.astype(bf16).astype(f32)
    h = h.astype(f32)
    return scale * (d - jnp.mean(d, axis=-1, keepdims=True) - h * jnp.mean(d * h, axis=-1, keepdims=True))


def norm_split(parts):
    size = sum(p.shape[-1] for p in parts)
    average = sum(jnp.sum(p, axis=-1, keepdims=True) for p in parts) / size
    parts = [p - average for p in parts]
    scale = lax.rsqrt(sum(jnp.sum(p * p, axis=-1, keepdims=True) for p in parts) / size + EPS)
    return [p * scale for p in parts], scale


def norm_back_split(ds, hs, scale):
    size = sum(d.shape[-1] for d in ds)
    ds = [d.astype(bf16).astype(f32) for d in ds]
    hs = [h.astype(f32) for h in hs]
    mean_d = sum(jnp.sum(d, axis=-1, keepdims=True) for d in ds) / size
    mean_dh = sum(jnp.sum(d * h, axis=-1, keepdims=True) for d, h in zip(ds, hs)) / size
    return [scale * (d - mean_d - h * mean_dh) for d, h in zip(ds, hs)]


def aligned(start, size, multiple):
    return pl.ds(pl.multiple_of(start, multiple), size)


def project_qkv(h, weight, tr, trr, rows, pairs, step):
    @pl.loop(0, rows // step)
    def _(i):
        part = aligned(i * step, step, 16)

        @pl.loop(0, pairs, unroll=2)
        def _(p):
            wide = nn(h[part, :], weight(p))
            tr[part, aligned(p * 384, 384, 128)] = wide.astype(bf16)
            ra, rb, rc = (pltpu.roll(wide[:, k * 128 : (k + 1) * 128], 64, 1) for k in range(3))
            low = lax.broadcasted_iota(jnp.int32, (1, 128), 1) < 64
            trr[part, aligned(p * 256, 128, 128)] = jnp.where(low, ra, rc).astype(bf16)
            trr[part, aligned(p * 256 + 128, 128, 128)] = jnp.where(low, rb, ra).astype(bf16)


def halves():
    lane = lax.broadcasted_iota(jnp.int32, (1, 128), 1)
    low = lane < 64
    one = jnp.where(low, 1.0, 0.0)
    return low, one.astype(bf16), (1.0 - one).astype(bf16)


def attend(tr, trr, ps, mix, bias, pairs, windows, wp, split, unroll, part=0, parts=1):
    steps = pairs * windows // unroll // parts

    @pl.loop(part * steps, (part + 1) * steps)
    def _(step):
        low, mlo, mhi = halves()
        stores = []
        for u in range(unroll):
            item = step * unroll + u
            w, p = lax.div(item, pairs), lax.rem(item, pairs)
            part = aligned(w * wp, wp, 16)
            a, b, c = (tr[part, aligned(p * 384 + k * 128, 128, 128)] for k in range(3))
            k2 = trr[part, aligned(p * 256, 128, 128)]
            eighth = jnp.asarray(HD**-0.5, bf16)
            q2 = jnp.concatenate([a * (mlo * eighth), b * (mhi * eighth)], 0)
            scores = nt(q2, k2) + bias[split(w)]
            e = jnp.exp(scores - jnp.max(scores, axis=-1, keepdims=True))
            weights = (e / jnp.sum(e, axis=-1, keepdims=True)).astype(bf16)
            mixed = jnp.where(low, nn(weights[:wp], b), nn(weights[wp:], c))
            stores.append((item, weights, (part, aligned(p * 128, 128, 128)), mixed.astype(bf16)))
        for item, weights, place, mixed in stores:
            ps[item] = weights
            mix[place] = mixed


def attend_back(tr, trr, ps, dmix, pairs, windows, wp, unroll):
    @pl.loop(0, pairs * windows // unroll)
    def _(step):
        low, mlo, mhi = halves()
        stores = []
        for u in range(unroll):
            item = step * unroll + u
            w, p = lax.div(item, pairs), lax.rem(item, pairs)
            part = aligned(w * wp, wp, 16)
            places = [(part, aligned(p * 384 + k * 128, 128, 128)) for k in range(3)]
            b, c = tr[places[1]], tr[places[2]]
            k2, q2 = (trr[part, aligned(p * 256 + k * 128, 128, 128)] for k in range(2))
            do = dmix[part, aligned(p * 128, 128, 128)]
            weights = ps[item]
            outs = []
            for half, mask, values in ((0, mlo, b), (1, mhi, c)):
                wt = weights[half * wp : (half + 1) * wp]
                wide = wt.astype(f32)
                dw = nt(do * mask, values)
                ds = wide * (dw - jnp.sum(wide * dw, axis=-1, keepdims=True)) * HD**-0.5
                outs.append((wt, ds.astype(bf16)))
            (w0, ds0), (w1, ds1) = outs
            stores.append((places[0], jnp.where(low, nn(ds0, k2), tn(ds0, q2)).astype(bf16)))
            stores.append((places[1], jnp.where(low, tn(w0, do), nn(ds1, k2)).astype(bf16)))
            stores.append((places[2], jnp.where(low, tn(ds1, q2), tn(w1, do)).astype(bf16)))
        for place, value in stores:
            tr[place] = value


def tiles(rows, step, cols, width, body):
    @pl.loop(0, rows // step)
    def _(i):
        part = aligned(i * step, step, 16)

        @pl.loop(0, cols // width, unroll=2)
        def _(j):
            body(part, aligned(j * width, width, 128))


VMEM_SCRATCH = dict(
    xf=((640, 512), bf16), hf=((640, 512), bf16), sf=((640, 1), f32), trf=((640, 1536), bf16),
    trrf=((640, 1024), bf16), psf=((32, 2 * WP, WP), bf16), mixf=((640, 512), bf16), yf=((640, 512), bf16),
    wide=((640, 512), f32),
    ff=((160, 2048), bf16), sff=((160, 1), f32),
    xm=((160, 1024), bf16), hm=((160, 1024), bf16), sm=((160, 1), f32), trm=((160, 3072), bf16),
    trrm=((160, 2048), bf16), psm=((16, 2 * WP, WP), bf16), mixm=((160, 1024), bf16), ym=((160, 1024), bf16),
    fc=((KP, 4096), bf16), sfc=((KP, 1), f32), fcs=((4, KP, 1024), bf16), fcr=((4, KP, 1024), bf16),
    pms=((4, 144, 512), bf16), pmr=((4, 144, 512), bf16), dmo=((144, 512), bf16), dms=((4, 144, 512), bf16), stage=((4, KP, 2048), bf16),
    dsr=((4, KP, 1024), bf16), dfc=((4 * KP, 1024), bf16),
    gm=((192, 1024), bf16),
    xc=((KP, 2048), bf16), hc=((KP, 2048), bf16), sc=((KP, 1), f32), hcs=((144, 512), bf16), hcr=((4, 144, 512), bf16),
    ac=((KP, 2048), bf16), acs=((144, 512), bf16), acr=((4, 144, 512), bf16),
    trc=((4 * KP, 1536), bf16), trrc=((4 * KP, 1024), bf16), psc=((8, 4 * KP, 2 * KP), bf16),
    mixc=((4 * KP, 512), bf16), dmixc=((4 * KP, 512), bf16),
    dhs=((4, 144, 512), bf16), dhr=((4, 144, 512), bf16), pos=((4, 144, 512), bf16), por=((4, 144, 512), bf16),
    wm=((4, 256, 2048), bf16), wq=((4, 2048, 384), bf16), wo=((4, 128, 2048), bf16),
)
EXCHANGES = dict(
    tok=(FINE, 512, 1), gf=(FINE, 512, 1), gm=(MID, 1024, 1), gc=(COARSE, 2048, 1), fold=(FOLD, 512, 1), foldc=(FOLDC, 1024, 1),
    foldc_b=(FOLDC, 1024, -1), fold_b=(FOLD, 512, -1), fine_b=(FINE, 512, -1), coarse_b=(COARSE, 2048, -1),
)
SENT_FROM = dict(fold="tok", fold_b="tok", fine_b="tok", foldc_b="foldc", coarse_b="gc")
N_LOCAL = len(ALL_LOADED) + 7
N_REMOTE = 96


class Lazy:
    def __init__(self, make):
        self.make = make

    def __getattr__(self, name):
        value = self.make(name)
        setattr(self, name, value)
        return value


def build(shapes):
    scratch = dict(VMEM_SCRATCH)
    loaded = {name: shapes[name] for name in ALL_LOADED}
    for name in ("tokens", "g_fine"):
        loaded[name] = ((TOP + 576, 512), bf16)
    sends, receives = {}, {}
    for name, (maps, width, _) in EXCHANGES.items():
        receives[name] = ((maps[1].shape[1], width), bf16)
        if name not in SENT_FROM:
            sends[name] = receives[name]

    def kernel(*refs):
        refs = list(refs)

        def take(names):
            return {name: refs.pop(0) for name in names}

        hbm = take(shapes)
        grad_ref, coarse_ref = refs.pop(0), refs.pop(0)
        v = SimpleNamespace(**take(scratch))
        vm, send_buf, recv_buf = take(loaded), take(sends), take(receives)
        local_sem, send_sem, recv_sem = refs

        lat, lon = lax.axis_index("lat"), lax.axis_index("lon")
        y, z, core = lax.div(lon, 8), lax.rem(lax.div(lon, 2), 4), lax.rem(lon, 2)

        def near(dlat, dlon):
            return (lax.rem(lat + dlat + LAT, LAT), lax.rem(lon + dlon + LON, LON))

        def at(yy, zz, cc):
            return (lat, yy * 8 + zz * 2 + cc)

        def turn(k):
            return lax.rem(z + k, 4)

        loads = {}
        for i, name in enumerate(ALL_LOADED):
            dest = vm[name].at[pl.ds(TOP, 576)] if name in ("tokens", "g_fine") else vm[name]
            loads[name] = pltpu.make_async_copy(hbm[name], dest, local_sem.at[i])

        def start_loads(group):
            for name in group:
                loads[name].start()

        start_loads(LOADED[0])

        def wait_load(name):
            loads[name].wait()
            return vm[name]

        got = Lazy(wait_load)

        own_slot = y * 2 + core
        own_loads = []
        for i, name in enumerate(("wm", "wq", "wo")):
            copy = pltpu.make_async_copy(hbm[name], getattr(v, name).at[own_slot], local_sem.at[len(ALL_LOADED) + i])
            own_loads.append(copy)

        barrier = pltpu.get_barrier_semaphore()
        others = [near(1, 0), near(-1, 0), near(1, 1), near(-1, -1)]
        others += [(lat + 1 - 2 * lax.rem(lat, 2), lax.rem(lon + 8, LON))]
        others += [(lat, y * 8 + lax.rem(lax.rem(lon, 8) + k, 8)) for k in range(1, 8)]
        for device in others:
            pl.semaphore_signal(barrier, inc=1, device_id=device, device_id_type=MESH)
        place = lax.rem(lon, 8)

        @pl.when(place == 7)
        def _():
            pl.semaphore_signal(barrier, inc=1, device_id=near(0, 1), device_id_type=MESH)

        @pl.when(place == 0)
        def _():
            pl.semaphore_signal(barrier, inc=1, device_id=near(0, -1), device_id_type=MESH)

        edge = jnp.where((place == 7) | (place == 0), 1, 0)
        pl.semaphore_wait(barrier, len(others) + edge)

        counter = [0]

        def sems(n):
            counter[0] += n
            assert counter[0] <= N_REMOTE
            return counter[0] - n

        def remote(src, dst, send, recv, device):
            return pltpu.make_async_remote_copy(
                src_ref=src, dst_ref=dst, send_sem=send_sem.at[send], recv_sem=recv_sem.at[recv],
                device_id=device, device_id_type=MESH,
            )

        pending = []

        def sender(name):
            return send_buf[SENT_FROM.get(name, name)]

        def finish(copies):
            for copy in copies:
                copy.wait()

        def sent(copies):
            for copy in copies:
                copy.wait_send()

        def shift(name):
            maps, _, sign = EXCHANGES[name]
            base = sems(3)
            copies = []
            for k, (start, size, dlat, dlon) in enumerate(maps[3]):
                part = pl.ds(start, size)
                copies.append(
                    remote(sender(name).at[part], recv_buf[name].at[part], base + k, base + k, near(sign * dlat, sign * dlon))
                )
            for copy in copies:
                copy.start()
            return copies

        def received(copies):
            for copy in copies:
                copy.wait_recv()

        sibling = at(y, z, 1 - core)
        partner_slot = (1 - y) * 2 + core
        y_low = lax.rem(lat, 2)
        beside = lat + 1 - 2 * y_low

        def weight_piece(name, start, size):
            base = sems(2)
            dest = getattr(v, name)
            half = hbm[name].shape[0] // 2
            mine = aligned(y_low * half + start, size, 16)
            other = aligned((1 - y_low) * half + start, size, 16)
            there = dest.at[partner_slot, other]
            return (
                remote(hbm[name].at[mine], dest.at[own_slot, mine], base, base, (beside, lax.rem(lon + 8, LON))),
                remote(there, there, base + 1, base + 1, (beside, lon)),
            )

        def core_copies(name):
            base = sems(2)
            dest = getattr(v, name)
            there = dest.at[partner_slot]
            return (
                remote(hbm[name], dest.at[own_slot], base, base, sibling),
                remote(there, there, base + 1, base + 1, sibling),
            )

        pieces = dict(
            wm=[weight_piece("wm", 0, 128)],
            wq=[weight_piece("wq", 0, 640), weight_piece("wq", 640, 384)],
            wo=[weight_piece("wo", 0, 64)],
        )
        between_cores = {name: core_copies(name) for name in pieces}

        def cross_weights(name, i):
            pieces[name][i][0].start()

        def relay_weights(name, i):
            pieces[name][i][0].wait_recv()
            pieces[name][i][1].start()

        def pass_weights(name):
            for piece in pieces[name]:
                piece[1].wait_recv()
            between_cores[name][1].start()

        def weights_ready(name):
            for copy in between_cores[name]:
                copy.wait_recv()
                pending.append(copy)
            for piece in pieces[name]:
                pending.extend(piece)

        def pack(name, source, matrix):
            sender(name)[...] = nn(matrix[...], source).astype(bf16)

        tokens = got.tokens
        pack("tok", tokens[TOP:, :], got.fine_pack)
        shift_tok = shift("tok")
        start_loads(LOADED[1])
        tokens[0:TOP, :] = jnp.zeros((TOP, 512), bf16)
        vm["g_fine"][0:TOP, :] = jnp.zeros((TOP, 512), bf16)
        v.gm[...] = jnp.zeros_like(v.gm)
        fine_own, fine_halo, qkv_f = got.fine_own, got.fine_halo, got.qkv_f

        def placed(part, source, name, own, halo):
            return nn(own[part, :], source[...]) + nn(halo[part, :], recv_buf[name][...])

        def placed_fine(i, source, name):
            return nn(fine_own[...], source[aligned(i * 144, 160, 16), :]) + nn(
                fine_halo[aligned(i * 160, 160, 16), :], recv_buf[name][...]
            )

        received(shift_tok)
        cross_weights("wm", 0)

        @pl.loop(0, 4, unroll=2)
        def _(i):
            part = aligned(i * 160, 160, 16)
            x = placed_fine(i, tokens, "tok")
            v.xf[part, :] = x.astype(bf16)
            h, scale = norm_rows(x)
            v.hf[part, :] = h.astype(bf16)
            v.sf[part, :] = scale

        for r in range(6):
            for k in range(2):
                v.gm[96 * k + 16 * r : 96 * k + 16 * r + 6, :] = got.g_coarse[r, :, k * 1024 : (k + 1) * 1024]
        for k in range(2):
            packed = nn(got.coarse_pack[...], v.gm[96 * k : 96 * (k + 1), :])
            sender("gc")[:, k * 1024 : (k + 1) * 1024] = packed.astype(bf16)
        shift_gc = shift("gc")
        start_loads(LOADED[2])
        for copy in own_loads:
            copy.start()
        for name in pieces:
            between_cores[name][0].start()
        project_qkv(v.hf, lambda p: qkv_f[:, aligned(p * 384, 384, 128)], v.trf, v.trrf, 640, 4, 320)
        first = lat == 0
        bias, out_f = got.bias, got.out_f
        attend(v.trf, v.trrf, v.psf, v.mixf, bias, 4, 8, WP, lambda w: jnp.where(first & (w < 2), 1, 0), 8)

        def out_fine(part, cols):
            v.yf[part, cols] = (nn(v.mixf[part, :], out_f[:, cols]) + v.xf[part, cols].astype(f32)).astype(bf16)

        tiles(640, 320, 512, 256, out_fine)

        sent(shift_tok)
        pack("fold", v.yf[...], got.fold_pack)
        shift_fold = shift("fold")
        fold_own, fold_halo, mrg_f = got.fold_own, got.fold_halo, got.mrg_f
        slot = lax.rem(z, 2) * 2 + core
        wide_group = lax.div(z, 2)

        def squeeze(x, dest):
            stacked = jnp.concatenate([x[:, k * 512 : (k + 1) * 512] for k in range(4)], 0)
            dest[...] = nn(got.squeeze[...], stacked).astype(bf16)

        def spread(packed):
            stacked = nn(got.squeeze_t[...], packed.astype(bf16))
            return [stacked[k * KP : (k + 1) * KP] for k in range(4)]

        def spread_all(packed):
            for s in range(4):
                for k, part in enumerate(spread(packed[s])):
                    v.stage[s, :, k * 512 : (k + 1) * 512] = part.astype(bf16)

        def total_of(packed):
            return jnp.concatenate(spread(sum(packed[k].astype(f32) for k in range(4))), 1)

        def to_group(source, dest):
            send, recv = sems(4), sems(4)
            for k in range(1, 4):
                copy = remote(source, dest.at[slot], send + k, recv + slot, at(y, turn(k), wide_group))
                copy.start()
                pending.append(copy)
            across = remote(source, dest.at[slot], send, recv + slot, sibling)

            @pl.when(core == wide_group)
            def _():
                dest[slot] = source[...]

            @pl.when(core != wide_group)
            def _():
                across.start()

            return source, dest, send, recv, across

        def is_own(s):
            return (z == core * 2 + s // 2) & (core == s % 2)

        def from_group(handle):
            source, dest, send, recv, across = handle

            @pl.when(core != wide_group)
            def _():
                across.wait_send()

            for s in range(4):

                @pl.when(jnp.logical_not(is_own(s)))
                def _(s=s):
                    remote(source, dest.at[s], send, recv + s, sibling).wait_recv()

        def to_owners(source, dest):
            send, recv = sems(4), sems(4)
            for s in range(4):
                copy = remote(source.at[s], dest.at[z], send + s, recv + z, at(y, core * 2 + s // 2, s % 2))

                @pl.when(is_own(s))
                def _(s=s):
                    dest[z] = source[s]

                @pl.when(jnp.logical_not(is_own(s)))
                def _(copy=copy):
                    copy.start()

            return source, dest, send, recv

        def from_members(handle):
            source, dest, send, recv = handle
            for k in range(4):

                @pl.when(jnp.logical_not((z == k) & (core == wide_group)))
                def _(k=k):
                    remote(source.at[0], dest.at[k], send, recv + k, sibling).wait_recv()

            for s in range(4):

                @pl.when(jnp.logical_not(is_own(s)))
                def _(s=s):
                    remote(source.at[s], dest.at[0], send + s, recv, sibling).wait_send()

        def around(pick, dest, own):
            base = sems(4)
            copies = []
            for k in range(1, 4):
                copy = remote(pick(k), dest.at[z], base + k, base + k, at(y, turn(k), core))
                copy.start()
                copies.append(copy)
            dest[z] = own
            return copies

        finish(shift_gc)
        v.ac[...] = nn(got.coarse_halo[...], recv_buf["gc"][...]).astype(bf16)
        squeeze(v.ac[...], v.acs)
        received(shift_fold)
        adjoint = to_group(v.acs, v.acr)
        relay_weights("wm", 0)
        cross_weights("wq", 0)

        quads = [placed(slice(k * 160, (k + 1) * 160), v.yf, "fold", fold_own, fold_halo) for k in range(4)]
        normed, scale = norm_split(quads)
        for k in range(4):
            v.ff[:, k * 512 : (k + 1) * 512] = normed[k].astype(bf16)
        v.sff[...] = scale
        def merge_fine(part, cols):
            v.xm[part, cols] = nn(v.ff[part, :], mrg_f[:, cols]).astype(bf16)

        tiles(160, 160, 1024, 256, merge_fine)

        for r in range(12):
            v.gm[16 * r : 16 * r + 12, :] = got.g_mid[r]
        pack("gm", v.gm[...], got.mid_pack)
        shift_gm = shift("gm")
        pack("gf", got.g_fine[TOP:, :], got.fine_pack)
        shift_gf = shift("gf")

        qkv_m, out_m = got.qkv_m, got.out_m
        h, scale = norm_rows(v.xm[...].astype(f32))
        v.hm[...] = h.astype(bf16)
        v.sm[...] = scale
        project_qkv(v.hm, lambda p: qkv_m[:, aligned(p * 384, 384, 128)], v.trm, v.trrm, 160, 8, 160)
        attend(v.trm, v.trrm, v.psm, v.mixm, bias, 8, 2, WP, lambda w: jnp.where(first & (w < 1), 1, 0), 8)

        def out_mid(part, cols):
            v.ym[part, cols] = (nn(v.mixm[part, :], out_m[:, cols]) + v.xm[part, cols].astype(f32)).astype(bf16)

        tiles(160, 160, 1024, 256, out_mid)

        pack("foldc", v.ym[...], got.foldc_pack)
        shift_foldc = shift("foldc")
        foldc_own, foldc_halo = got.foldc_own, got.foldc_halo
        received(shift_foldc)
        relay_weights("wq", 0)
        cross_weights("wq", 1)
        cross_weights("wo", 0)
        pass_weights("wm")
        folded = placed(slice(None), v.ym, "foldc", foldc_own, foldc_halo)
        quads = [folded[k * KP : (k + 1) * KP] for k in range(4)]
        normed, scale = norm_split(quads)
        v.sfc[...] = scale
        for k in range(4):
            h = normed[k].astype(bf16)
            v.fc[:, k * 1024 : (k + 1) * 1024] = h
            for j in range(2):
                block = 2 * k + j
                v.fcs[block % 4, :, (block // 4) * 512 : (block // 4 + 1) * 512] = h[:, j * 512 : (j + 1) * 512]
        copies = around(lambda k: v.fcs.at[turn(k)], v.fcr, v.fcs[z])
        finish(copies)
        for copy in own_loads:
            copy.wait()
        weights_ready("wm")
        gathered = v.fcr[...].reshape(4 * KP, 1024)

        @pl.loop(0, 8, unroll=4)
        def _(j):
            cols = aligned(j * 256, 256, 128)
            total = nn(gathered[:, 0:256], v.wm[0, :, cols])
            for s in range(1, 4):
                total += nn(gathered[:, s * 256 : (s + 1) * 256], v.wm[s, :, cols])
            v.stage[:, :, cols] = total.astype(bf16).reshape(4, KP, 256)

        for k in range(4):
            squeeze(v.stage[k], v.pms.at[k])
        copies = around(lambda k: v.pms.at[turn(k)], v.pmr, v.pms[z])
        relay_weights("wq", 1)
        relay_weights("wo", 0)
        finish(shift_gf)

        @pl.loop(0, 4, unroll=2)
        def _(i):
            part = aligned(i * 160, 160, 16)
            v.yf[part, :] = placed_fine(i, got.g_fine, "gf").astype(bf16)

        finish(copies)
        x = total_of(v.pmr).astype(bf16)
        v.xc[...] = x
        h, scale = norm_rows(x.astype(f32))
        v.hc[...] = h.astype(bf16)
        v.sc[...] = scale

        squeeze(v.hc[...], v.hcs)
        forward = to_group(v.hcs, v.hcr)
        pass_weights("wq")
        pass_weights("wo")
        biasc = got.biasc
        from_group(adjoint)
        spread_all(v.acr)
        weights_ready("wo")
        for p in range(4):
            v.dmixc[:, p * 128 : (p + 1) * 128] = nt(v.stage[...].reshape(4 * KP, 2048), v.wo[p]).astype(bf16)
        weights_ready("wq")
        from_group(forward)
        spread_all(v.hcr)
        project_qkv(v.stage.reshape(4 * KP, 2048), lambda p: v.wq[p], v.trc, v.trrc, 4 * KP, 4, 4 * KP)
        attend(v.trc, v.trrc, v.psc, v.mixc, biasc, 4, 2, 2 * KP, lambda w: jnp.where(first, 1, 0), 8)
        attend_back(v.trc, v.trrc, v.psc, v.dmixc, 4, 2, 2 * KP, 8)

        @pl.loop(0, 8, unroll=4)
        def _(j):
            rows = aligned(j * 256, 256, 128)
            total = nt(v.trc[:, 0:384], v.wq[0, rows, :])
            for s in range(1, 4):
                total += nt(v.trc[:, s * 384 : (s + 1) * 384], v.wq[s, rows, :])
            v.stage[:, :, rows] = total.astype(bf16).reshape(4, KP, 256)

        for k in range(4):
            squeeze(v.stage[k], v.dhs.at[k])
        backward = to_owners(v.dhs, v.dhr)

        @pl.loop(0, 8, unroll=4)
        def _(j):
            cols = aligned(j * 256, 256, 128)
            total = nn(v.mixc[:, 0:128], v.wo[0, :, cols])
            for s in range(1, 4):
                total += nn(v.mixc[:, s * 128 : (s + 1) * 128], v.wo[s, :, cols])
            v.stage[:, :, cols] = total.astype(bf16).reshape(4, KP, 256)

        for k in range(4):
            squeeze(v.stage[k], v.pos.at[k])
        from_members(backward)
        d = total_of(v.dhr)
        d = norm_back(d, v.hc[...], v.sc[...])
        d = (d.astype(bf16).astype(f32) + v.ac[...].astype(f32)).astype(bf16)
        squeeze(d, v.dmo)

        copies = around(lambda k: v.dmo, v.dms, v.dmo[...])
        finish(copies)
        spread_all(v.dms)
        gathered_d = v.stage[...].reshape(4 * KP, 2048)
        for s in range(4):
            block = nt(gathered_d, v.wm[s]).astype(bf16)
            v.fcs[:, :, s * 256 : (s + 1) * 256] = block.reshape(4, KP, 256)
        copies = around(lambda k: v.fcs.at[turn(k)], v.dsr, v.fcs[z])
        outward = to_owners(v.pos, v.por)
        finish(copies)

        ds = []
        hs = []
        for b in range(8):
            ds.append(v.dsr[b % 4, :, (b // 4) * 512 : (b // 4 + 1) * 512])
            hs.append(v.fc[:, b * 512 : (b + 1) * 512])
        for b, d in enumerate(norm_back_split(ds, hs, v.sfc[...])):
            k = b // 2
            v.dfc[k * KP : (k + 1) * KP, (b % 2) * 512 : (b % 2 + 1) * 512] = d.astype(bf16)
        sent(shift_foldc)
        pack("foldc_b", v.dfc[...], got.foldc_halo_t)
        copies = shift("foldc_b")
        foldc_own_t, foldc_pack_t = got.foldc_own_t, got.foldc_pack_t
        finish(shift_gm)
        adjoint_mid = placed(slice(None), v.gm, "gm", got.mid_own, got.mid_halo).astype(bf16).astype(f32)
        finish(copies)
        d = placed(slice(None), v.dfc, "foldc_b", foldc_own_t, foldc_pack_t)
        v.ym[...] = (adjoint_mid + d.astype(bf16).astype(f32)).astype(bf16)

        def dmix_mid(part, cols):
            v.mixm[part, cols] = nt(v.ym[part, :], out_m[cols, :]).astype(bf16)

        tiles(160, 160, 1024, 256, dmix_mid)
        attend_back(v.trm, v.trrm, v.psm, v.mixm, 8, 2, WP, 8)

        from_members(outward)
        total = total_of(v.por)
        pack("coarse_b", (v.xc[...].astype(f32) + total).astype(bf16), got.coarse_halo_t)
        shift_out = shift("coarse_b")

        def to_wide(left, weight, blocks):
            @pl.loop(0, 2 * blocks, unroll=4)
            def _(j):
                v.wide[aligned(lax.div(j, 2) * 160, 160, 16), aligned(lax.rem(j, 2) * 256, 256, 128)] = nt(
                    left[...], weight[aligned(j * 256, 256, 128), :]
                )

        def wide_back(blocks, h, scale):
            ds = [v.wide[k * 160 : (k + 1) * 160, :] for k in range(blocks)]
            hs = [h[:, k * 512 : (k + 1) * 512] for k in range(blocks)]
            return [d.astype(bf16) for d in norm_back_split(ds, hs, scale[...])]

        to_wide(v.trm, qkv_m, 2)
        for k, d in enumerate(wide_back(2, v.hm, v.sm)):
            cols = slice(k * 512, (k + 1) * 512)
            v.xm[:, cols] = (d.astype(f32) + v.ym[:, cols].astype(f32)).astype(bf16)

        to_wide(v.xm, mrg_f, 4)
        for k, d in enumerate(wide_back(4, v.ff, v.sff)):
            v.mixf[k * 160 : (k + 1) * 160, :] = d
        sent(shift_fold)
        pack("fold_b", v.mixf[...], got.fold_halo_t)
        copies = shift("fold_b")
        fold_pack_t = got.fold_pack_t
        finish(copies)

        @pl.loop(0, 5, unroll=5)
        def _(i):
            part = aligned(i * 128, 128, 128)
            d = tn(fold_own[:, part], v.mixf[...]) + nn(fold_pack_t[part, :], recv_buf["fold_b"][...])
            v.yf[part, :] = (v.yf[part, :].astype(f32) + d.astype(bf16).astype(f32)).astype(bf16)

        def dmix_fine(part, cols):
            v.mixf[part, cols] = nt(v.yf[part, :], out_f[cols, :]).astype(bf16)

        tiles(640, 320, 512, 256, dmix_fine)
        attend_back(v.trf, v.trrf, v.psf, v.mixf, 4, 8, WP, 8)

        def dh_fine(part, cols):
            v.wide[part, cols] = nt(v.trf[part, :], qkv_f[cols, :])

        tiles(640, 320, 512, 256, dh_fine)

        @pl.loop(0, 4, unroll=2)
        def _(i):
            part = aligned(i * 160, 160, 16)
            d = norm_back(v.wide[part, :], v.hf[part, :], v.sf[part, :])
            v.xf[part, :] = (d.astype(bf16).astype(f32) + v.yf[part, :].astype(f32)).astype(bf16)

        pack("fine_b", v.xf[...], got.fine_halo_t)
        copies = shift("fine_b")
        fine_pack_t = got.fine_pack_t
        finish(shift_out)
        out = nn(got.coarse_pack_t[...], recv_buf["coarse_b"][...]).astype(bf16)
        for r in range(6):
            coarse_ref[r] = out[16 * r : 16 * r + 6]
        writes = []
        fine_own_t = got.fine_own_t
        for j in range(4):
            here = (j * 160, min(j * 160 + 320, 640))
            v.wide[pl.ds(j * 144, 144), :] = nn(fine_own_t[:, : here[1] - here[0]], v.xf[here[0] : here[1], :])
        finish(copies)
        for j in range(4):
            part = pl.ds(j * 144, 144)
            d = v.wide[part, :] + nn(fine_pack_t[part, :], recv_buf["fine_b"][...])
            tokens[part, :] = d.astype(bf16)
            writes.append(pltpu.make_async_copy(tokens.at[part], grad_ref.at[part], local_sem.at[len(ALL_LOADED) + 3 + j]))
            writes[-1].start()
        for write in writes:
            write.wait()
        for copy in pending:
            copy.wait_send()
        for name in ALL_LOADED:
            getattr(got, name)

    any_space = pl.BlockSpec(memory_space=pl.ANY)
    whole = pl.BlockSpec(memory_space=pltpu.VMEM)
    return pl.pallas_call(
        kernel,
        out_shape=(jax.ShapeDtypeStruct((576, 512), bf16), jax.ShapeDtypeStruct((6, 6, 2048), bf16)),
        in_specs=[any_space] * len(shapes),
        out_specs=(any_space, whole),
        scratch_shapes=[pltpu.VMEM(*shape) for group in (scratch, loaded, sends, receives) for shape in group.values()]
        + [pltpu.SemaphoreType.DMA((N_LOCAL,)), pltpu.SemaphoreType.DMA((N_REMOTE,)), pltpu.SemaphoreType.DMA((N_REMOTE,))],
        compiler_params=pltpu.CompilerParams(
            collective_id=0, has_side_effects=True, vmem_limit_bytes=66_584_576
        ),
    )


def shards(
    tokens, qkv_fine, out_fine, merge_fine, qkv_mid, out_mid, merge_mid, qkv_coarse, out_coarse, grad_fine, grad_mid, grad_coarse
):
    values = dict(
        tokens=tokens.reshape(576, 512),
        qkv_f=qkv_fine,
        out_f=out_fine,
        mrg_f=merge_fine,
        qkv_m=qkv_mid,
        out_m=out_mid,
        wm=merge_mid,
        wq=qkv_coarse,
        wo=out_coarse,
        g_fine=grad_fine.reshape(576, 512),
        g_mid=grad_mid,
        g_coarse=grad_coarse,
        bias=jnp.asarray(BIAS),
        biasc=jnp.asarray(BIASC),
    )
    for name, matrix in CONSTANTS.items():
        values[name] = jnp.asarray(matrix, bf16)
    shapes = {name: (value.shape, value.dtype) for name, value in values.items()}
    gradient, coarse = build(shapes)(*values.values())
    return gradient.reshape(24, 24, 512), coarse


def solution(mesh):
    placed = (
        P("lat", "lon", None),
        P(),
        P(),
        P(),
        P(),
        P(),
        P("lon", None),
        P(None, "lon"),
        P("lon", None),
        P("lat", "lon", None),
        P("lat", "lon", None),
        P("lat", "lon", None),
    )
    return jax.shard_map(
        shards,
        mesh=mesh,
        in_specs=placed,
        out_specs=(P("lat", "lon", None), P("lat", "lon", None)),
        check_vma=False,
    )
```

```python
from types import SimpleNamespace

import jax
import jax.numpy as jnp
import numpy as np
from jax import lax
from jax.experimental import pallas as pl
from jax.experimental.pallas import tpu as pltpu
from jax.sharding import PartitionSpec as P

HD = 64
WH = 6
WW = 12
WP = 80
KP = 48
EPS = 1e-05
LAT = 8
LON = 16
bf16 = jnp.bfloat16
f32 = jnp.float32
MESH = pl.DeviceIdType.MESH


def window_order(cols):
    across = cols // WW

    def index(r, c):
        return ((r // WH) * across + c // WW) * WP + (r % WH) * WW + c % WW

    return index


def raster(stride):
    return lambda r, c: r * stride + c


def fold_order(inner, stride):
    def index(r, c):
        return ((c % 2) * 2 + r % 2) * stride + inner(r // 2, c // 2)

    return index


def shift_maps(size, src, n_src, dst, n_dst):
    dr, dc = WH // 2, WW // 2
    up = -(-(size - dr) * dc // 32) * 32
    down = -(-max(dr * (size - dc), 0) // 32) * 32
    corner = 32
    parts = [(0, up, 0, 1), (up, down, 1, 0), (up + down, corner, 1, 1)]
    total = up + down + corner
    own = np.zeros((n_dst, n_src), np.float32)
    halo = np.zeros((n_dst, total), np.float32)
    pack = np.zeros((total, n_src), np.float32)
    for r in range(size):
        for c in range(size):
            to = dst(r, c)
            if r >= dr and c >= dc:
                own[to, src(r - dr, c - dc)] = 1
                continue
            if r >= dr:
                slot = (r - dr) * dc + c
            elif c >= dc:
                slot = up + r * (size - dc) + c - dc
            else:
                slot = up + down + r * dc + c
            halo[to, slot] = 1
            pack[slot, src((r - dr) % size, (c - dc) % size)] = 1
    return own, halo, pack, [part for part in parts if part[1]]


def window_bias(stride, rows, groups):
    token = np.arange(rows)
    real = token % stride < groups * 2
    upper = token % stride < groups
    allowed = np.broadcast_to(real[None, :], (rows, rows))
    split = allowed & (upper[:, None] == upper[None, :])
    both = np.stack([allowed, split])
    both = np.concatenate([both, both], 1)
    return np.where(both, 0.0, -1e30).astype(np.float32)


FINE = shift_maps(24, raster(24), 576, window_order(24), 640)
FOLD = shift_maps(24, window_order(24), 640, fold_order(window_order(12), 160), 640)
MID = shift_maps(12, raster(16), 192, window_order(12), 160)
FOLDC = shift_maps(12, window_order(12), 160, fold_order(raster(6), KP), 4 * KP)
COARSE = shift_maps(6, raster(16), 96, raster(6), KP)
BIAS = window_bias(WP, WP, 36)
BIASC = window_bias(KP, 2 * KP, 18)

SQUEEZE = np.zeros((144, 4 * KP), np.float32)
for k in range(4):
    SQUEEZE[k * 36 : (k + 1) * 36, k * KP : k * KP + 36] = np.eye(36)
TOP = 80
FINE_BAND = np.ascontiguousarray(FINE[0][160:320, 144 - TOP : 304 - TOP])
FINE_BAND_BACK = np.ascontiguousarray(FINE[0][160:480, 144:288].T)
CONSTANTS = dict(
    fine_own=FINE_BAND, fine_halo=FINE[1], fine_pack=FINE[2],
    fine_own_t=FINE_BAND_BACK, fine_halo_t=FINE[1].T, fine_pack_t=FINE[2].T,
    fold_own=FOLD[0], fold_halo=FOLD[1], fold_pack=FOLD[2], fold_halo_t=FOLD[1].T, fold_pack_t=FOLD[2].T,
    mid_own=MID[0], mid_halo=MID[1], mid_pack=MID[2],
    foldc_own=FOLDC[0], foldc_halo=FOLDC[1], foldc_pack=FOLDC[2],
    foldc_own_t=FOLDC[0].T, foldc_halo_t=FOLDC[1].T, foldc_pack_t=FOLDC[2].T,
    squeeze=SQUEEZE, squeeze_t=SQUEEZE.T,
    coarse_halo=COARSE[1], coarse_pack=COARSE[2], coarse_halo_t=COARSE[1].T, coarse_pack_t=COARSE[2].T,
)

LOADED = (
    tuple(dict(tokens=1, fine_pack=1, fine_own=1, fine_halo=1)),
    tuple(dict(
        qkv_f=1, g_coarse=1, coarse_pack=1, g_mid=1, mid_pack=1, g_fine=1, bias=1, out_f=1, fold_pack=1, fold_own=1, fold_halo=1,
    )),
    tuple(dict(
        mrg_f=1, coarse_halo=1, squeeze=1, squeeze_t=1, qkv_m=1, out_m=1, foldc_pack=1, foldc_own=1, foldc_halo=1, biasc=1,
        mid_own=1, mid_halo=1, foldc_halo_t=1, foldc_own_t=1, foldc_pack_t=1, fold_halo_t=1, fold_pack_t=1,
        fine_halo_t=1, fine_own_t=1, fine_pack_t=1, coarse_halo_t=1, coarse_pack_t=1,
    )),
)
ALL_LOADED = [name for group in LOADED for name in group]


def nn(a, b):
    return jnp.dot(a, b, preferred_element_type=f32)


def nt(a, b):
    return lax.dot_general(a, b, (((1,), (1,)), ((), ())), preferred_element_type=f32)


def tn(a, b):
    return lax.dot_general(a, b, (((0,), (0,)), ((), ())), preferred_element_type=f32)


def norm_rows(x):
    centred = x - jnp.mean(x, axis=-1, keepdims=True)
    scale = lax.rsqrt(jnp.mean(centred * centred, axis=-1, keepdims=True) + EPS)
    return centred * scale, scale


def norm_back(d, h, scale):
    d = d.astype(bf16).astype(f32)
    h = h.astype(f32)
    return scale * (d - jnp.mean(d, axis=-1, keepdims=True) - h * jnp.mean(d * h, axis=-1, keepdims=True))


def norm_split(parts):
    size = sum(p.shape[-1] for p in parts)
    average = sum(jnp.sum(p, axis=-1, keepdims=True) for p in parts) / size
    parts = [p - average for p in parts]
    scale = lax.rsqrt(sum(jnp.sum(p * p, axis=-1, keepdims=True) for p in parts) / size + EPS)
    return [p * scale for p in parts], scale


def norm_back_split(ds, hs, scale):
    size = sum(d.shape[-1] for d in ds)
    ds = [d.astype(bf16).astype(f32) for d in ds]
    hs = [h.astype(f32) for h in hs]
    mean_d = sum(jnp.sum(d, axis=-1, keepdims=True) for d in ds) / size
    mean_dh = sum(jnp.sum(d * h, axis=-1, keepdims=True) for d, h in zip(ds, hs)) / size
    return [scale * (d - mean_d - h * mean_dh) for d, h in zip(ds, hs)]


def aligned(start, size, multiple):
    return pl.ds(pl.multiple_of(start, multiple), size)


def project_qkv(h, weight, tr, trr, rows, pairs, step):
    @pl.loop(0, rows // step)
    def _(i):
        part = aligned(i * step, step, 16)

        @pl.loop(0, pairs, unroll=2)
        def _(p):
            wide = nn(h[part, :], weight(p))
            tr[part, aligned(p * 384, 384, 128)] = wide.astype(bf16)
            ra, rb, rc = (pltpu.roll(wide[:, k * 128 : (k + 1) * 128], 64, 1) for k in range(3))
            low = lax.broadcasted_iota(jnp.int32, (1, 128), 1) < 64
            trr[part, aligned(p * 256, 128, 128)] = jnp.where(low, ra, rc).astype(bf16)
            trr[part, aligned(p * 256 + 128, 128, 128)] = jnp.where(low, rb, ra).astype(bf16)


def halves():
    lane = lax.broadcasted_iota(jnp.int32, (1, 128), 1)
    low = lane < 64
    one = jnp.where(low, 1.0, 0.0)
    return low, one.astype(bf16), (1.0 - one).astype(bf16)


def attend(tr, trr, ps, mix, bias, pairs, windows, wp, split, unroll, part=0, parts=1):
    steps = pairs * windows // unroll // parts

    @pl.loop(part * steps, (part + 1) * steps)
    def _(step):
        low, mlo, mhi = halves()
        stores = []
        for u in range(unroll):
            item = step * unroll + u
            w, p = lax.div(item, pairs), lax.rem(item, pairs)
            part = aligned(w * wp, wp, 16)
            a, b, c = (tr[part, aligned(p * 384 + k * 128, 128, 128)] for k in range(3))
            k2 = trr[part, aligned(p * 256, 128, 128)]
            eighth = jnp.asarray(HD**-0.5, bf16)
            q2 = jnp.concatenate([a * (mlo * eighth), b * (mhi * eighth)], 0)
            scores = nt(q2, k2) + bias[split(w)]
            e = jnp.exp(scores - jnp.max(scores, axis=-1, keepdims=True))
            weights = (e / jnp.sum(e, axis=-1, keepdims=True)).astype(bf16)
            mixed = jnp.where(low, nn(weights[:wp], b), nn(weights[wp:], c))
            stores.append((item, weights, (part, aligned(p * 128, 128, 128)), mixed.astype(bf16)))
        for item, weights, place, mixed in stores:
            ps[item] = weights
            mix[place] = mixed


def attend_back(tr, trr, ps, dmix, pairs, windows, wp, unroll):
    @pl.loop(0, pairs * windows // unroll)
    def _(step):
        low, mlo, mhi = halves()
        stores = []
        for u in range(unroll):
            item = step * unroll + u
            w, p = lax.div(item, pairs), lax.rem(item, pairs)
            part = aligned(w * wp, wp, 16)
            places = [(part, aligned(p * 384 + k * 128, 128, 128)) for k in range(3)]
            b, c = tr[places[1]], tr[places[2]]
            k2, q2 = (trr[part, aligned(p * 256 + k * 128, 128, 128)] for k in range(2))
            do = dmix[part, aligned(p * 128, 128, 128)]
            weights = ps[item]
            outs = []
            for half, mask, values in ((0, mlo, b), (1, mhi, c)):
                wt = weights[half * wp : (half + 1) * wp]
                wide = wt.astype(f32)
                dw = nt(do * mask, values)
                ds = wide * (dw - jnp.sum(wide * dw, axis=-1, keepdims=True)) * HD**-0.5
                outs.append((wt, ds.astype(bf16)))
            (w0, ds0), (w1, ds1) = outs
            stores.append((places[0], jnp.where(low, nn(ds0, k2), tn(ds0, q2)).astype(bf16)))
            stores.append((places[1], jnp.where(low, tn(w0, do), nn(ds1, k2)).astype(bf16)))
            stores.append((places[2], jnp.where(low, tn(ds1, q2), tn(w1, do)).astype(bf16)))
        for place, value in stores:
            tr[place] = value


def tiles(rows, step, cols, width, body):
    @pl.loop(0, rows // step)
    def _(i):
        part = aligned(i * step, step, 16)

        @pl.loop(0, cols // width, unroll=min(4, cols // width))
        def _(j):
            body(part, aligned(j * width, width, 128))


VMEM_SCRATCH = dict(
    xf=((640, 512), bf16), hf=((640, 512), bf16), sf=((640, 1), f32), trf=((640, 1536), bf16),
    trrf=((640, 1024), bf16), psf=((32, 2 * WP, WP), bf16), mixf=((640, 512), bf16), yf=((640, 512), bf16),
    wide=((640, 512), f32),
    ff=((160, 2048), bf16), sff=((160, 1), f32),
    xm=((160, 1024), bf16), hm=((160, 1024), bf16), sm=((160, 1), f32), trm=((160, 3072), bf16),
    trrm=((160, 2048), bf16), psm=((16, 2 * WP, WP), bf16), mixm=((160, 1024), bf16), ym=((160, 1024), bf16),
    fc=((KP, 4096), bf16), sfc=((KP, 1), f32), fcs=((4, KP, 1024), bf16), fcr=((4, KP, 1024), bf16),
    pms=((4, 144, 512), bf16), pmr=((4, 144, 512), bf16), dmo=((144, 512), bf16), dms=((4, 144, 512), bf16), stage=((4, KP, 2048), bf16),
    dsr=((4, KP, 1024), bf16), dfc=((4 * KP, 1024), bf16),
    gm=((192, 1024), bf16),
    xc=((KP, 2048), bf16), hc=((KP, 2048), bf16), sc=((KP, 1), f32), hcs=((144, 512), bf16), hcr=((4, 144, 512), bf16),
    ac=((KP, 2048), bf16), acs=((144, 512), bf16), acr=((4, 144, 512), bf16),
    trc=((4 * KP, 1536), bf16), trrc=((4 * KP, 1024), bf16), psc=((8, 4 * KP, 2 * KP), bf16),
    mixc=((4 * KP, 512), bf16), dmixc=((4 * KP, 512), bf16),
    dhs=((4, 144, 512), bf16), dhr=((4, 144, 512), bf16), pos=((4, 144, 512), bf16), por=((4, 144, 512), bf16),
    wm=((4, 256, 2048), bf16), wq=((4, 2048, 384), bf16), wo=((4, 128, 2048), bf16),
)
EXCHANGES = dict(
    tok=(FINE, 512, 1), gf=(FINE, 512, 1), gm=(MID, 1024, 1), gc=(COARSE, 2048, 1), fold=(FOLD, 512, 1), foldc=(FOLDC, 1024, 1),
    foldc_b=(FOLDC, 1024, -1), fold_b=(FOLD, 512, -1), fine_b=(FINE, 512, -1), coarse_b=(COARSE, 2048, -1),
)
SENT_FROM = dict(fold="tok", fold_b="tok", fine_b="tok", foldc_b="foldc", coarse_b="gc")
N_LOCAL = len(ALL_LOADED) + 7
N_REMOTE = 96


class Lazy:
    def __init__(self, make):
        self.make = make

    def __getattr__(self, name):
        value = self.make(name)
        setattr(self, name, value)
        return value


def build(shapes):
    scratch = dict(VMEM_SCRATCH)
    loaded = {name: shapes[name] for name in ALL_LOADED}
    for name in ("tokens", "g_fine"):
        loaded[name] = ((TOP + 576, 512), bf16)
    sends, receives = {}, {}
    for name, (maps, width, _) in EXCHANGES.items():
        receives[name] = ((maps[1].shape[1], width), bf16)
        if name not in SENT_FROM:
            sends[name] = receives[name]

    def kernel(*refs):
        refs = list(refs)

        def take(names):
            return {name: refs.pop(0) for name in names}

        hbm = take(shapes)
        grad_ref, coarse_ref = refs.pop(0), refs.pop(0)
        v = SimpleNamespace(**take(scratch))
        vm, send_buf, recv_buf = take(loaded), take(sends), take(receives)
        local_sem, send_sem, recv_sem = refs

        lat, lon = lax.axis_index("lat"), lax.axis_index("lon")
        y, z, core = lax.div(lon, 8), lax.rem(lax.div(lon, 2), 4), lax.rem(lon, 2)

        def near(dlat, dlon):
            return (lax.rem(lat + dlat + LAT, LAT), lax.rem(lon + dlon + LON, LON))

        def at(yy, zz, cc):
            return (lat, yy * 8 + zz * 2 + cc)

        def turn(k):
            return lax.rem(z + k, 4)

        loads = {}
        for i, name in enumerate(ALL_LOADED):
            dest = vm[name].at[pl.ds(TOP, 576)] if name in ("tokens", "g_fine") else vm[name]
            loads[name] = pltpu.make_async_copy(hbm[name], dest, local_sem.at[i])

        def start_loads(group):
            for name in group:
                loads[name].start()

        start_loads(LOADED[0])

        def wait_load(name):
            loads[name].wait()
            return vm[name]

        got = Lazy(wait_load)

        own_slot = y * 2 + core
        own_loads = []
        for i, name in enumerate(("wm", "wq", "wo")):
            copy = pltpu.make_async_copy(hbm[name], getattr(v, name).at[own_slot], local_sem.at[len(ALL_LOADED) + i])
            own_loads.append(copy)

        barrier = pltpu.get_barrier_semaphore()
        others = [near(1, 0), near(-1, 0), near(1, 1), near(-1, -1)]
        others += [(lat + 1 - 2 * lax.rem(lat, 2), lax.rem(lon + 8, LON))]
        others += [(lat, y * 8 + lax.rem(lax.rem(lon, 8) + k, 8)) for k in range(1, 8)]
        for device in others:
            pl.semaphore_signal(barrier, inc=1, device_id=device, device_id_type=MESH)
        place = lax.rem(lon, 8)

        @pl.when(place == 7)
        def _():
            pl.semaphore_signal(barrier, inc=1, device_id=near(0, 1), device_id_type=MESH)

        @pl.when(place == 0)
        def _():
            pl.semaphore_signal(barrier, inc=1, device_id=near(0, -1), device_id_type=MESH)

        edge = jnp.where((place == 7) | (place == 0), 1, 0)
        pl.semaphore_wait(barrier, len(others) + edge)

        counter = [0]

        def sems(n):
            counter[0] += n
            assert counter[0] <= N_REMOTE
            return counter[0] - n

        def remote(src, dst, send, recv, device):
            return pltpu.make_async_remote_copy(
                src_ref=src, dst_ref=dst, send_sem=send_sem.at[send], recv_sem=recv_sem.at[recv],
                device_id=device, device_id_type=MESH,
            )

        pending = []

        def sender(name):
            return send_buf[SENT_FROM.get(name, name)]

        def finish(copies):
            for copy in copies:
                copy.wait()

        def sent(copies):
            for copy in copies:
                copy.wait_send()

        def shift(name):
            maps, _, sign = EXCHANGES[name]
            base = sems(3)
            copies = []
            for k, (start, size, dlat, dlon) in enumerate(maps[3]):
                part = pl.ds(start, size)
                copies.append(
                    remote(sender(name).at[part], recv_buf[name].at[part], base + k, base + k, near(sign * dlat, sign * dlon))
                )
            for copy in copies:
                copy.start()
            return copies

        def received(copies):
            for copy in copies:
                copy.wait_recv()

        sibling = at(y, z, 1 - core)
        partner_slot = (1 - y) * 2 + core
        y_low = lax.rem(lat, 2)
        beside = lat + 1 - 2 * y_low

        def weight_piece(name, start, size):
            base = sems(2)
            dest = getattr(v, name)
            half = hbm[name].shape[0] // 2
            mine = aligned(y_low * half + start, size, 16)
            other = aligned((1 - y_low) * half + start, size, 16)
            there = dest.at[partner_slot, other]
            return (
                remote(hbm[name].at[mine], dest.at[own_slot, mine], base, base, (beside, lax.rem(lon + 8, LON))),
                remote(there, there, base + 1, base + 1, (beside, lon)),
            )

        def core_copies(name):
            base = sems(2)
            dest = getattr(v, name)
            there = dest.at[partner_slot]
            return (
                remote(hbm[name], dest.at[own_slot], base, base, sibling),
                remote(there, there, base + 1, base + 1, sibling),
            )

        pieces = dict(
            wm=[weight_piece("wm", 0, 128)],
            wq=[weight_piece("wq", 0, 640), weight_piece("wq", 640, 384)],
            wo=[weight_piece("wo", 0, 64)],
        )
        between_cores = {name: core_copies(name) for name in pieces}

        def cross_weights(name, i):
            pieces[name][i][0].start()

        def relay_weights(name, i):
            pieces[name][i][0].wait_recv()
            pieces[name][i][1].start()

        def pass_weights(name):
            for piece in pieces[name]:
                piece[1].wait_recv()
            between_cores[name][1].start()

        def weights_ready(name):
            for copy in between_cores[name]:
                copy.wait_recv()
                pending.append(copy)
            for piece in pieces[name]:
                pending.extend(piece)

        def pack(name, source, matrix):
            sender(name)[...] = nn(matrix[...], source).astype(bf16)

        tokens = got.tokens
        pack("tok", tokens[TOP:, :], got.fine_pack)
        shift_tok = shift("tok")
        start_loads(LOADED[1])
        tokens[0:TOP, :] = jnp.zeros((TOP, 512), bf16)
        vm["g_fine"][0:TOP, :] = jnp.zeros((TOP, 512), bf16)
        v.gm[...] = jnp.zeros_like(v.gm)
        fine_own, fine_halo, qkv_f = got.fine_own, got.fine_halo, got.qkv_f

        def placed(part, source, name, own, halo):
            return nn(own[part, :], source[...]) + nn(halo[part, :], recv_buf[name][...])

        def placed_fine(i, source, name):
            return nn(fine_own[...], source[aligned(i * 144, 160, 16), :]) + nn(
                fine_halo[aligned(i * 160, 160, 16), :], recv_buf[name][...]
            )

        received(shift_tok)
        cross_weights("wm", 0)

        @pl.loop(0, 4, unroll=2)
        def _(i):
            part = aligned(i * 160, 160, 16)
            x = placed_fine(i, tokens, "tok")
            v.xf[part, :] = x.astype(bf16)
            h, scale = norm_rows(x)
            v.hf[part, :] = h.astype(bf16)
            v.sf[part, :] = scale

        for r in range(6):
            for k in range(2):
                v.gm[96 * k + 16 * r : 96 * k + 16 * r + 6, :] = got.g_coarse[r, :, k * 1024 : (k + 1) * 1024]
        for k in range(2):
            packed = nn(got.coarse_pack[...], v.gm[96 * k : 96 * (k + 1), :])
            sender("gc")[:, k * 1024 : (k + 1) * 1024] = packed.astype(bf16)
        shift_gc = shift("gc")
        start_loads(LOADED[2])
        for copy in own_loads:
            copy.start()
        for name in pieces:
            between_cores[name][0].start()
        project_qkv(v.hf, lambda p: qkv_f[:, aligned(p * 384, 384, 128)], v.trf, v.trrf, 640, 4, 320)
        first = lat == 0
        bias, out_f = got.bias, got.out_f
        attend(v.trf, v.trrf, v.psf, v.mixf, bias, 4, 8, WP, lambda w: jnp.where(first & (w < 2), 1, 0), 8)

        def out_fine(part, cols):
            v.yf[part, cols] = (nn(v.mixf[part, :], out_f[:, cols]) + v.xf[part, cols].astype(f32)).astype(bf16)

        tiles(640, 320, 512, 256, out_fine)

        sent(shift_tok)
        pack("fold", v.yf[...], got.fold_pack)
        shift_fold = shift("fold")
        fold_own, fold_halo, mrg_f = got.fold_own, got.fold_halo, got.mrg_f
        slot = lax.rem(z, 2) * 2 + core
        wide_group = lax.div(z, 2)

        def squeeze(x, dest):
            stacked = jnp.concatenate([x[:, k * 512 : (k + 1) * 512] for k in range(4)], 0)
            dest[...] = nn(got.squeeze[...], stacked).astype(bf16)

        def spread(packed):
            stacked = nn(got.squeeze_t[...], packed.astype(bf16))
            return [stacked[k * KP : (k + 1) * KP] for k in range(4)]

        def spread_all(packed):
            for s in range(4):
                for k, part in enumerate(spread(packed[s])):
                    v.stage[s, :, k * 512 : (k + 1) * 512] = part.astype(bf16)

        def total_of(packed):
            return jnp.concatenate(spread(sum(packed[k].astype(f32) for k in range(4))), 1)

        def to_group(source, dest):
            send, recv = sems(4), sems(4)
            for k in range(1, 4):
                copy = remote(source, dest.at[slot], send + k, recv + slot, at(y, turn(k), wide_group))
                copy.start()
                pending.append(copy)
            across = remote(source, dest.at[slot], send, recv + slot, sibling)

            @pl.when(core == wide_group)
            def _():
                dest[slot] = source[...]

            @pl.when(core != wide_group)
            def _():
                across.start()

            return source, dest, send, recv, across

        def is_own(s):
            return (z == core * 2 + s // 2) & (core == s % 2)

        def from_group(handle):
            source, dest, send, recv, across = handle

            @pl.when(core != wide_group)
            def _():
                across.wait_send()

            for s in range(4):

                @pl.when(jnp.logical_not(is_own(s)))
                def _(s=s):
                    remote(source, dest.at[s], send, recv + s, sibling).wait_recv()

        def to_owners(source, dest):
            send, recv = sems(4), sems(4)
            for s in range(4):
                copy = remote(source.at[s], dest.at[z], send + s, recv + z, at(y, core * 2 + s // 2, s % 2))

                @pl.when(is_own(s))
                def _(s=s):
                    dest[z] = source[s]

                @pl.when(jnp.logical_not(is_own(s)))
                def _(copy=copy):
                    copy.start()

            return source, dest, send, recv

        def from_members(handle):
            source, dest, send, recv = handle
            for k in range(4):

                @pl.when(jnp.logical_not((z == k) & (core == wide_group)))
                def _(k=k):
                    remote(source.at[0], dest.at[k], send, recv + k, sibling).wait_recv()

            for s in range(4):

                @pl.when(jnp.logical_not(is_own(s)))
                def _(s=s):
                    remote(source.at[s], dest.at[0], send + s, recv, sibling).wait_send()

        def around(pick, dest, own):
            base = sems(4)
            copies = []
            for k in range(1, 4):
                copy = remote(pick(k), dest.at[z], base + k, base + k, at(y, turn(k), core))
                copy.start()
                copies.append(copy)
            dest[z] = own
            return copies

        for r in range(12):
            v.gm[16 * r : 16 * r + 12, :] = got.g_mid[r]
        pack("gm", v.gm[...], got.mid_pack)
        shift_gm = shift("gm")
        pack("gf", got.g_fine[TOP:, :], got.fine_pack)
        shift_gf = shift("gf")

        finish(shift_gc)
        v.ac[...] = nn(got.coarse_halo[...], recv_buf["gc"][...]).astype(bf16)
        squeeze(v.ac[...], v.acs)
        received(shift_fold)
        adjoint = to_group(v.acs, v.acr)
        relay_weights("wm", 0)
        cross_weights("wq", 0)

        quads = [placed(slice(k * 160, (k + 1) * 160), v.yf, "fold", fold_own, fold_halo) for k in range(4)]
        normed, scale = norm_split(quads)
        for k in range(4):
            v.ff[:, k * 512 : (k + 1) * 512] = normed[k].astype(bf16)
        v.sff[...] = scale
        def merge_fine(part, cols):
            v.xm[part, cols] = nn(v.ff[part, :], mrg_f[:, cols]).astype(bf16)

        tiles(160, 160, 1024, 256, merge_fine)

        qkv_m, out_m = got.qkv_m, got.out_m
        h, scale = norm_rows(v.xm[...].astype(f32))
        v.hm[...] = h.astype(bf16)
        v.sm[...] = scale
        project_qkv(v.hm, lambda p: qkv_m[:, aligned(p * 384, 384, 128)], v.trm, v.trrm, 160, 8, 160)
        attend(v.trm, v.trrm, v.psm, v.mixm, bias, 8, 2, WP, lambda w: jnp.where(first & (w < 1), 1, 0), 8)

        def out_mid(part, cols):
            v.ym[part, cols] = (nn(v.mixm[part, :], out_m[:, cols]) + v.xm[part, cols].astype(f32)).astype(bf16)

        tiles(160, 160, 1024, 256, out_mid)

        pack("foldc", v.ym[...], got.foldc_pack)
        shift_foldc = shift("foldc")
        foldc_own, foldc_halo = got.foldc_own, got.foldc_halo
        received(shift_foldc)
        relay_weights("wq", 0)
        cross_weights("wq", 1)
        cross_weights("wo", 0)
        pass_weights("wm")
        folded = placed(slice(None), v.ym, "foldc", foldc_own, foldc_halo)
        quads = [folded[k * KP : (k + 1) * KP] for k in range(4)]
        normed, scale = norm_split(quads)
        v.sfc[...] = scale
        for k in range(4):
            h = normed[k].astype(bf16)
            v.fc[:, k * 1024 : (k + 1) * 1024] = h
            for j in range(2):
                block = 2 * k + j
                v.fcs[block % 4, :, (block // 4) * 512 : (block // 4 + 1) * 512] = h[:, j * 512 : (j + 1) * 512]
        copies = around(lambda k: v.fcs.at[turn(k)], v.fcr, v.fcs[z])
        finish(copies)
        for copy in own_loads:
            copy.wait()
        weights_ready("wm")
        gathered = v.fcr[...].reshape(4 * KP, 1024)

        @pl.loop(0, 8, unroll=4)
        def _(j):
            cols = aligned(j * 256, 256, 128)
            total = nn(gathered[:, 0:256], v.wm[0, :, cols])
            for s in range(1, 4):
                total += nn(gathered[:, s * 256 : (s + 1) * 256], v.wm[s, :, cols])
            v.stage[:, :, cols] = total.astype(bf16).reshape(4, KP, 256)

        for k in range(4):
            squeeze(v.stage[k], v.pms.at[k])
        copies = around(lambda k: v.pms.at[turn(k)], v.pmr, v.pms[z])
        relay_weights("wq", 1)
        relay_weights("wo", 0)
        finish(shift_gf)

        @pl.loop(0, 4, unroll=2)
        def _(i):
            part = aligned(i * 160, 160, 16)
            v.yf[part, :] = placed_fine(i, got.g_fine, "gf").astype(bf16)

        finish(copies)
        x = total_of(v.pmr).astype(bf16)
        v.xc[...] = x
        h, scale = norm_rows(x.astype(f32))
        v.hc[...] = h.astype(bf16)
        v.sc[...] = scale

        squeeze(v.hc[...], v.hcs)
        forward = to_group(v.hcs, v.hcr)
        pass_weights("wq")
        pass_weights("wo")
        biasc = got.biasc
        from_group(adjoint)
        spread_all(v.acr)
        weights_ready("wo")
        for p in range(4):
            v.dmixc[:, p * 128 : (p + 1) * 128] = nt(v.stage[...].reshape(4 * KP, 2048), v.wo[p]).astype(bf16)
        weights_ready("wq")
        from_group(forward)
        spread_all(v.hcr)
        project_qkv(v.stage.reshape(4 * KP, 2048), lambda p: v.wq[p], v.trc, v.trrc, 4 * KP, 4, 4 * KP)
        attend(v.trc, v.trrc, v.psc, v.mixc, biasc, 4, 2, 2 * KP, lambda w: jnp.where(first, 1, 0), 8)
        attend_back(v.trc, v.trrc, v.psc, v.dmixc, 4, 2, 2 * KP, 8)

        @pl.loop(0, 8, unroll=4)
        def _(j):
            rows = aligned(j * 256, 256, 128)
            total = nt(v.trc[:, 0:384], v.wq[0, rows, :])
            for s in range(1, 4):
                total += nt(v.trc[:, s * 384 : (s + 1) * 384], v.wq[s, rows, :])
            v.stage[:, :, rows] = total.astype(bf16).reshape(4, KP, 256)

        for k in range(4):
            squeeze(v.stage[k], v.dhs.at[k])
        backward = to_owners(v.dhs, v.dhr)

        @pl.loop(0, 8, unroll=4)
        def _(j):
            cols = aligned(j * 256, 256, 128)
            total = nn(v.mixc[:, 0:128], v.wo[0, :, cols])
            for s in range(1, 4):
                total += nn(v.mixc[:, s * 128 : (s + 1) * 128], v.wo[s, :, cols])
            v.stage[:, :, cols] = total.astype(bf16).reshape(4, KP, 256)

        for k in range(4):
            squeeze(v.stage[k], v.pos.at[k])
        from_members(backward)
        d = total_of(v.dhr)
        d = norm_back(d, v.hc[...], v.sc[...])
        d = (d.astype(bf16).astype(f32) + v.ac[...].astype(f32)).astype(bf16)
        squeeze(d, v.dmo)

        copies = around(lambda k: v.dmo, v.dms, v.dmo[...])
        finish(copies)
        spread_all(v.dms)
        gathered_d = v.stage[...].reshape(4 * KP, 2048)
        for s in range(4):
            block = nt(gathered_d, v.wm[s]).astype(bf16)
            v.fcs[:, :, s * 256 : (s + 1) * 256] = block.reshape(4, KP, 256)
        copies = around(lambda k: v.fcs.at[turn(k)], v.dsr, v.fcs[z])
        outward = to_owners(v.pos, v.por)
        finish(copies)

        ds = []
        hs = []
        for b in range(8):
            ds.append(v.dsr[b % 4, :, (b // 4) * 512 : (b // 4 + 1) * 512])
            hs.append(v.fc[:, b * 512 : (b + 1) * 512])
        for b, d in enumerate(norm_back_split(ds, hs, v.sfc[...])):
            k = b // 2
            v.dfc[k * KP : (k + 1) * KP, (b % 2) * 512 : (b % 2 + 1) * 512] = d.astype(bf16)
        sent(shift_foldc)
        pack("foldc_b", v.dfc[...], got.foldc_halo_t)
        copies = shift("foldc_b")
        foldc_own_t, foldc_pack_t = got.foldc_own_t, got.foldc_pack_t
        finish(shift_gm)
        adjoint_mid = placed(slice(None), v.gm, "gm", got.mid_own, got.mid_halo).astype(bf16).astype(f32)
        finish(copies)
        d = placed(slice(None), v.dfc, "foldc_b", foldc_own_t, foldc_pack_t)
        v.ym[...] = (adjoint_mid + d.astype(bf16).astype(f32)).astype(bf16)

        def dmix_mid(part, cols):
            v.mixm[part, cols] = nt(v.ym[part, :], out_m[cols, :]).astype(bf16)

        tiles(160, 160, 1024, 256, dmix_mid)
        attend_back(v.trm, v.trrm, v.psm, v.mixm, 8, 2, WP, 8)

        def to_wide(left, weight, blocks):
            @pl.loop(0, 2 * blocks, unroll=4)
            def _(j):
                v.wide[aligned(lax.div(j, 2) * 160, 160, 16), aligned(lax.rem(j, 2) * 256, 256, 128)] = nt(
                    left[...], weight[aligned(j * 256, 256, 128), :]
                )

        def wide_back(blocks, h, scale):
            ds = [v.wide[k * 160 : (k + 1) * 160, :] for k in range(blocks)]
            hs = [h[:, k * 512 : (k + 1) * 512] for k in range(blocks)]
            return [d.astype(bf16) for d in norm_back_split(ds, hs, scale[...])]

        to_wide(v.trm, qkv_m, 2)
        for k, d in enumerate(wide_back(2, v.hm, v.sm)):
            cols = slice(k * 512, (k + 1) * 512)
            v.xm[:, cols] = (d.astype(f32) + v.ym[:, cols].astype(f32)).astype(bf16)

        to_wide(v.xm, mrg_f, 4)
        for k, d in enumerate(wide_back(4, v.ff, v.sff)):
            v.mixf[k * 160 : (k + 1) * 160, :] = d
        sent(shift_fold)
        pack("fold_b", v.mixf[...], got.fold_halo_t)
        copies = shift("fold_b")

        from_members(outward)
        total = total_of(v.por)
        pack("coarse_b", (v.xc[...].astype(f32) + total).astype(bf16), got.coarse_halo_t)
        shift_out = shift("coarse_b")

        fold_pack_t = got.fold_pack_t
        finish(copies)

        @pl.loop(0, 5, unroll=5)
        def _(i):
            part = aligned(i * 128, 128, 128)
            d = tn(fold_own[:, part], v.mixf[...]) + nn(fold_pack_t[part, :], recv_buf["fold_b"][...])
            v.yf[part, :] = (v.yf[part, :].astype(f32) + d.astype(bf16).astype(f32)).astype(bf16)

        def dmix_fine(part, cols):
            v.mixf[part, cols] = nt(v.yf[part, :], out_f[cols, :]).astype(bf16)

        tiles(640, 320, 512, 256, dmix_fine)
        attend_back(v.trf, v.trrf, v.psf, v.mixf, 4, 8, WP, 8)

        def dh_fine(part, cols):
            v.wide[part, cols] = nt(v.trf[part, :], qkv_f[cols, :])

        tiles(640, 320, 512, 256, dh_fine)

        @pl.loop(0, 4, unroll=2)
        def _(i):
            part = aligned(i * 160, 160, 16)
            d = norm_back(v.wide[part, :], v.hf[part, :], v.sf[part, :])
            v.xf[part, :] = (d.astype(bf16).astype(f32) + v.yf[part, :].astype(f32)).astype(bf16)

        pack("fine_b", v.xf[...], got.fine_halo_t)
        copies = shift("fine_b")
        fine_pack_t = got.fine_pack_t
        finish(shift_out)
        out = nn(got.coarse_pack_t[...], recv_buf["coarse_b"][...]).astype(bf16)
        for r in range(6):
            coarse_ref[r] = out[16 * r : 16 * r + 6]
        writes = []
        fine_own_t = got.fine_own_t
        for j in range(4):
            here = (j * 160, min(j * 160 + 320, 640))
            v.wide[pl.ds(j * 144, 144), :] = nn(fine_own_t[:, : here[1] - here[0]], v.xf[here[0] : here[1], :])
        finish(copies)
        for j in range(4):
            part = pl.ds(j * 144, 144)
            d = v.wide[part, :] + nn(fine_pack_t[part, :], recv_buf["fine_b"][...])
            tokens[part, :] = d.astype(bf16)
            writes.append(pltpu.make_async_copy(tokens.at[part], grad_ref.at[part], local_sem.at[len(ALL_LOADED) + 3 + j]))
            writes[-1].start()
        for write in writes:
            write.wait()
        for copy in pending:
            copy.wait_send()
        for name in ALL_LOADED:
            getattr(got, name)

    any_space = pl.BlockSpec(memory_space=pl.ANY)
    whole = pl.BlockSpec(memory_space=pltpu.VMEM)
    return pl.pallas_call(
        kernel,
        out_shape=(jax.ShapeDtypeStruct((576, 512), bf16), jax.ShapeDtypeStruct((6, 6, 2048), bf16)),
        in_specs=[any_space] * len(shapes),
        out_specs=(any_space, whole),
        scratch_shapes=[pltpu.VMEM(*shape) for group in (scratch, loaded, sends, receives) for shape in group.values()]
        + [pltpu.SemaphoreType.DMA((N_LOCAL,)), pltpu.SemaphoreType.DMA((N_REMOTE,)), pltpu.SemaphoreType.DMA((N_REMOTE,))],
        compiler_params=pltpu.CompilerParams(
            collective_id=0, has_side_effects=True, vmem_limit_bytes=66_584_576
        ),
    )


def shards(
    tokens, qkv_fine, out_fine, merge_fine, qkv_mid, out_mid, merge_mid, qkv_coarse, out_coarse, grad_fine, grad_mid, grad_coarse
):
    values = dict(
        tokens=tokens.reshape(576, 512),
        qkv_f=qkv_fine,
        out_f=out_fine,
        mrg_f=merge_fine,
        qkv_m=qkv_mid,
        out_m=out_mid,
        wm=merge_mid,
        wq=qkv_coarse,
        wo=out_coarse,
        g_fine=grad_fine.reshape(576, 512),
        g_mid=grad_mid,
        g_coarse=grad_coarse,
        bias=jnp.asarray(BIAS),
        biasc=jnp.asarray(BIASC),
    )
    for name, matrix in CONSTANTS.items():
        values[name] = jnp.asarray(matrix, bf16)
    shapes = {name: (value.shape, value.dtype) for name, value in values.items()}
    gradient, coarse = build(shapes)(*values.values())
    return gradient.reshape(24, 24, 512), coarse


def solution(mesh):
    placed = (
        P("lat", "lon", None),
        P(),
        P(),
        P(),
        P(),
        P(),
        P("lon", None),
        P(None, "lon"),
        P("lon", None),
        P("lat", "lon", None),
        P("lat", "lon", None),
        P("lat", "lon", None),
    )
    return jax.shard_map(
        shards,
        mesh=mesh,
        in_specs=placed,
        out_specs=(P("lat", "lon", None), P("lat", "lon", None)),
        check_vma=False,
    )
```

```python
from types import SimpleNamespace

import jax
import jax.numpy as jnp
import numpy as np
from jax import lax
from jax.experimental import pallas as pl
from jax.experimental.pallas import tpu as pltpu
from jax.sharding import PartitionSpec as P

HD = 64
WH = 6
WW = 12
WP = 80
KP = 48
EPS = 1e-05
LAT = 8
LON = 16
bf16 = jnp.bfloat16
f32 = jnp.float32
MESH = pl.DeviceIdType.MESH


def window_order(cols):
    across = cols // WW

    def index(r, c):
        return ((r // WH) * across + c // WW) * WP + (r % WH) * WW + c % WW

    return index


def raster(stride):
    return lambda r, c: r * stride + c


def fold_order(inner, stride):
    def index(r, c):
        return ((c % 2) * 2 + r % 2) * stride + inner(r // 2, c // 2)

    return index


def shift_maps(size, src, n_src, dst, n_dst):
    dr, dc = WH // 2, WW // 2
    up = -(-(size - dr) * dc // 32) * 32
    down = -(-max(dr * (size - dc), 0) // 32) * 32
    corner = 32
    parts = [(0, up, 0, 1), (up, down, 1, 0), (up + down, corner, 1, 1)]
    total = up + down + corner
    own = np.zeros((n_dst, n_src), np.float32)
    halo = np.zeros((n_dst, total), np.float32)
    pack = np.zeros((total, n_src), np.float32)
    for r in range(size):
        for c in range(size):
            to = dst(r, c)
            if r >= dr and c >= dc:
                own[to, src(r - dr, c - dc)] = 1
                continue
            if r >= dr:
                slot = (r - dr) * dc + c
            elif c >= dc:
                slot = up + r * (size - dc) + c - dc
            else:
                slot = up + down + r * dc + c
            halo[to, slot] = 1
            pack[slot, src((r - dr) % size, (c - dc) % size)] = 1
    return own, halo, pack, [part for part in parts if part[1]]


def window_bias(stride, rows, groups):
    token = np.arange(rows)
    real = token % stride < groups * 2
    upper = token % stride < groups
    allowed = np.broadcast_to(real[None, :], (rows, rows))
    split = allowed & (upper[:, None] == upper[None, :])
    both = np.stack([allowed, split])
    both = np.concatenate([both, both], 1)
    return np.where(both, 0.0, -1e30).astype(np.float32)


FINE = shift_maps(24, raster(24), 576, window_order(24), 640)
FOLD = shift_maps(24, window_order(24), 640, fold_order(window_order(12), 160), 640)
MID = shift_maps(12, raster(16), 192, window_order(12), 160)
FOLDC = shift_maps(12, window_order(12), 160, fold_order(raster(6), KP), 4 * KP)
COARSE = shift_maps(6, raster(16), 96, raster(6), KP)
BIAS = window_bias(WP, WP, 36)
BIASC = window_bias(KP, 2 * KP, 18)

SQUEEZE = np.zeros((144, 4 * KP), np.float32)
for k in range(4):
    SQUEEZE[k * 36 : (k + 1) * 36, k * KP : k * KP + 36] = np.eye(36)
TOP = 80
FINE_BAND = np.ascontiguousarray(FINE[0][160:320, 144 - TOP : 304 - TOP])
FINE_BAND_BACK = np.ascontiguousarray(FINE[0][160:480, 144:288].T)
CONSTANTS = dict(
    fine_own=FINE_BAND, fine_halo=FINE[1], fine_pack=FINE[2],
    fine_own_t=FINE_BAND_BACK, fine_halo_t=FINE[1].T, fine_pack_t=FINE[2].T,
    fold_own=FOLD[0], fold_halo=FOLD[1], fold_pack=FOLD[2], fold_halo_t=FOLD[1].T, fold_pack_t=FOLD[2].T,
    mid_own=MID[0], mid_halo=MID[1], mid_pack=MID[2],
    foldc_own=FOLDC[0], foldc_halo=FOLDC[1], foldc_pack=FOLDC[2],
    foldc_own_t=FOLDC[0].T, foldc_halo_t=FOLDC[1].T, foldc_pack_t=FOLDC[2].T,
    squeeze=SQUEEZE, squeeze_t=SQUEEZE.T,
    coarse_halo=COARSE[1], coarse_pack=COARSE[2], coarse_halo_t=COARSE[1].T, coarse_pack_t=COARSE[2].T,
)

LOADED = (
    tuple(dict(tokens=1, fine_pack=1, fine_own=1, fine_halo=1)),
    tuple(dict(
        qkv_f=1, g_coarse=1, coarse_pack=1, g_mid=1, mid_pack=1, g_fine=1, bias=1, out_f=1, fold_pack=1, fold_own=1, fold_halo=1,
    )),
    tuple(dict(
        mrg_f=1, coarse_halo=1, squeeze=1, squeeze_t=1, qkv_m=1, out_m=1, foldc_pack=1, foldc_own=1, foldc_halo=1, biasc=1,
        mid_own=1, mid_halo=1, foldc_halo_t=1, foldc_own_t=1, foldc_pack_t=1, fold_halo_t=1, fold_pack_t=1,
        fine_halo_t=1, fine_own_t=1, fine_pack_t=1, coarse_halo_t=1, coarse_pack_t=1,
    )),
)
ALL_LOADED = [name for group in LOADED for name in group]


def nn(a, b):
    return jnp.dot(a, b, preferred_element_type=f32)


def nt(a, b):
    return lax.dot_general(a, b, (((1,), (1,)), ((), ())), preferred_element_type=f32)


def tn(a, b):
    return lax.dot_general(a, b, (((0,), (0,)), ((), ())), preferred_element_type=f32)


def norm_rows(x):
    centred = x - jnp.mean(x, axis=-1, keepdims=True)
    scale = lax.rsqrt(jnp.mean(centred * centred, axis=-1, keepdims=True) + EPS)
    return centred * scale, scale


def norm_back(d, h, scale):
    d = d.astype(bf16).astype(f32)
    h = h.astype(f32)
    return scale * (d - jnp.mean(d, axis=-1, keepdims=True) - h * jnp.mean(d * h, axis=-1, keepdims=True))


def norm_split(parts):
    size = sum(p.shape[-1] for p in parts)
    average = sum(jnp.sum(p, axis=-1, keepdims=True) for p in parts) / size
    parts = [p - average for p in parts]
    scale = lax.rsqrt(sum(jnp.sum(p * p, axis=-1, keepdims=True) for p in parts) / size + EPS)
    return [p * scale for p in parts], scale


def norm_back_split(ds, hs, scale):
    size = sum(d.shape[-1] for d in ds)
    ds = [d.astype(bf16).astype(f32) for d in ds]
    hs = [h.astype(f32) for h in hs]
    mean_d = sum(jnp.sum(d, axis=-1, keepdims=True) for d in ds) / size
    mean_dh = sum(jnp.sum(d * h, axis=-1, keepdims=True) for d, h in zip(ds, hs)) / size
    return [scale * (d - mean_d - h * mean_dh) for d, h in zip(ds, hs)]


def aligned(start, size, multiple):
    return pl.ds(pl.multiple_of(start, multiple), size)


def project_qkv(h, weight, tr, trr, rows, pairs, step):
    @pl.loop(0, rows // step)
    def _(i):
        part = aligned(i * step, step, 16)

        @pl.loop(0, pairs, unroll=2)
        def _(p):
            wide = nn(h[part, :], weight(p))
            tr[part, aligned(p * 384, 384, 128)] = wide.astype(bf16)
            ra, rb, rc = (pltpu.roll(wide[:, k * 128 : (k + 1) * 128], 64, 1) for k in range(3))
            low = lax.broadcasted_iota(jnp.int32, (1, 128), 1) < 64
            trr[part, aligned(p * 256, 128, 128)] = jnp.where(low, ra, rc).astype(bf16)
            trr[part, aligned(p * 256 + 128, 128, 128)] = jnp.where(low, rb, ra).astype(bf16)


def halves():
    lane = lax.broadcasted_iota(jnp.int32, (1, 128), 1)
    low = lane < 64
    one = jnp.where(low, 1.0, 0.0)
    return low, one.astype(bf16), (1.0 - one).astype(bf16)


def attend(tr, trr, ps, mix, bias, pairs, windows, wp, split, unroll, part=0, parts=1):
    steps = pairs * windows // unroll // parts

    @pl.loop(part * steps, (part + 1) * steps)
    def _(step):
        low, mlo, mhi = halves()
        stores = []
        for u in range(unroll):
            item = step * unroll + u
            w, p = lax.div(item, pairs), lax.rem(item, pairs)
            part = aligned(w * wp, wp, 16)
            a, b, c = (tr[part, aligned(p * 384 + k * 128, 128, 128)] for k in range(3))
            k2 = trr[part, aligned(p * 256, 128, 128)]
            eighth = jnp.asarray(HD**-0.5, bf16)
            q2 = jnp.concatenate([a * (mlo * eighth), b * (mhi * eighth)], 0)
            scores = nt(q2, k2) + bias[split(w)]
            e = jnp.exp(scores - jnp.max(scores, axis=-1, keepdims=True))
            weights = (e / jnp.sum(e, axis=-1, keepdims=True)).astype(bf16)
            mixed = jnp.where(low, nn(weights[:wp], b), nn(weights[wp:], c))
            stores.append((item, weights, (part, aligned(p * 128, 128, 128)), mixed.astype(bf16)))
        for item, weights, place, mixed in stores:
            ps[item] = weights
            mix[place] = mixed


def attend_back(tr, trr, ps, dmix, pairs, windows, wp, unroll):
    @pl.loop(0, pairs * windows // unroll)
    def _(step):
        low, mlo, mhi = halves()
        stores = []
        for u in range(unroll):
            item = step * unroll + u
            w, p = lax.div(item, pairs), lax.rem(item, pairs)
            part = aligned(w * wp, wp, 16)
            places = [(part, aligned(p * 384 + k * 128, 128, 128)) for k in range(3)]
            b, c = tr[places[1]], tr[places[2]]
            k2, q2 = (trr[part, aligned(p * 256 + k * 128, 128, 128)] for k in range(2))
            do = dmix[part, aligned(p * 128, 128, 128)]
            weights = ps[item]
            outs = []
            for half, mask, values in ((0, mlo, b), (1, mhi, c)):
                wt = weights[half * wp : (half + 1) * wp]
                wide = wt.astype(f32)
                dw = nt(do * mask, values)
                ds = wide * (dw - jnp.sum(wide * dw, axis=-1, keepdims=True)) * HD**-0.5
                outs.append((wt, ds.astype(bf16)))
            (w0, ds0), (w1, ds1) = outs
            stores.append((places[0], jnp.where(low, nn(ds0, k2), tn(ds0, q2)).astype(bf16)))
            stores.append((places[1], jnp.where(low, tn(w0, do), nn(ds1, k2)).astype(bf16)))
            stores.append((places[2], jnp.where(low, tn(ds1, q2), tn(w1, do)).astype(bf16)))
        for place, value in stores:
            tr[place] = value


def tiles(rows, step, cols, width, body):
    @pl.loop(0, rows // step)
    def _(i):
        part = aligned(i * step, step, 16)

        @pl.loop(0, cols // width, unroll=min(4, cols // width))
        def _(j):
            body(part, aligned(j * width, width, 128))


VMEM_SCRATCH = dict(
    xf=((640, 512), bf16), hf=((640, 512), bf16), sf=((640, 1), f32), trf=((640, 1536), bf16),
    trrf=((640, 1024), bf16), psf=((32, 2 * WP, WP), bf16), mixf=((640, 512), bf16), yf=((640, 512), bf16),
    wide=((640, 512), f32),
    ff=((160, 2048), bf16), sff=((160, 1), f32),
    xm=((160, 1024), bf16), hm=((160, 1024), bf16), sm=((160, 1), f32), trm=((160, 3072), bf16),
    trrm=((160, 2048), bf16), psm=((16, 2 * WP, WP), bf16), mixm=((160, 1024), bf16), ym=((160, 1024), bf16),
    fc=((KP, 4096), bf16), sfc=((KP, 1), f32), fcs=((4, KP, 1024), bf16), fcr=((4, KP, 1024), bf16),
    pms=((4, 144, 512), bf16), pmr=((4, 144, 512), bf16), dmo=((144, 512), bf16), dms=((4, 144, 512), bf16), stage=((4, KP, 2048), bf16),
    dsr=((4, KP, 1024), bf16), dfc=((4 * KP, 1024), bf16),
    gm=((192, 1024), bf16),
    xc=((KP, 2048), bf16), hc=((KP, 2048), bf16), sc=((KP, 1), f32), hcs=((144, 512), bf16), hcr=((4, 144, 512), bf16),
    ac=((KP, 2048), bf16), acs=((144, 512), bf16), acr=((4, 144, 512), bf16),
    trc=((4 * KP, 1536), bf16), trrc=((4 * KP, 1024), bf16), psc=((8, 4 * KP, 2 * KP), bf16),
    mixc=((4 * KP, 512), bf16), dmixc=((4 * KP, 512), bf16),
    dhs=((4, 144, 512), bf16), dhr=((4, 144, 512), bf16), pos=((4, 144, 512), bf16), por=((4, 144, 512), bf16),
    wm=((4, 256, 2048), bf16), wq=((4, 2048, 384), bf16), wo=((4, 128, 2048), bf16),
)
EXCHANGES = dict(
    tok=(FINE, 512, 1), gf=(FINE, 512, 1), gm=(MID, 1024, 1), gc=(COARSE, 2048, 1), fold=(FOLD, 512, 1), foldc=(FOLDC, 1024, 1),
    foldc_b=(FOLDC, 1024, -1), fold_b=(FOLD, 512, -1), fine_b=(FINE, 512, -1), coarse_b=(COARSE, 2048, -1),
)
SENT_FROM = dict(fold="tok", fold_b="tok", fine_b="tok", foldc_b="foldc", coarse_b="gc")
N_LOCAL = len(ALL_LOADED) + 7
N_REMOTE = 96


class Lazy:
    def __init__(self, make):
        self.make = make

    def __getattr__(self, name):
        value = self.make(name)
        setattr(self, name, value)
        return value


def build(shapes):
    scratch = dict(VMEM_SCRATCH)
    loaded = {name: shapes[name] for name in ALL_LOADED}
    for name in ("tokens", "g_fine"):
        loaded[name] = ((TOP + 576, 512), bf16)
    sends, receives = {}, {}
    for name, (maps, width, _) in EXCHANGES.items():
        receives[name] = ((maps[1].shape[1], width), bf16)
        if name not in SENT_FROM:
            sends[name] = receives[name]

    def kernel(*refs):
        refs = list(refs)

        def take(names):
            return {name: refs.pop(0) for name in names}

        hbm = take(shapes)
        grad_ref, coarse_ref = refs.pop(0), refs.pop(0)
        v = SimpleNamespace(**take(scratch))
        vm, send_buf, recv_buf = take(loaded), take(sends), take(receives)
        local_sem, send_sem, recv_sem = refs

        lat, lon = lax.axis_index("lat"), lax.axis_index("lon")
        y, z, core = lax.div(lon, 8), lax.rem(lax.div(lon, 2), 4), lax.rem(lon, 2)

        def near(dlat, dlon):
            return (lax.rem(lat + dlat + LAT, LAT), lax.rem(lon + dlon + LON, LON))

        def at(yy, zz, cc):
            return (lat, yy * 8 + zz * 2 + cc)

        def turn(k):
            return lax.rem(z + k, 4)

        loads = {}
        for i, name in enumerate(ALL_LOADED):
            dest = vm[name].at[pl.ds(TOP, 576)] if name in ("tokens", "g_fine") else vm[name]
            loads[name] = pltpu.make_async_copy(hbm[name], dest, local_sem.at[i])

        def start_loads(group):
            for name in group:
                loads[name].start()

        start_loads(LOADED[0])

        def wait_load(name):
            loads[name].wait()
            return vm[name]

        got = Lazy(wait_load)

        own_slot = y * 2 + core
        own_loads = []
        for i, name in enumerate(("wm", "wq", "wo")):
            copy = pltpu.make_async_copy(hbm[name], getattr(v, name).at[own_slot], local_sem.at[len(ALL_LOADED) + i])
            own_loads.append(copy)

        barrier = pltpu.get_barrier_semaphore()
        others = [near(1, 0), near(-1, 0), near(1, 1), near(-1, -1)]
        others += [(lat + 1 - 2 * lax.rem(lat, 2), lax.rem(lon + 8, LON))]
        others += [(lat, y * 8 + lax.rem(lax.rem(lon, 8) + k, 8)) for k in range(1, 8)]
        for device in others:
            pl.semaphore_signal(barrier, inc=1, device_id=device, device_id_type=MESH)
        place = lax.rem(lon, 8)

        @pl.when(place == 7)
        def _():
            pl.semaphore_signal(barrier, inc=1, device_id=near(0, 1), device_id_type=MESH)

        @pl.when(place == 0)
        def _():
            pl.semaphore_signal(barrier, inc=1, device_id=near(0, -1), device_id_type=MESH)

        edge = jnp.where((place == 7) | (place == 0), 1, 0)

        counter = [0]

        def sems(n):
            counter[0] += n
            assert counter[0] <= N_REMOTE
            return counter[0] - n

        def remote(src, dst, send, recv, device):
            return pltpu.make_async_remote_copy(
                src_ref=src, dst_ref=dst, send_sem=send_sem.at[send], recv_sem=recv_sem.at[recv],
                device_id=device, device_id_type=MESH,
            )

        pending = []

        def sender(name):
            return send_buf[SENT_FROM.get(name, name)]

        def finish(copies):
            for copy in copies:
                copy.wait()

        def sent(copies):
            for copy in copies:
                copy.wait_send()

        def shift(name):
            maps, _, sign = EXCHANGES[name]
            base = sems(3)
            copies = []
            for k, (start, size, dlat, dlon) in enumerate(maps[3]):
                part = pl.ds(start, size)
                copies.append(
                    remote(sender(name).at[part], recv_buf[name].at[part], base + k, base + k, near(sign * dlat, sign * dlon))
                )
            for copy in copies:
                copy.start()
            return copies

        def received(copies):
            for copy in copies:
                copy.wait_recv()

        sibling = at(y, z, 1 - core)
        partner_slot = (1 - y) * 2 + core
        y_low = lax.rem(lat, 2)
        beside = lat + 1 - 2 * y_low

        def weight_piece(name, start, size):
            base = sems(2)
            dest = getattr(v, name)
            half = hbm[name].shape[0] // 2
            mine = aligned(y_low * half + start, size, 16)
            other = aligned((1 - y_low) * half + start, size, 16)
            there = dest.at[partner_slot, other]
            return (
                remote(hbm[name].at[mine], dest.at[own_slot, mine], base, base, (beside, lax.rem(lon + 8, LON))),
                remote(there, there, base + 1, base + 1, (beside, lon)),
            )

        def core_copies(name):
            base = sems(2)
            dest = getattr(v, name)
            there = dest.at[partner_slot]
            return (
                remote(hbm[name], dest.at[own_slot], base, base, sibling),
                remote(there, there, base + 1, base + 1, sibling),
            )

        pieces = dict(
            wm=[weight_piece("wm", 0, 128)],
            wq=[weight_piece("wq", 0, 640), weight_piece("wq", 640, 384)],
            wo=[weight_piece("wo", 0, 64)],
        )
        between_cores = {name: core_copies(name) for name in pieces}

        def cross_weights(name, i):
            pieces[name][i][0].start()

        def relay_weights(name, i):
            pieces[name][i][0].wait_recv()
            pieces[name][i][1].start()

        def pass_weights(name):
            for piece in pieces[name]:
                piece[1].wait_recv()
            between_cores[name][1].start()

        def weights_ready(name):
            for copy in between_cores[name]:
                copy.wait_recv()
                pending.append(copy)
            for piece in pieces[name]:
                pending.extend(piece)

        def pack(name, source, matrix):
            sender(name)[...] = nn(matrix[...], source).astype(bf16)

        tokens = got.tokens
        pack("tok", tokens[TOP:, :], got.fine_pack)
        pl.semaphore_wait(barrier, len(others) + edge)
        shift_tok = shift("tok")
        start_loads(LOADED[1])
        tokens[0:TOP, :] = jnp.zeros((TOP, 512), bf16)
        vm["g_fine"][0:TOP, :] = jnp.zeros((TOP, 512), bf16)
        v.gm[...] = jnp.zeros_like(v.gm)
        fine_own, fine_halo, qkv_f = got.fine_own, got.fine_halo, got.qkv_f

        def placed(part, source, name, own, halo):
            return nn(own[part, :], source[...]) + nn(halo[part, :], recv_buf[name][...])

        def placed_fine(i, source, name):
            return nn(fine_own[...], source[aligned(i * 144, 160, 16), :]) + nn(
                fine_halo[aligned(i * 160, 160, 16), :], recv_buf[name][...]
            )

        received(shift_tok)
        cross_weights("wm", 0)

        @pl.loop(0, 4, unroll=2)
        def _(i):
            part = aligned(i * 160, 160, 16)
            x = placed_fine(i, tokens, "tok")
            v.xf[part, :] = x.astype(bf16)
            h, scale = norm_rows(x)
            v.hf[part, :] = h.astype(bf16)
            v.sf[part, :] = scale

        for r in range(6):
            for k in range(2):
                v.gm[96 * k + 16 * r : 96 * k + 16 * r + 6, :] = got.g_coarse[r, :, k * 1024 : (k + 1) * 1024]
        for k in range(2):
            packed = nn(got.coarse_pack[...], v.gm[96 * k : 96 * (k + 1), :])
            sender("gc")[:, k * 1024 : (k + 1) * 1024] = packed.astype(bf16)
        shift_gc = shift("gc")
        start_loads(LOADED[2])
        for copy in own_loads:
            copy.start()
        for name in pieces:
            between_cores[name][0].start()
        project_qkv(v.hf, lambda p: qkv_f[:, aligned(p * 384, 384, 128)], v.trf, v.trrf, 640, 4, 320)
        first = lat == 0
        bias, out_f = got.bias, got.out_f
        attend(v.trf, v.trrf, v.psf, v.mixf, bias, 4, 8, WP, lambda w: jnp.where(first & (w < 2), 1, 0), 8)

        def out_fine(part, cols):
            v.yf[part, cols] = (nn(v.mixf[part, :], out_f[:, cols]) + v.xf[part, cols].astype(f32)).astype(bf16)

        tiles(640, 320, 512, 256, out_fine)

        sent(shift_tok)
        pack("fold", v.yf[...], got.fold_pack)
        shift_fold = shift("fold")
        fold_own, fold_halo, mrg_f = got.fold_own, got.fold_halo, got.mrg_f
        slot = lax.rem(z, 2) * 2 + core
        wide_group = lax.div(z, 2)

        def squeeze(x, dest):
            stacked = jnp.concatenate([x[:, k * 512 : (k + 1) * 512] for k in range(4)], 0)
            dest[...] = nn(got.squeeze[...], stacked).astype(bf16)

        def spread(packed):
            stacked = nn(got.squeeze_t[...], packed.astype(bf16))
            return [stacked[k * KP : (k + 1) * KP] for k in range(4)]

        def spread_all(packed):
            for s in range(4):
                for k, part in enumerate(spread(packed[s])):
                    v.stage[s, :, k * 512 : (k + 1) * 512] = part.astype(bf16)

        def total_of(packed):
            return jnp.concatenate(spread(sum(packed[k].astype(f32) for k in range(4))), 1)

        def to_group(source, dest):
            send, recv = sems(4), sems(4)
            for k in range(1, 4):
                copy = remote(source, dest.at[slot], send + k, recv + slot, at(y, turn(k), wide_group))
                copy.start()
                pending.append(copy)
            across = remote(source, dest.at[slot], send, recv + slot, sibling)

            @pl.when(core == wide_group)
            def _():
                dest[slot] = source[...]

            @pl.when(core != wide_group)
            def _():
                across.start()

            return source, dest, send, recv, across

        def is_own(s):
            return (z == core * 2 + s // 2) & (core == s % 2)

        def from_group(handle):
            source, dest, send, recv, across = handle

            @pl.when(core != wide_group)
            def _():
                across.wait_send()

            for s in range(4):

                @pl.when(jnp.logical_not(is_own(s)))
                def _(s=s):
                    remote(source, dest.at[s], send, recv + s, sibling).wait_recv()

        def to_owners(source, dest, prepare):
            send, recv = sems(4), sems(4)
            for s in range(4):
                prepare(s)
                copy = remote(source.at[s], dest.at[z], send + s, recv + z, at(y, core * 2 + s // 2, s % 2))

                @pl.when(is_own(s))
                def _(s=s):
                    dest[z] = source[s]

                @pl.when(jnp.logical_not(is_own(s)))
                def _(copy=copy):
                    copy.start()

            return source, dest, send, recv

        def from_members(handle):
            source, dest, send, recv = handle
            for k in range(4):

                @pl.when(jnp.logical_not((z == k) & (core == wide_group)))
                def _(k=k):
                    remote(source.at[0], dest.at[k], send, recv + k, sibling).wait_recv()

            for s in range(4):

                @pl.when(jnp.logical_not(is_own(s)))
                def _(s=s):
                    remote(source.at[s], dest.at[0], send + s, recv, sibling).wait_send()

        def around(pick, dest, own):
            base = sems(4)
            copies = []
            for k in range(1, 4):
                copy = remote(pick(k), dest.at[z], base + k, base + k, at(y, turn(k), core))
                copy.start()
                copies.append(copy)
            dest[z] = own()
            return copies

        for r in range(12):
            v.gm[16 * r : 16 * r + 12, :] = got.g_mid[r]
        pack("gm", v.gm[...], got.mid_pack)
        shift_gm = shift("gm")
        pack("gf", got.g_fine[TOP:, :], got.fine_pack)
        shift_gf = shift("gf")

        finish(shift_gc)
        v.ac[...] = nn(got.coarse_halo[...], recv_buf["gc"][...]).astype(bf16)
        squeeze(v.ac[...], v.acs)
        received(shift_fold)
        adjoint = to_group(v.acs, v.acr)
        relay_weights("wm", 0)
        cross_weights("wq", 0)

        quads = [placed(slice(k * 160, (k + 1) * 160), v.yf, "fold", fold_own, fold_halo) for k in range(4)]
        normed, scale = norm_split(quads)
        for k in range(4):
            v.ff[:, k * 512 : (k + 1) * 512] = normed[k].astype(bf16)
        v.sff[...] = scale
        def merge_fine(part, cols):
            v.xm[part, cols] = nn(v.ff[part, :], mrg_f[:, cols]).astype(bf16)

        tiles(160, 160, 1024, 256, merge_fine)

        qkv_m, out_m = got.qkv_m, got.out_m
        h, scale = norm_rows(v.xm[...].astype(f32))
        v.hm[...] = h.astype(bf16)
        v.sm[...] = scale
        project_qkv(v.hm, lambda p: qkv_m[:, aligned(p * 384, 384, 128)], v.trm, v.trrm, 160, 8, 160)
        attend(v.trm, v.trrm, v.psm, v.mixm, bias, 8, 2, WP, lambda w: jnp.where(first & (w < 1), 1, 0), 8)

        def out_mid(part, cols):
            v.ym[part, cols] = (nn(v.mixm[part, :], out_m[:, cols]) + v.xm[part, cols].astype(f32)).astype(bf16)

        tiles(160, 160, 1024, 256, out_mid)

        pack("foldc", v.ym[...], got.foldc_pack)
        shift_foldc = shift("foldc")
        foldc_own, foldc_halo = got.foldc_own, got.foldc_halo
        received(shift_foldc)
        relay_weights("wq", 0)
        cross_weights("wq", 1)
        cross_weights("wo", 0)
        pass_weights("wm")
        folded = placed(slice(None), v.ym, "foldc", foldc_own, foldc_halo)
        quads = [folded[k * KP : (k + 1) * KP] for k in range(4)]
        normed, scale = norm_split(quads)
        v.sfc[...] = scale
        for k in range(4):
            h = normed[k].astype(bf16)
            v.fc[:, k * 1024 : (k + 1) * 1024] = h
            for j in range(2):
                block = 2 * k + j
                v.fcs[block % 4, :, (block // 4) * 512 : (block // 4 + 1) * 512] = h[:, j * 512 : (j + 1) * 512]
        copies = around(lambda k: v.fcs.at[turn(k)], v.fcr, lambda: v.fcs[z])
        finish(copies)
        for copy in own_loads:
            copy.wait()
        weights_ready("wm")
        gathered = v.fcr[...].reshape(4 * KP, 1024)

        @pl.loop(0, 8, unroll=4)
        def _(j):
            cols = aligned(j * 256, 256, 128)
            total = nn(gathered[:, 0:256], v.wm[0, :, cols])
            for s in range(1, 4):
                total += nn(gathered[:, s * 256 : (s + 1) * 256], v.wm[s, :, cols])
            v.stage[:, :, cols] = total.astype(bf16).reshape(4, KP, 256)

        def merged_block(k):
            block = v.pms.at[turn(k)]
            squeeze(v.stage[turn(k)], block)
            return block

        copies = around(merged_block, v.pmr, lambda: merged_block(0)[...])
        relay_weights("wq", 1)
        relay_weights("wo", 0)
        finish(shift_gf)

        @pl.loop(0, 4, unroll=2)
        def _(i):
            part = aligned(i * 160, 160, 16)
            v.yf[part, :] = placed_fine(i, got.g_fine, "gf").astype(bf16)

        finish(copies)
        x = total_of(v.pmr).astype(bf16)
        v.xc[...] = x
        h, scale = norm_rows(x.astype(f32))
        v.hc[...] = h.astype(bf16)
        v.sc[...] = scale

        squeeze(v.hc[...], v.hcs)
        forward = to_group(v.hcs, v.hcr)
        pass_weights("wq")
        pass_weights("wo")
        biasc = got.biasc
        from_group(adjoint)
        spread_all(v.acr)
        weights_ready("wo")
        for p in range(4):
            v.dmixc[:, p * 128 : (p + 1) * 128] = nt(v.stage[...].reshape(4 * KP, 2048), v.wo[p]).astype(bf16)
        weights_ready("wq")
        from_group(forward)
        spread_all(v.hcr)
        project_qkv(v.stage.reshape(4 * KP, 2048), lambda p: v.wq[p], v.trc, v.trrc, 4 * KP, 4, 4 * KP)
        attend(v.trc, v.trrc, v.psc, v.mixc, biasc, 4, 2, 2 * KP, lambda w: jnp.where(first, 1, 0), 8)
        attend_back(v.trc, v.trrc, v.psc, v.dmixc, 4, 2, 2 * KP, 8)

        @pl.loop(0, 8, unroll=4)
        def _(j):
            rows = aligned(j * 256, 256, 128)
            total = nt(v.trc[:, 0:384], v.wq[0, rows, :])
            for s in range(1, 4):
                total += nt(v.trc[:, s * 384 : (s + 1) * 384], v.wq[s, rows, :])
            v.stage[:, :, rows] = total.astype(bf16).reshape(4, KP, 256)

        backward = to_owners(v.dhs, v.dhr, lambda s: squeeze(v.stage[s], v.dhs.at[s]))

        @pl.loop(0, 8, unroll=4)
        def _(j):
            cols = aligned(j * 256, 256, 128)
            total = nn(v.mixc[:, 0:128], v.wo[0, :, cols])
            for s in range(1, 4):
                total += nn(v.mixc[:, s * 128 : (s + 1) * 128], v.wo[s, :, cols])
            v.stage[:, :, cols] = total.astype(bf16).reshape(4, KP, 256)

        for k in range(4):
            squeeze(v.stage[k], v.pos.at[k])
        from_members(backward)
        d = total_of(v.dhr)
        d = norm_back(d, v.hc[...], v.sc[...])
        d = (d.astype(bf16).astype(f32) + v.ac[...].astype(f32)).astype(bf16)
        squeeze(d, v.dmo)

        copies = around(lambda k: v.dmo, v.dms, lambda: v.dmo[...])
        finish(copies)
        spread_all(v.dms)
        gathered_d = v.stage[...].reshape(4 * KP, 2048)
        for s in range(4):
            block = nt(gathered_d, v.wm[s]).astype(bf16)
            v.fcs[:, :, s * 256 : (s + 1) * 256] = block.reshape(4, KP, 256)
        copies = around(lambda k: v.fcs.at[turn(k)], v.dsr, lambda: v.fcs[z])
        outward = to_owners(v.pos, v.por, lambda s: None)
        finish(copies)

        ds = []
        hs = []
        for b in range(8):
            ds.append(v.dsr[b % 4, :, (b // 4) * 512 : (b // 4 + 1) * 512])
            hs.append(v.fc[:, b * 512 : (b + 1) * 512])
        for b, d in enumerate(norm_back_split(ds, hs, v.sfc[...])):
            k = b // 2
            v.dfc[k * KP : (k + 1) * KP, (b % 2) * 512 : (b % 2 + 1) * 512] = d.astype(bf16)
        sent(shift_foldc)
        pack("foldc_b", v.dfc[...], got.foldc_halo_t)
        copies = shift("foldc_b")
        foldc_own_t, foldc_pack_t = got.foldc_own_t, got.foldc_pack_t
        finish(shift_gm)
        adjoint_mid = placed(slice(None), v.gm, "gm", got.mid_own, got.mid_halo).astype(bf16).astype(f32)
        finish(copies)
        d = placed(slice(None), v.dfc, "foldc_b", foldc_own_t, foldc_pack_t)
        v.ym[...] = (adjoint_mid + d.astype(bf16).astype(f32)).astype(bf16)

        def dmix_mid(part, cols):
            v.mixm[part, cols] = nt(v.ym[part, :], out_m[cols, :]).astype(bf16)

        tiles(160, 160, 1024, 256, dmix_mid)
        attend_back(v.trm, v.trrm, v.psm, v.mixm, 8, 2, WP, 8)

        def to_wide(left, weight, blocks):
            @pl.loop(0, 2 * blocks, unroll=4)
            def _(j):
                v.wide[aligned(lax.div(j, 2) * 160, 160, 16), aligned(lax.rem(j, 2) * 256, 256, 128)] = nt(
                    left[...], weight[aligned(j * 256, 256, 128), :]
                )

        def wide_back(blocks, h, scale):
            ds = [v.wide[k * 160 : (k + 1) * 160, :] for k in range(blocks)]
            hs = [h[:, k * 512 : (k + 1) * 512] for k in range(blocks)]
            return [d.astype(bf16) for d in norm_back_split(ds, hs, scale[...])]

        to_wide(v.trm, qkv_m, 2)
        for k, d in enumerate(wide_back(2, v.hm, v.sm)):
            cols = slice(k * 512, (k + 1) * 512)
            v.xm[:, cols] = (d.astype(f32) + v.ym[:, cols].astype(f32)).astype(bf16)

        to_wide(v.xm, mrg_f, 4)
        for k, d in enumerate(wide_back(4, v.ff, v.sff)):
            v.mixf[k * 160 : (k + 1) * 160, :] = d
        sent(shift_fold)
        pack("fold_b", v.mixf[...], got.fold_halo_t)
        copies = shift("fold_b")

        from_members(outward)
        total = total_of(v.por)
        pack("coarse_b", (v.xc[...].astype(f32) + total).astype(bf16), got.coarse_halo_t)
        shift_out = shift("coarse_b")

        fold_pack_t = got.fold_pack_t
        finish(copies)

        @pl.loop(0, 5, unroll=5)
        def _(i):
            part = aligned(i * 128, 128, 128)
            d = tn(fold_own[:, part], v.mixf[...]) + nn(fold_pack_t[part, :], recv_buf["fold_b"][...])
            v.yf[part, :] = (v.yf[part, :].astype(f32) + d.astype(bf16).astype(f32)).astype(bf16)

        def dmix_fine(part, cols):
            v.mixf[part, cols] = nt(v.yf[part, :], out_f[cols, :]).astype(bf16)

        tiles(640, 320, 512, 256, dmix_fine)
        attend_back(v.trf, v.trrf, v.psf, v.mixf, 4, 8, WP, 8)

        def dh_fine(part, cols):
            v.wide[part, cols] = nt(v.trf[part, :], qkv_f[cols, :])

        tiles(640, 320, 512, 256, dh_fine)

        @pl.loop(0, 4, unroll=2)
        def _(i):
            part = aligned(i * 160, 160, 16)
            d = norm_back(v.wide[part, :], v.hf[part, :], v.sf[part, :])
            v.xf[part, :] = (d.astype(bf16).astype(f32) + v.yf[part, :].astype(f32)).astype(bf16)

        pack("fine_b", v.xf[...], got.fine_halo_t)
        copies = shift("fine_b")
        fine_pack_t = got.fine_pack_t
        finish(shift_out)
        out = nn(got.coarse_pack_t[...], recv_buf["coarse_b"][...]).astype(bf16)
        for r in range(6):
            coarse_ref[r] = out[16 * r : 16 * r + 6]
        writes = []
        fine_own_t = got.fine_own_t
        for j in range(4):
            here = (j * 160, min(j * 160 + 320, 640))
            v.wide[pl.ds(j * 144, 144), :] = nn(fine_own_t[:, : here[1] - here[0]], v.xf[here[0] : here[1], :])
        finish(copies)
        for j in range(4):
            part = pl.ds(j * 144, 144)
            d = v.wide[part, :] + nn(fine_pack_t[part, :], recv_buf["fine_b"][...])
            tokens[part, :] = d.astype(bf16)
            writes.append(pltpu.make_async_copy(tokens.at[part], grad_ref.at[part], local_sem.at[len(ALL_LOADED) + 3 + j]))
            writes[-1].start()
        for write in writes:
            write.wait()
        for copy in pending:
            copy.wait_send()
        for name in ALL_LOADED:
            getattr(got, name)

    any_space = pl.BlockSpec(memory_space=pl.ANY)
    whole = pl.BlockSpec(memory_space=pltpu.VMEM)
    return pl.pallas_call(
        kernel,
        out_shape=(jax.ShapeDtypeStruct((576, 512), bf16), jax.ShapeDtypeStruct((6, 6, 2048), bf16)),
        in_specs=[any_space] * len(shapes),
        out_specs=(any_space, whole),
        scratch_shapes=[pltpu.VMEM(*shape) for group in (scratch, loaded, sends, receives) for shape in group.values()]
        + [pltpu.SemaphoreType.DMA((N_LOCAL,)), pltpu.SemaphoreType.DMA((N_REMOTE,)), pltpu.SemaphoreType.DMA((N_REMOTE,))],
        compiler_params=pltpu.CompilerParams(
            collective_id=0, has_side_effects=True, vmem_limit_bytes=66_584_576
        ),
    )


def shards(
    tokens, qkv_fine, out_fine, merge_fine, qkv_mid, out_mid, merge_mid, qkv_coarse, out_coarse, grad_fine, grad_mid, grad_coarse
):
    values = dict(
        tokens=tokens.reshape(576, 512),
        qkv_f=qkv_fine,
        out_f=out_fine,
        mrg_f=merge_fine,
        qkv_m=qkv_mid,
        out_m=out_mid,
        wm=merge_mid,
        wq=qkv_coarse,
        wo=out_coarse,
        g_fine=grad_fine.reshape(576, 512),
        g_mid=grad_mid,
        g_coarse=grad_coarse,
        bias=jnp.asarray(BIAS),
        biasc=jnp.asarray(BIASC),
    )
    for name, matrix in CONSTANTS.items():
        values[name] = jnp.asarray(matrix, bf16)
    shapes = {name: (value.shape, value.dtype) for name, value in values.items()}
    gradient, coarse = build(shapes)(*values.values())
    return gradient.reshape(24, 24, 512), coarse


def solution(mesh):
    placed = (
        P("lat", "lon", None),
        P(),
        P(),
        P(),
        P(),
        P(),
        P("lon", None),
        P(None, "lon"),
        P("lon", None),
        P("lat", "lon", None),
        P("lat", "lon", None),
        P("lat", "lon", None),
    )
    return jax.shard_map(
        shards,
        mesh=mesh,
        in_specs=placed,
        out_specs=(P("lat", "lon", None), P("lat", "lon", None)),
        check_vma=False,
    )
```

```python
from types import SimpleNamespace

import jax
import jax.numpy as jnp
import numpy as np
from jax import lax
from jax.experimental import pallas as pl
from jax.experimental.pallas import tpu as pltpu
from jax.sharding import PartitionSpec as P

HD = 64
WH = 6
WW = 12
WP = 80
KP = 48
EPS = 1e-05
LAT = 8
LON = 16
bf16 = jnp.bfloat16
f32 = jnp.float32
MESH = pl.DeviceIdType.MESH


def window_order(cols):
    across = cols // WW

    def index(r, c):
        return ((r // WH) * across + c // WW) * WP + (r % WH) * WW + c % WW

    return index


def raster(stride):
    return lambda r, c: r * stride + c


def fold_order(inner, stride):
    def index(r, c):
        return ((c % 2) * 2 + r % 2) * stride + inner(r // 2, c // 2)

    return index


def shift_maps(size, src, n_src, dst, n_dst):
    dr, dc = WH // 2, WW // 2
    up = -(-(size - dr) * dc // 32) * 32
    down = -(-max(dr * (size - dc), 0) // 32) * 32
    corner = 32
    parts = [(0, up, 0, 1), (up, down, 1, 0), (up + down, corner, 1, 1)]
    total = up + down + corner
    own = np.zeros((n_dst, n_src), np.float32)
    halo = np.zeros((n_dst, total), np.float32)
    pack = np.zeros((total, n_src), np.float32)
    for r in range(size):
        for c in range(size):
            to = dst(r, c)
            if r >= dr and c >= dc:
                own[to, src(r - dr, c - dc)] = 1
                continue
            if r >= dr:
                slot = (r - dr) * dc + c
            elif c >= dc:
                slot = up + r * (size - dc) + c - dc
            else:
                slot = up + down + r * dc + c
            halo[to, slot] = 1
            pack[slot, src((r - dr) % size, (c - dc) % size)] = 1
    return own, halo, pack, [part for part in parts if part[1]]


def window_bias(stride, rows, groups):
    token = np.arange(rows)
    real = token % stride < groups * 2
    upper = token % stride < groups
    allowed = np.broadcast_to(real[None, :], (rows, rows))
    split = allowed & (upper[:, None] == upper[None, :])
    both = np.stack([allowed, split])
    both = np.concatenate([both, both], 1)
    return np.where(both, 0.0, -1e30).astype(np.float32)


FINE = shift_maps(24, raster(24), 576, window_order(24), 640)
FOLD = shift_maps(24, window_order(24), 640, fold_order(window_order(12), 160), 640)
MID = shift_maps(12, raster(16), 192, window_order(12), 160)
FOLDC = shift_maps(12, window_order(12), 160, fold_order(raster(6), KP), 4 * KP)
COARSE = shift_maps(6, raster(16), 96, raster(6), KP)
BIAS = window_bias(WP, WP, 36)
BIASC = window_bias(KP, 2 * KP, 18)

SQUEEZE = np.zeros((144, 4 * KP), np.float32)
for k in range(4):
    SQUEEZE[k * 36 : (k + 1) * 36, k * KP : k * KP + 36] = np.eye(36)
TOP = 80
FINE_BAND = np.ascontiguousarray(FINE[0][160:320, 144 - TOP : 304 - TOP])
FINE_BAND_BACK = np.ascontiguousarray(FINE[0][160:480, 144:288].T)
CONSTANTS = dict(
    fine_own=FINE_BAND, fine_halo=FINE[1], fine_pack=FINE[2],
    fine_own_t=FINE_BAND_BACK, fine_halo_t=FINE[1].T, fine_pack_t=FINE[2].T,
    fold_own=FOLD[0], fold_halo=FOLD[1], fold_pack=FOLD[2], fold_halo_t=FOLD[1].T, fold_pack_t=FOLD[2].T,
    mid_own=MID[0], mid_halo=MID[1], mid_pack=MID[2],
    foldc_own=FOLDC[0], foldc_halo=FOLDC[1], foldc_pack=FOLDC[2],
    foldc_own_t=FOLDC[0].T, foldc_halo_t=FOLDC[1].T, foldc_pack_t=FOLDC[2].T,
    squeeze=SQUEEZE, squeeze_t=SQUEEZE.T,
    coarse_halo=COARSE[1], coarse_pack=COARSE[2], coarse_halo_t=COARSE[1].T, coarse_pack_t=COARSE[2].T,
)

LOADED = (
    tuple(dict(tokens=1, fine_pack=1, fine_own=1, fine_halo=1)),
    tuple(dict(
        qkv_f=1, g_coarse=1, coarse_pack=1, g_mid=1, mid_pack=1, g_fine=1, bias=1, out_f=1, fold_pack=1, fold_own=1, fold_halo=1,
    )),
    tuple(dict(
        mrg_f=1, coarse_halo=1, squeeze=1, squeeze_t=1, qkv_m=1, out_m=1, foldc_pack=1, foldc_own=1, foldc_halo=1, biasc=1,
        mid_own=1, mid_halo=1, foldc_halo_t=1, foldc_own_t=1, foldc_pack_t=1, fold_halo_t=1, fold_pack_t=1,
        fine_halo_t=1, fine_own_t=1, fine_pack_t=1, coarse_halo_t=1, coarse_pack_t=1,
    )),
)
ALL_LOADED = [name for group in LOADED for name in group]


def nn(a, b):
    return jnp.dot(a, b, preferred_element_type=f32)


def nt(a, b):
    return lax.dot_general(a, b, (((1,), (1,)), ((), ())), preferred_element_type=f32)


def tn(a, b):
    return lax.dot_general(a, b, (((0,), (0,)), ((), ())), preferred_element_type=f32)


def norm_rows(x):
    centred = x - jnp.mean(x, axis=-1, keepdims=True)
    scale = lax.rsqrt(jnp.mean(centred * centred, axis=-1, keepdims=True) + EPS)
    return centred * scale, scale


def norm_back(d, h, scale):
    d = d.astype(bf16).astype(f32)
    h = h.astype(f32)
    return scale * (d - jnp.mean(d, axis=-1, keepdims=True) - h * jnp.mean(d * h, axis=-1, keepdims=True))


def norm_split(parts):
    size = sum(p.shape[-1] for p in parts)
    average = sum(jnp.sum(p, axis=-1, keepdims=True) for p in parts) / size
    parts = [p - average for p in parts]
    scale = lax.rsqrt(sum(jnp.sum(p * p, axis=-1, keepdims=True) for p in parts) / size + EPS)
    return [p * scale for p in parts], scale


def norm_back_split(ds, hs, scale):
    size = sum(d.shape[-1] for d in ds)
    ds = [d.astype(bf16).astype(f32) for d in ds]
    hs = [h.astype(f32) for h in hs]
    mean_d = sum(jnp.sum(d, axis=-1, keepdims=True) for d in ds) / size
    mean_dh = sum(jnp.sum(d * h, axis=-1, keepdims=True) for d, h in zip(ds, hs)) / size
    return [scale * (d - mean_d - h * mean_dh) for d, h in zip(ds, hs)]


def aligned(start, size, multiple):
    return pl.ds(pl.multiple_of(start, multiple), size)


def project_qkv(h, weight, tr, trr, rows, pairs, step):
    @pl.loop(0, rows // step)
    def _(i):
        part = aligned(i * step, step, 16)

        @pl.loop(0, pairs, unroll=2)
        def _(p):
            wide = nn(h[part, :], weight(p))
            tr[part, aligned(p * 384, 384, 128)] = wide.astype(bf16)
            ra, rb, rc = (pltpu.roll(wide[:, k * 128 : (k + 1) * 128], 64, 1) for k in range(3))
            low = lax.broadcasted_iota(jnp.int32, (1, 128), 1) < 64
            trr[part, aligned(p * 256, 128, 128)] = jnp.where(low, ra, rc).astype(bf16)
            trr[part, aligned(p * 256 + 128, 128, 128)] = jnp.where(low, rb, ra).astype(bf16)


def halves():
    lane = lax.broadcasted_iota(jnp.int32, (1, 128), 1)
    low = lane < 64
    one = jnp.where(low, 1.0, 0.0)
    return low, one.astype(bf16), (1.0 - one).astype(bf16)


def attend(tr, trr, ps, mix, bias, pairs, windows, wp, split, unroll, part=0, parts=1):
    steps = pairs * windows // unroll // parts

    @pl.loop(part * steps, (part + 1) * steps)
    def _(step):
        low, mlo, mhi = halves()
        stores = []
        for u in range(unroll):
            item = step * unroll + u
            w, p = lax.div(item, pairs), lax.rem(item, pairs)
            part = aligned(w * wp, wp, 16)
            a, b, c = (tr[part, aligned(p * 384 + k * 128, 128, 128)] for k in range(3))
            k2 = trr[part, aligned(p * 256, 128, 128)]
            eighth = jnp.asarray(HD**-0.5, bf16)
            q2 = jnp.concatenate([a * (mlo * eighth), b * (mhi * eighth)], 0)
            scores = nt(q2, k2) + bias[split(w)]
            e = jnp.exp(scores - jnp.max(scores, axis=-1, keepdims=True))
            weights = (e / jnp.sum(e, axis=-1, keepdims=True)).astype(bf16)
            mixed = jnp.where(low, nn(weights[:wp], b), nn(weights[wp:], c))
            stores.append((item, weights, (part, aligned(p * 128, 128, 128)), mixed.astype(bf16)))
        for item, weights, place, mixed in stores:
            ps[item] = weights
            mix[place] = mixed


def attend_back(tr, trr, ps, dmix, pairs, windows, wp, unroll):
    @pl.loop(0, pairs * windows // unroll)
    def _(step):
        low, mlo, mhi = halves()
        stores = []
        for u in range(unroll):
            item = step * unroll + u
            w, p = lax.div(item, pairs), lax.rem(item, pairs)
            part = aligned(w * wp, wp, 16)
            places = [(part, aligned(p * 384 + k * 128, 128, 128)) for k in range(3)]
            b, c = tr[places[1]], tr[places[2]]
            k2, q2 = (trr[part, aligned(p * 256 + k * 128, 128, 128)] for k in range(2))
            do = dmix[part, aligned(p * 128, 128, 128)]
            weights = ps[item]
            outs = []
            for half, mask, values in ((0, mlo, b), (1, mhi, c)):
                wt = weights[half * wp : (half + 1) * wp]
                wide = wt.astype(f32)
                dw = nt(do * mask, values)
                ds = wide * (dw - jnp.sum(wide * dw, axis=-1, keepdims=True)) * HD**-0.5
                outs.append((wt, ds.astype(bf16)))
            (w0, ds0), (w1, ds1) = outs
            stores.append((places[0], jnp.where(low, nn(ds0, k2), tn(ds0, q2)).astype(bf16)))
            stores.append((places[1], jnp.where(low, tn(w0, do), nn(ds1, k2)).astype(bf16)))
            stores.append((places[2], jnp.where(low, tn(ds1, q2), tn(w1, do)).astype(bf16)))
        for place, value in stores:
            tr[place] = value


def tiles(rows, step, cols, width, body):
    @pl.loop(0, rows // step)
    def _(i):
        part = aligned(i * step, step, 16)

        @pl.loop(0, cols // width, unroll=min(4, cols // width))
        def _(j):
            body(part, aligned(j * width, width, 128))


VMEM_SCRATCH = dict(
    xf=((640, 512), bf16), hf=((640, 512), bf16), sf=((640, 1), f32), trf=((640, 1536), bf16),
    trrf=((640, 1024), bf16), psf=((32, 2 * WP, WP), bf16), mixf=((640, 512), bf16), yf=((640, 512), bf16),
    wide=((640, 512), f32),
    ff=((160, 2048), bf16), sff=((160, 1), f32),
    xm=((160, 1024), bf16), hm=((160, 1024), bf16), sm=((160, 1), f32), trm=((160, 3072), bf16),
    trrm=((160, 2048), bf16), psm=((16, 2 * WP, WP), bf16), mixm=((160, 1024), bf16), ym=((160, 1024), bf16),
    fc=((KP, 4096), bf16), sfc=((KP, 1), f32), fcs=((4, KP, 1024), bf16), fcr=((4, KP, 1024), bf16),
    pms=((4, 144, 512), bf16), pmr=((4, 144, 512), bf16), dmo=((144, 512), bf16), dms=((4, 144, 512), bf16), stage=((4, KP, 2048), bf16),
    dsr=((4, KP, 1024), bf16), dfc=((4 * KP, 1024), bf16),
    gm=((192, 1024), bf16),
    xc=((KP, 2048), bf16), hc=((KP, 2048), bf16), sc=((KP, 1), f32), hcs=((144, 512), bf16), hcr=((4, 144, 512), bf16),
    ac=((KP, 2048), bf16), acs=((144, 512), bf16), acr=((4, 144, 512), bf16),
    trc=((4 * KP, 1536), bf16), trrc=((4 * KP, 1024), bf16), psc=((8, 4 * KP, 2 * KP), bf16),
    mixc=((4 * KP, 512), bf16), dmixc=((4 * KP, 512), bf16),
    dhs=((4, 144, 512), bf16), dhr=((4, 144, 512), bf16), pos=((4, 144, 512), bf16), por=((4, 144, 512), bf16),
    wm=((4, 256, 2048), bf16), wq=((4, 2048, 384), bf16), wo=((4, 128, 2048), bf16),
)
EXCHANGES = dict(
    tok=(FINE, 512, 1), gf=(FINE, 512, 1), gm=(MID, 1024, 1), gc=(COARSE, 2048, 1), fold=(FOLD, 512, 1), foldc=(FOLDC, 1024, 1),
    foldc_b=(FOLDC, 1024, -1), fold_b=(FOLD, 512, -1), fine_b=(FINE, 512, -1), coarse_b=(COARSE, 2048, -1),
)
SENT_FROM = dict(fold="tok", fold_b="tok", fine_b="tok", foldc_b="foldc", coarse_b="gc")
N_LOCAL = len(ALL_LOADED) + 7
N_REMOTE = 96


class Lazy:
    def __init__(self, make):
        self.make = make

    def __getattr__(self, name):
        value = self.make(name)
        setattr(self, name, value)
        return value


def build(shapes):
    scratch = dict(VMEM_SCRATCH)
    loaded = {name: shapes[name] for name in ALL_LOADED}
    for name in ("tokens", "g_fine"):
        loaded[name] = ((TOP + 576, 512), bf16)
    sends, receives = {}, {}
    for name, (maps, width, _) in EXCHANGES.items():
        receives[name] = ((maps[1].shape[1], width), bf16)
        if name not in SENT_FROM:
            sends[name] = receives[name]

    def kernel(*refs):
        refs = list(refs)

        def take(names):
            return {name: refs.pop(0) for name in names}

        hbm = take(shapes)
        grad_ref, coarse_ref = refs.pop(0), refs.pop(0)
        v = SimpleNamespace(**take(scratch))
        vm, send_buf, recv_buf = take(loaded), take(sends), take(receives)
        local_sem, send_sem, recv_sem = refs

        lat, lon = lax.axis_index("lat"), lax.axis_index("lon")
        y, z, core = lax.div(lon, 8), lax.rem(lax.div(lon, 2), 4), lax.rem(lon, 2)

        def near(dlat, dlon):
            return (lax.rem(lat + dlat + LAT, LAT), lax.rem(lon + dlon + LON, LON))

        def at(yy, zz, cc):
            return (lat, yy * 8 + zz * 2 + cc)

        def turn(k):
            return lax.rem(z + k, 4)

        loads = {}
        for i, name in enumerate(ALL_LOADED):
            dest = vm[name].at[pl.ds(TOP, 576)] if name in ("tokens", "g_fine") else vm[name]
            loads[name] = pltpu.make_async_copy(hbm[name], dest, local_sem.at[i])

        def start_loads(group):
            for name in group:
                loads[name].start()

        start_loads(LOADED[0])

        def wait_load(name):
            loads[name].wait()
            return vm[name]

        got = Lazy(wait_load)

        own_slot = y * 2 + core
        own_loads = []
        for i, name in enumerate(("wm", "wq", "wo")):
            copy = pltpu.make_async_copy(hbm[name], getattr(v, name).at[own_slot], local_sem.at[len(ALL_LOADED) + i])
            own_loads.append(copy)

        barrier = pltpu.get_barrier_semaphore()
        others = [near(1, 0), near(-1, 0), near(1, 1), near(-1, -1)]
        others += [(lat + 1 - 2 * lax.rem(lat, 2), lax.rem(lon + 8, LON))]
        others += [(lat, y * 8 + lax.rem(lax.rem(lon, 8) + k, 8)) for k in range(1, 8)]
        for device in others:
            pl.semaphore_signal(barrier, inc=1, device_id=device, device_id_type=MESH)
        place = lax.rem(lon, 8)

        @pl.when(place == 7)
        def _():
            pl.semaphore_signal(barrier, inc=1, device_id=near(0, 1), device_id_type=MESH)

        @pl.when(place == 0)
        def _():
            pl.semaphore_signal(barrier, inc=1, device_id=near(0, -1), device_id_type=MESH)

        edge = jnp.where((place == 7) | (place == 0), 1, 0)

        counter = [0]

        def sems(n):
            counter[0] += n
            assert counter[0] <= N_REMOTE
            return counter[0] - n

        def remote(src, dst, send, recv, device):
            return pltpu.make_async_remote_copy(
                src_ref=src, dst_ref=dst, send_sem=send_sem.at[send], recv_sem=recv_sem.at[recv],
                device_id=device, device_id_type=MESH,
            )

        pending = []

        def sender(name):
            return send_buf[SENT_FROM.get(name, name)]

        def finish(copies):
            for copy in copies:
                copy.wait()

        def sent(copies):
            for copy in copies:
                copy.wait_send()

        def shift(name):
            maps, _, sign = EXCHANGES[name]
            base = sems(3)
            copies = []
            for k, (start, size, dlat, dlon) in enumerate(maps[3]):
                part = pl.ds(start, size)
                copies.append(
                    remote(sender(name).at[part], recv_buf[name].at[part], base + k, base + k, near(sign * dlat, sign * dlon))
                )
            for copy in copies:
                copy.start()
            return copies

        def received(copies):
            for copy in copies:
                copy.wait_recv()

        sibling = at(y, z, 1 - core)
        partner_slot = (1 - y) * 2 + core
        y_low = lax.rem(lat, 2)
        beside = lat + 1 - 2 * y_low

        def weight_piece(name, start, size):
            base = sems(2)
            dest = getattr(v, name)
            half = hbm[name].shape[0] // 2
            mine = aligned(y_low * half + start, size, 16)
            other = aligned((1 - y_low) * half + start, size, 16)
            there = dest.at[partner_slot, other]
            return (
                remote(hbm[name].at[mine], dest.at[own_slot, mine], base, base, (beside, lax.rem(lon + 8, LON))),
                remote(there, there, base + 1, base + 1, (beside, lon)),
            )

        def core_copies(name):
            base = sems(2)
            dest = getattr(v, name)
            there = dest.at[partner_slot]
            return (
                remote(hbm[name], dest.at[own_slot], base, base, sibling),
                remote(there, there, base + 1, base + 1, sibling),
            )

        pieces = dict(
            wm=[weight_piece("wm", 0, 128)],
            wq=[weight_piece("wq", 0, 640), weight_piece("wq", 640, 384)],
            wo=[weight_piece("wo", 0, 64)],
        )
        between_cores = {name: core_copies(name) for name in pieces}

        def cross_weights(name, i):
            pieces[name][i][0].start()

        def relay_weights(name, i):
            pieces[name][i][0].wait_recv()
            pieces[name][i][1].start()

        def pass_weights(name):
            for piece in pieces[name]:
                piece[1].wait_recv()
            between_cores[name][1].start()

        def weights_ready(name):
            for copy in between_cores[name]:
                copy.wait_recv()
                pending.append(copy)
            for piece in pieces[name]:
                pending.extend(piece)

        def pack(name, source, matrix):
            sender(name)[...] = nn(matrix[...], source).astype(bf16)

        tokens = got.tokens
        pack("tok", tokens[TOP:, :], got.fine_pack)
        pl.semaphore_wait(barrier, len(others) + edge)
        shift_tok = shift("tok")
        start_loads(LOADED[1])
        tokens[0:TOP, :] = jnp.zeros((TOP, 512), bf16)
        vm["g_fine"][0:TOP, :] = jnp.zeros((TOP, 512), bf16)
        v.gm[...] = jnp.zeros_like(v.gm)
        fine_own, fine_halo, qkv_f = got.fine_own, got.fine_halo, got.qkv_f

        def placed(part, source, name, own, halo):
            return nn(own[part, :], source[...]) + nn(halo[part, :], recv_buf[name][...])

        def placed_fine(i, source, name):
            return nn(fine_own[...], source[aligned(i * 144, 160, 16), :]) + nn(
                fine_halo[aligned(i * 160, 160, 16), :], recv_buf[name][...]
            )

        received(shift_tok)
        cross_weights("wm", 0)

        @pl.loop(0, 4, unroll=2)
        def _(i):
            part = aligned(i * 160, 160, 16)
            x = placed_fine(i, tokens, "tok")
            v.xf[part, :] = x.astype(bf16)
            h, scale = norm_rows(x)
            v.hf[part, :] = h.astype(bf16)
            v.sf[part, :] = scale

        for r in range(6):
            for k in range(2):
                v.gm[96 * k + 16 * r : 96 * k + 16 * r + 6, :] = got.g_coarse[r, :, k * 1024 : (k + 1) * 1024]
        for k in range(2):
            packed = nn(got.coarse_pack[...], v.gm[96 * k : 96 * (k + 1), :])
            sender("gc")[:, k * 1024 : (k + 1) * 1024] = packed.astype(bf16)
        shift_gc = shift("gc")
        start_loads(LOADED[2])
        for copy in own_loads:
            copy.start()
        for name in pieces:
            between_cores[name][0].start()
        project_qkv(v.hf, lambda p: qkv_f[:, aligned(p * 384, 384, 128)], v.trf, v.trrf, 640, 4, 320)
        first = lat == 0
        bias, out_f = got.bias, got.out_f
        attend(v.trf, v.trrf, v.psf, v.mixf, bias, 4, 8, WP, lambda w: jnp.where(first & (w < 2), 1, 0), 8)

        def out_fine(part, cols):
            v.yf[part, cols] = (nn(v.mixf[part, :], out_f[:, cols]) + v.xf[part, cols].astype(f32)).astype(bf16)

        tiles(640, 320, 512, 256, out_fine)

        sent(shift_tok)
        pack("fold", v.yf[...], got.fold_pack)
        shift_fold = shift("fold")
        fold_own, fold_halo, mrg_f = got.fold_own, got.fold_halo, got.mrg_f
        slot = lax.rem(z, 2) * 2 + core
        wide_group = lax.div(z, 2)

        def squeeze(x, dest):
            stacked = jnp.concatenate([x[:, k * 512 : (k + 1) * 512] for k in range(4)], 0)
            dest[...] = nn(got.squeeze[...], stacked).astype(bf16)

        def spread(packed):
            stacked = nn(got.squeeze_t[...], packed.astype(bf16))
            return [stacked[k * KP : (k + 1) * KP] for k in range(4)]

        def spread_all(packed):
            for s in range(4):
                for k, part in enumerate(spread(packed[s])):
                    v.stage[s, :, k * 512 : (k + 1) * 512] = part.astype(bf16)

        def total_of(packed):
            return jnp.concatenate(spread(sum(packed[k].astype(f32) for k in range(4))), 1)

        def to_group(source, dest):
            send, recv = sems(4), sems(4)
            for k in range(1, 4):
                copy = remote(source, dest.at[slot], send + k, recv + slot, at(y, turn(k), wide_group))
                copy.start()
                pending.append(copy)
            across = remote(source, dest.at[slot], send, recv + slot, sibling)

            @pl.when(core == wide_group)
            def _():
                dest[slot] = source[...]

            @pl.when(core != wide_group)
            def _():
                across.start()

            return source, dest, send, recv, across

        def is_own(s):
            return (z == core * 2 + s // 2) & (core == s % 2)

        def from_group(handle):
            source, dest, send, recv, across = handle

            @pl.when(core != wide_group)
            def _():
                across.wait_send()

            for s in range(4):

                @pl.when(jnp.logical_not(is_own(s)))
                def _(s=s):
                    remote(source, dest.at[s], send, recv + s, sibling).wait_recv()

        def to_owners(source, dest, prepare):
            send, recv = sems(4), sems(4)
            for s in range(4):
                prepare(s)
                copy = remote(source.at[s], dest.at[z], send + s, recv + z, at(y, core * 2 + s // 2, s % 2))

                @pl.when(is_own(s))
                def _(s=s):
                    dest[z] = source[s]

                @pl.when(jnp.logical_not(is_own(s)))
                def _(copy=copy):
                    copy.start()

            return source, dest, send, recv

        def from_members(handle):
            source, dest, send, recv = handle
            for k in range(4):

                @pl.when(jnp.logical_not((z == k) & (core == wide_group)))
                def _(k=k):
                    remote(source.at[0], dest.at[k], send, recv + k, sibling).wait_recv()

            for s in range(4):

                @pl.when(jnp.logical_not(is_own(s)))
                def _(s=s):
                    remote(source.at[s], dest.at[0], send + s, recv, sibling).wait_send()

        def around(pick, dest, own):
            base = sems(4)
            copies = []
            for k in range(1, 4):
                copy = remote(pick(k), dest.at[z], base + k, base + k, at(y, turn(k), core))
                copy.start()
                copies.append(copy)
            dest[z] = own()
            return copies

        for r in range(12):
            v.gm[16 * r : 16 * r + 12, :] = got.g_mid[r]
        pack("gm", v.gm[...], got.mid_pack)
        shift_gm = shift("gm")
        pack("gf", got.g_fine[TOP:, :], got.fine_pack)
        shift_gf = shift("gf")

        relay_weights("wm", 0)
        cross_weights("wq", 0)
        finish(shift_gc)
        v.ac[...] = nn(got.coarse_halo[...], recv_buf["gc"][...]).astype(bf16)
        squeeze(v.ac[...], v.acs)
        received(shift_fold)
        adjoint = to_group(v.acs, v.acr)

        quads = [placed(slice(k * 160, (k + 1) * 160), v.yf, "fold", fold_own, fold_halo) for k in range(4)]
        normed, scale = norm_split(quads)
        for k in range(4):
            v.ff[:, k * 512 : (k + 1) * 512] = normed[k].astype(bf16)
        v.sff[...] = scale
        def merge_fine(part, cols):
            v.xm[part, cols] = nn(v.ff[part, :], mrg_f[:, cols]).astype(bf16)

        tiles(160, 160, 1024, 256, merge_fine)

        qkv_m, out_m = got.qkv_m, got.out_m
        h, scale = norm_rows(v.xm[...].astype(f32))
        v.hm[...] = h.astype(bf16)
        v.sm[...] = scale
        project_qkv(v.hm, lambda p: qkv_m[:, aligned(p * 384, 384, 128)], v.trm, v.trrm, 160, 8, 160)
        attend(v.trm, v.trrm, v.psm, v.mixm, bias, 8, 2, WP, lambda w: jnp.where(first & (w < 1), 1, 0), 8)

        def out_mid(part, cols):
            v.ym[part, cols] = (nn(v.mixm[part, :], out_m[:, cols]) + v.xm[part, cols].astype(f32)).astype(bf16)

        tiles(160, 160, 1024, 256, out_mid)

        pack("foldc", v.ym[...], got.foldc_pack)
        shift_foldc = shift("foldc")
        foldc_own, foldc_halo = got.foldc_own, got.foldc_halo
        relay_weights("wq", 0)
        cross_weights("wq", 1)
        cross_weights("wo", 0)
        pass_weights("wm")
        received(shift_foldc)
        folded = placed(slice(None), v.ym, "foldc", foldc_own, foldc_halo)
        quads = [folded[k * KP : (k + 1) * KP] for k in range(4)]
        normed, scale = norm_split(quads)
        v.sfc[...] = scale
        for k in range(4):
            h = normed[k].astype(bf16)
            v.fc[:, k * 1024 : (k + 1) * 1024] = h
            for j in range(2):
                block = 2 * k + j
                v.fcs[block % 4, :, (block // 4) * 512 : (block // 4 + 1) * 512] = h[:, j * 512 : (j + 1) * 512]
        copies = around(lambda k: v.fcs.at[turn(k)], v.fcr, lambda: v.fcs[z])
        finish(copies)
        for copy in own_loads:
            copy.wait()
        weights_ready("wm")
        gathered = v.fcr[...].reshape(4 * KP, 1024)

        @pl.loop(0, 8, unroll=4)
        def _(j):
            cols = aligned(j * 256, 256, 128)
            total = nn(gathered[:, 0:256], v.wm[0, :, cols])
            for s in range(1, 4):
                total += nn(gathered[:, s * 256 : (s + 1) * 256], v.wm[s, :, cols])
            v.stage[:, :, cols] = total.astype(bf16).reshape(4, KP, 256)

        def merged_block(k):
            block = v.pms.at[turn(k)]
            squeeze(v.stage[turn(k)], block)
            return block

        copies = around(merged_block, v.pmr, lambda: merged_block(0)[...])
        relay_weights("wq", 1)
        relay_weights("wo", 0)
        finish(shift_gf)

        @pl.loop(0, 4, unroll=2)
        def _(i):
            part = aligned(i * 160, 160, 16)
            v.yf[part, :] = placed_fine(i, got.g_fine, "gf").astype(bf16)

        finish(copies)
        x = total_of(v.pmr).astype(bf16)
        v.xc[...] = x
        h, scale = norm_rows(x.astype(f32))
        v.hc[...] = h.astype(bf16)
        v.sc[...] = scale

        squeeze(v.hc[...], v.hcs)
        forward = to_group(v.hcs, v.hcr)
        pass_weights("wq")
        pass_weights("wo")
        biasc = got.biasc
        from_group(adjoint)
        spread_all(v.acr)
        weights_ready("wo")
        for p in range(4):
            v.dmixc[:, p * 128 : (p + 1) * 128] = nt(v.stage[...].reshape(4 * KP, 2048), v.wo[p]).astype(bf16)
        weights_ready("wq")
        from_group(forward)
        spread_all(v.hcr)
        project_qkv(v.stage.reshape(4 * KP, 2048), lambda p: v.wq[p], v.trc, v.trrc, 4 * KP, 4, 4 * KP)
        attend(v.trc, v.trrc, v.psc, v.mixc, biasc, 4, 2, 2 * KP, lambda w: jnp.where(first, 1, 0), 8)
        attend_back(v.trc, v.trrc, v.psc, v.dmixc, 4, 2, 2 * KP, 8)

        @pl.loop(0, 8, unroll=4)
        def _(j):
            rows = aligned(j * 256, 256, 128)
            total = nt(v.trc[:, 0:384], v.wq[0, rows, :])
            for s in range(1, 4):
                total += nt(v.trc[:, s * 384 : (s + 1) * 384], v.wq[s, rows, :])
            v.stage[:, :, rows] = total.astype(bf16).reshape(4, KP, 256)

        backward = to_owners(v.dhs, v.dhr, lambda s: squeeze(v.stage[s], v.dhs.at[s]))

        @pl.loop(0, 8, unroll=4)
        def _(j):
            cols = aligned(j * 256, 256, 128)
            total = nn(v.mixc[:, 0:128], v.wo[0, :, cols])
            for s in range(1, 4):
                total += nn(v.mixc[:, s * 128 : (s + 1) * 128], v.wo[s, :, cols])
            v.stage[:, :, cols] = total.astype(bf16).reshape(4, KP, 256)

        for k in range(4):
            squeeze(v.stage[k], v.pos.at[k])
        from_members(backward)
        d = total_of(v.dhr)
        d = norm_back(d, v.hc[...], v.sc[...])
        d = (d.astype(bf16).astype(f32) + v.ac[...].astype(f32)).astype(bf16)
        squeeze(d, v.dmo)

        copies = around(lambda k: v.dmo, v.dms, lambda: v.dmo[...])
        finish(copies)
        spread_all(v.dms)
        gathered_d = v.stage[...].reshape(4 * KP, 2048)
        for s in range(4):
            block = nt(gathered_d, v.wm[s]).astype(bf16)
            v.fcs[:, :, s * 256 : (s + 1) * 256] = block.reshape(4, KP, 256)
        copies = around(lambda k: v.fcs.at[turn(k)], v.dsr, lambda: v.fcs[z])
        outward = to_owners(v.pos, v.por, lambda s: None)
        finish(copies)

        ds = []
        hs = []
        for b in range(8):
            ds.append(v.dsr[b % 4, :, (b // 4) * 512 : (b // 4 + 1) * 512])
            hs.append(v.fc[:, b * 512 : (b + 1) * 512])
        for b, d in enumerate(norm_back_split(ds, hs, v.sfc[...])):
            k = b // 2
            v.dfc[k * KP : (k + 1) * KP, (b % 2) * 512 : (b % 2 + 1) * 512] = d.astype(bf16)
        sent(shift_foldc)
        pack("foldc_b", v.dfc[...], got.foldc_halo_t)
        copies = shift("foldc_b")
        foldc_own_t, foldc_pack_t = got.foldc_own_t, got.foldc_pack_t
        finish(shift_gm)
        adjoint_mid = placed(slice(None), v.gm, "gm", got.mid_own, got.mid_halo).astype(bf16).astype(f32)
        finish(copies)
        d = placed(slice(None), v.dfc, "foldc_b", foldc_own_t, foldc_pack_t)
        v.ym[...] = (adjoint_mid + d.astype(bf16).astype(f32)).astype(bf16)

        def dmix_mid(part, cols):
            v.mixm[part, cols] = nt(v.ym[part, :], out_m[cols, :]).astype(bf16)

        tiles(160, 160, 1024, 256, dmix_mid)
        attend_back(v.trm, v.trrm, v.psm, v.mixm, 8, 2, WP, 8)

        def to_wide(left, weight, blocks):
            @pl.loop(0, 2 * blocks, unroll=4)
            def _(j):
                v.wide[aligned(lax.div(j, 2) * 160, 160, 16), aligned(lax.rem(j, 2) * 256, 256, 128)] = nt(
                    left[...], weight[aligned(j * 256, 256, 128), :]
                )

        def wide_back(blocks, h, scale):
            ds = [v.wide[k * 160 : (k + 1) * 160, :] for k in range(blocks)]
            hs = [h[:, k * 512 : (k + 1) * 512] for k in range(blocks)]
            return [d.astype(bf16) for d in norm_back_split(ds, hs, scale[...])]

        to_wide(v.trm, qkv_m, 2)
        for k, d in enumerate(wide_back(2, v.hm, v.sm)):
            cols = slice(k * 512, (k + 1) * 512)
            v.xm[:, cols] = (d.astype(f32) + v.ym[:, cols].astype(f32)).astype(bf16)

        to_wide(v.xm, mrg_f, 4)
        for k, d in enumerate(wide_back(4, v.ff, v.sff)):
            v.mixf[k * 160 : (k + 1) * 160, :] = d
        sent(shift_fold)
        pack("fold_b", v.mixf[...], got.fold_halo_t)
        copies = shift("fold_b")

        from_members(outward)
        total = total_of(v.por)
        pack("coarse_b", (v.xc[...].astype(f32) + total).astype(bf16), got.coarse_halo_t)
        shift_out = shift("coarse_b")

        fold_pack_t = got.fold_pack_t
        finish(copies)

        @pl.loop(0, 5, unroll=5)
        def _(i):
            part = aligned(i * 128, 128, 128)
            d = tn(fold_own[:, part], v.mixf[...]) + nn(fold_pack_t[part, :], recv_buf["fold_b"][...])
            v.yf[part, :] = (v.yf[part, :].astype(f32) + d.astype(bf16).astype(f32)).astype(bf16)

        def dmix_fine(part, cols):
            v.mixf[part, cols] = nt(v.yf[part, :], out_f[cols, :]).astype(bf16)

        tiles(640, 320, 512, 256, dmix_fine)
        attend_back(v.trf, v.trrf, v.psf, v.mixf, 4, 8, WP, 8)

        def dh_fine(part, cols):
            v.wide[part, cols] = nt(v.trf[part, :], qkv_f[cols, :])

        tiles(640, 320, 512, 256, dh_fine)

        @pl.loop(0, 4, unroll=2)
        def _(i):
            part = aligned(i * 160, 160, 16)
            d = norm_back(v.wide[part, :], v.hf[part, :], v.sf[part, :])
            v.xf[part, :] = (d.astype(bf16).astype(f32) + v.yf[part, :].astype(f32)).astype(bf16)

        pack("fine_b", v.xf[...], got.fine_halo_t)
        copies = shift("fine_b")
        fine_pack_t = got.fine_pack_t
        finish(shift_out)
        out = nn(got.coarse_pack_t[...], recv_buf["coarse_b"][...]).astype(bf16)
        for r in range(6):
            coarse_ref[r] = out[16 * r : 16 * r + 6]
        writes = []
        fine_own_t = got.fine_own_t
        for j in range(4):
            here = (j * 160, min(j * 160 + 320, 640))
            v.wide[pl.ds(j * 144, 144), :] = nn(fine_own_t[:, : here[1] - here[0]], v.xf[here[0] : here[1], :])
        finish(copies)
        for j in range(4):
            part = pl.ds(j * 144, 144)
            d = v.wide[part, :] + nn(fine_pack_t[part, :], recv_buf["fine_b"][...])
            tokens[part, :] = d.astype(bf16)
            writes.append(pltpu.make_async_copy(tokens.at[part], grad_ref.at[part], local_sem.at[len(ALL_LOADED) + 3 + j]))
            writes[-1].start()
        for write in writes:
            write.wait()
        for copy in pending:
            copy.wait_send()
        for name in ALL_LOADED:
            getattr(got, name)

    any_space = pl.BlockSpec(memory_space=pl.ANY)
    whole = pl.BlockSpec(memory_space=pltpu.VMEM)
    return pl.pallas_call(
        kernel,
        out_shape=(jax.ShapeDtypeStruct((576, 512), bf16), jax.ShapeDtypeStruct((6, 6, 2048), bf16)),
        in_specs=[any_space] * len(shapes),
        out_specs=(any_space, whole),
        scratch_shapes=[pltpu.VMEM(*shape) for group in (scratch, loaded, sends, receives) for shape in group.values()]
        + [pltpu.SemaphoreType.DMA((N_LOCAL,)), pltpu.SemaphoreType.DMA((N_REMOTE,)), pltpu.SemaphoreType.DMA((N_REMOTE,))],
        compiler_params=pltpu.CompilerParams(
            collective_id=0, has_side_effects=True, vmem_limit_bytes=66_584_576
        ),
    )


def shards(
    tokens, qkv_fine, out_fine, merge_fine, qkv_mid, out_mid, merge_mid, qkv_coarse, out_coarse, grad_fine, grad_mid, grad_coarse
):
    values = dict(
        tokens=tokens.reshape(576, 512),
        qkv_f=qkv_fine,
        out_f=out_fine,
        mrg_f=merge_fine,
        qkv_m=qkv_mid,
        out_m=out_mid,
        wm=merge_mid,
        wq=qkv_coarse,
        wo=out_coarse,
        g_fine=grad_fine.reshape(576, 512),
        g_mid=grad_mid,
        g_coarse=grad_coarse,
        bias=jnp.asarray(BIAS),
        biasc=jnp.asarray(BIASC),
    )
    for name, matrix in CONSTANTS.items():
        values[name] = jnp.asarray(matrix, bf16)
    shapes = {name: (value.shape, value.dtype) for name, value in values.items()}
    gradient, coarse = build(shapes)(*values.values())
    return gradient.reshape(24, 24, 512), coarse


def solution(mesh):
    placed = (
        P("lat", "lon", None),
        P(),
        P(),
        P(),
        P(),
        P(),
        P("lon", None),
        P(None, "lon"),
        P("lon", None),
        P("lat", "lon", None),
        P("lat", "lon", None),
        P("lat", "lon", None),
    )
    return jax.shard_map(
        shards,
        mesh=mesh,
        in_specs=placed,
        out_specs=(P("lat", "lon", None), P("lat", "lon", None)),
        check_vma=False,
    )
```
